32 devices in a mesh: batch: 4 (over y, x), seq: 8 (over z, core).
Axes of the slice: x: 2, y: 2, z: 4, core: 2. Of those that a mesh axis runs over, the one named last changes fastest.
Arguments:
- block_in: bfloat16 [16, 1024, 1024], P('batch', 'seq'), may hold values from -6 to 6
- attn_in: bfloat16 [1024, 4096], P(None, 'seq'), may hold values from -0.1875 to 0.1875
- attn_out: bfloat16 [1024, 1024], P(None, 'seq'), may hold values from -0.375 to 0.375
- out_gain: bfloat16 [1024], P('seq'), may hold values from 0.5 to 1.5
- glu_in: bfloat16 [1024, 5632], P(None, 'seq'), may hold values from -0.1875 to 0.1875
- glu_out: bfloat16 [2816, 1024], P(None, 'seq'), may hold values from -0.109375 to 0.109375
- block_grad: bfloat16 [16, 1024, 1024], P('batch', 'seq'), may hold values from -6 to 6
Outputs:
- block_out: bfloat16 [16, 1024, 1024], P('batch', 'seq')
- input_grad: float32 [16, 1024, 1024], P('batch', 'seq')
- attn_in_grad: float32 [1024, 4096], P(None, 'seq')
- attn_out_grad: float32 [1024, 1024], P(None, 'seq')
- out_gain_grad: float32 [1024], P('seq')
- glu_in_grad: float32 [1024, 5632], P(None, 'seq')
- glu_out_grad: float32 [2816, 1024], P(None, 'seq')
The draws below stay inside these ranges and needn't reach their ends.
All inputs are finite; a program needn't handle non-finite values.
Results may differ from the reference program's by a relative error of at most 0.02.
Values may be sent and summed in bfloat16 or wider, within the bound.
A program may use at most 320 MiB of HBM per device.

```python
import jax
import jax.numpy as jnp
from jax import lax

HEADS = 16
HEAD_DIM = 64
D = 1024
FF = 2816
SPAN = 128
SEQS = 16
LEN = 1024


def shard_levels(own_key, dims, pieces, least, top_value):
    factor_of, own = 1.0, jax.random.fold_in(own_key, 6)
    for dim, blocks in pieces:
        steps = jnp.exp(jax.random.uniform(jax.random.fold_in(own, dim), (blocks,), jnp.float32, least / len(pieces), top_value / len(pieces)))
        factor_of = factor_of * jnp.repeat(steps, dims[dim] // blocks).reshape([-1 if axis == dim else 1 for axis in range(len(dims))])
    return factor_of


def centred(key, shape, deviation, bound, cuts=(), held_as=jnp.bfloat16):
    values = deviation * jax.random.normal(key, shape, jnp.float32)
    if cuts:
        values = values * shard_levels(key, shape, cuts, -0.22, 0.18)
    return jnp.clip(values, -bound, bound).astype(held_as)


def setup_inputs(seed: int = 0) -> dict:
    streams_of = jax.random.split(jax.random.key(seed), 8)
    return {
        "block_in": centred(streams_of[0], (SEQS, LEN, D), 1.0, 6.0, ((0, 4), (1, 8))),
        "attn_in": centred(streams_of[1], (D, 4 * D), D ** -0.5, 0.1875, ((1, 8),)),
        "attn_out": centred(streams_of[2], (D, D), (D // 4) ** -0.5, 0.375, ((1, 8),)),
        "out_gain": jnp.clip(0.5 + 1.0 * jax.random.uniform(streams_of[3], (D,), jnp.float32) ** shard_levels(streams_of[3], (D,), ((0, 8),), -0.2, 0.2), 0.5, 1.5).astype(jnp.bfloat16),
        "glu_in": centred(streams_of[4], (D, 2 * FF), D ** -0.5, 0.1875, ((1, 8),)),
        "glu_out": centred(streams_of[5], (FF, D), FF ** -0.5, 0.109375, ((1, 8),)),
        "block_grad": centred(streams_of[6], (SEQS, LEN, D), 1.0, 6.0, ((0, 4), (1, 8))),
    }


@jax.custom_vjp
def low(v):
    return lax.optimization_barrier(v.astype(jnp.bfloat16)).astype(jnp.float32)

@jax.custom_vjp
def low_back(v):
    return v

def low_keep(v):
    return (low(v), None)

def low_pass(kept, grad):
    return (grad,)

def back_keep(v):
    return (v, None)

def back_low(kept, grad):
    return (low(grad),)
low.defvjp(low_keep, low_pass)
low_back.defvjp(back_keep, back_low)

def rms_scaled(field, norm_eps):
    return field * lax.rsqrt(lax.optimization_barrier(jnp.mean(field * field, axis=-1, keepdims=True)) + norm_eps)

def block_forward(source, attn_in, attn_out, out_gain, glu_in, glu_out):
    highest = lax.Precision.HIGHEST
    norm_a = low(rms_scaled(source, 1e-06))
    projected = low_back(jnp.dot(norm_a, attn_in, preferred_element_type=jnp.float32, precision=highest))
    query_raw = projected[:, :D]
    key_raw = projected[:, D:2 * D]
    value_raw = projected[:, 2 * D:3 * D]
    gate_raw = projected[:, 3 * D:]
    queries = low(jax.nn.softplus(query_raw)).reshape(-1, SPAN, HEADS, HEAD_DIM)
    keys_low = low(jax.nn.softplus(key_raw)).reshape(-1, SPAN, HEADS, HEAD_DIM)
    values = low(value_raw).reshape(-1, SPAN, HEADS, HEAD_DIM)
    causal = jnp.tril(jnp.ones((SPAN, SPAN), dtype=bool))
    scores = jnp.einsum('bthe,bshe->bhts', queries, keys_low, precision=highest)
    scores = low_back(low(jnp.where(causal, scores, 0.0)))
    block_state = low_back(jnp.einsum('bthe,bthf->bhef', keys_low, values, precision=highest))
    running = jnp.cumsum(block_state, axis=0)
    earlier = low(jnp.concatenate([jnp.zeros_like(block_state[:1]), running[:-1]], axis=0))
    attended = jnp.einsum('bhts,bshe->bthe', scores, values, precision=highest)
    attended = attended + jnp.einsum('bthe,bhef->bthf', queries, earlier, precision=highest)
    attended = low_back(attended)
    head_scale = lax.rsqrt(lax.optimization_barrier(jnp.mean(attended * attended, axis=-1, keepdims=True)) + 1e-05)
    unit_rows = (attended * head_scale).reshape(-1, D)
    normed = unit_rows * out_gain
    gated_low = low(jax.nn.sigmoid(gate_raw) * normed)
    branch = low_back(jnp.dot(gated_low, attn_out, preferred_element_type=jnp.float32, precision=highest))
    middle = source + branch
    norm_b = low(rms_scaled(middle, 1e-06))
    glu_pair = low_back(jnp.dot(norm_b, glu_in, preferred_element_type=jnp.float32, precision=highest))
    hidden = low(glu_pair[:, :FF] * glu_pair[:, FF:])
    return middle + jnp.dot(hidden, glu_out, preferred_element_type=jnp.float32, precision=highest)

def reference(block_in, attn_in, attn_out, out_gain, glu_in, glu_out, block_grad):
    weights = (attn_in.astype(jnp.float32), attn_out.astype(jnp.float32), out_gain.astype(jnp.float32), glu_in.astype(jnp.float32), glu_out.astype(jnp.float32))

    def one_sequence(carried, inputs_pair):
        seq_in, seq_grad = inputs_pair
        seq_out, pullback = jax.vjp(block_forward, seq_in.astype(jnp.float32), weights[0], weights[1], weights[2], weights[3], weights[4])
        seq_grads = pullback(seq_grad.astype(jnp.float32))
        carried = (carried[0] + seq_grads[1], carried[1] + seq_grads[2], carried[2] + seq_grads[3], carried[3] + seq_grads[4], carried[4] + seq_grads[5])
        return (carried, (seq_out.astype(jnp.bfloat16), seq_grads[0]))
    zero_grads = (jnp.zeros_like(weights[0]), jnp.zeros_like(weights[1]), jnp.zeros_like(weights[2]), jnp.zeros_like(weights[3]), jnp.zeros_like(weights[4]))
    totals, stacked = lax.scan(one_sequence, zero_grads, (block_in, block_grad))
    return (stacked[0], stacked[1], totals[0], totals[1], totals[2], totals[3], totals[4])
```

```python
import functools

import jax
import jax.numpy as jnp
from jax import lax
from jax.experimental import pallas as pl
from jax.experimental.pallas import tpu as pltpu
from jax.sharding import PartitionSpec as P

HEADS = 16
HEAD_DIM = 64
D = 1024
FF = 2816
MESH = pl.DeviceIdType.MESH
BF16 = jnp.bfloat16
F32 = jnp.float32
PAD_ROWS = 16
GAIN_ROWS = 128


def run_if(cond, fn):
    if cond is None:
        fn()
    else:
        pl.when(cond)(fn)


class Place:
    def __init__(self, batch, seq):
        self.planes = seq // 2
        self.square = batch == 4
        self.b = lax.axis_index("batch")
        self.s = lax.axis_index("seq")
        self.z = lax.div(self.s, 2)
        self.c = lax.rem(self.s, 2)
        self.bx = self.b + 1 - 2 * lax.rem(self.b, 2)
        self.by = lax.rem(self.b + 2, 4)
        self.bd = lax.rem(self.bx + 2, 4)
        self.sib = (self.b, self.s + 1 - 2 * self.c)
        self.up = (self.b, self.s + 2)
        self.down = (self.b, self.s - 2)
        self.x = (self.bx, self.s)
        self.y = (self.by, self.s)
        self.has_up = self.z < self.planes - 1
        self.has_down = self.z > 0
        self.sent = []

    def barrier(self):
        sem = pltpu.get_barrier_semaphore()
        always = [self.sib] + ([self.x, self.y] if self.square else [])
        for device in always:
            pl.semaphore_signal(sem, inc=1, device_id=device, device_id_type=MESH)
        for cond, device in ((self.has_up, self.up), (self.has_down, self.down)):
            pl.when(cond)(
                lambda device=device: pl.semaphore_signal(
                    sem, inc=1, device_id=device, device_id_type=MESH
                )
            )
        ends = self.has_up.astype(jnp.int32) + self.has_down.astype(jnp.int32)
        pl.semaphore_wait(sem, len(always) + ends)

    def copy(self, src, dst, send_sem, recv_sem, device):
        return pltpu.make_async_remote_copy(
            src_ref=src,
            dst_ref=dst,
            send_sem=send_sem,
            recv_sem=recv_sem,
            device_id=device,
            device_id_type=MESH,
        )

    def send(self, make, cond=None):
        run_if(cond, lambda: make().start())
        self.sent.append((cond, make))

    def finish(self):
        for cond, make in self.sent:
            run_if(cond, lambda make=make: make().wait_send())
        self.sent = []


class Gather:
    Z_UP, Z_DOWN, Z_IN, X_OUT, X_IN, Y_OUT, Y_IN, FX_OUT, FX_IN, FY_OUT, FY_IN, S_OUT, S_IN = range(13)
    KINDS = 13

    def __init__(self, place, shards, fulls, quartered, sems, local_sems):
        self.p, self.shards, self.fulls, self.sems = place, shards, fulls, sems
        self.local_sems = local_sems
        self.quartered = [q and place.square for q in quartered]

    def rows(self, w, owner, half=None):
        rows = self.shards[w].shape[0]
        if not self.quartered[w]:
            return pl.ds(0, rows)
        part = rows // 4
        if half is None:
            return pl.ds(pl.multiple_of(owner * part, 16), part)
        return pl.ds(pl.multiple_of(owner * part + half * (part // 2), 16), part // 2)

    def move(self, w, zz, rows, out, into, device):
        block = self.fulls[w].at[2 * zz + self.p.c, rows]
        return self.p.copy(
            block, block, self.sems.at[out, w, zz], self.sems.at[into, w, zz], device
        )

    def start(self, w):
        p, own = self.p, self.shards[w]
        here = self.fulls[w].at[p.s]
        rows = self.rows(w, p.b)
        for cond, device, out in (
            (p.has_up, p.up, self.Z_UP),
            (p.has_down, p.down, self.Z_DOWN),
        ):
            p.send(
                lambda device=device, out=out: p.copy(
                    own.at[rows],
                    here.at[rows],
                    self.sems.at[out, w, p.z],
                    self.sems.at[self.Z_IN, w, p.z],
                    device,
                ),
                cond,
            )
        p.send(
            lambda: p.copy(
                own, here, self.sems.at[self.S_OUT, w, p.z], self.sems.at[self.S_IN, w, p.z], p.sib
            )
        )
        pltpu.make_async_copy(own, here, self.local_sems.at[w]).start()

    def sides(self, d):
        p = self.p
        return (
            (p.z >= d, p.z - d, p.has_up, p.up, self.Z_UP),
            (p.z + d < p.planes, p.z + d, p.has_down, p.down, self.Z_DOWN),
        )

    def from_z(self, w, d):
        p = self.p
        rows = self.rows(w, p.b)
        for cond, zz, more, device, out in self.sides(d):
            run_if(
                cond, lambda zz=zz: self.move(w, zz, rows, self.Z_UP, self.Z_IN, p.up).wait_recv()
            )
            p.send(
                lambda zz=zz, device=device, out=out: self.move(
                    w, zz, rows, out, self.Z_IN, device
                ),
                jnp.logical_and(cond, more),
            )
            if self.quartered[w]:
                p.send(lambda zz=zz: self.move(w, zz, rows, self.X_OUT, self.X_IN, p.x), cond)
                p.send(lambda zz=zz: self.move(w, zz, rows, self.Y_OUT, self.Y_IN, p.y), cond)

    def from_plane(self, w, d):
        p = self.p
        if not self.quartered[w]:
            return
        from_x, from_y = self.rows(w, p.bx), self.rows(w, p.by)
        half_x, half_y = self.rows(w, p.bx, 0), self.rows(w, p.by, 1)
        for cond, zz, *_ in self.sides(d):
            run_if(
                cond, lambda zz=zz: self.move(w, zz, from_x, self.X_OUT, self.X_IN, p.x).wait_recv()
            )
            p.send(lambda zz=zz: self.move(w, zz, half_x, self.FY_OUT, self.FY_IN, p.y), cond)
            run_if(
                cond, lambda zz=zz: self.move(w, zz, from_y, self.Y_OUT, self.Y_IN, p.y).wait_recv()
            )
            p.send(lambda zz=zz: self.move(w, zz, half_y, self.FX_OUT, self.FX_IN, p.x), cond)

    def from_diagonal(self, w, d):
        p = self.p
        half_0, half_1 = self.rows(w, p.bd, 0), self.rows(w, p.bd, 1)
        for cond, zz, *_ in self.sides(d):
            if self.quartered[w]:
                run_if(
                    cond,
                    lambda zz=zz: self.move(w, zz, half_0, self.FY_OUT, self.FY_IN, p.y).wait_recv(),
                )
                run_if(
                    cond,
                    lambda zz=zz: self.move(w, zz, half_1, self.FX_OUT, self.FX_IN, p.x).wait_recv(),
                )
            p.send(lambda zz=zz: self.whole(w, zz, p.c), cond)

    def whole(self, w, zz, core):
        block = self.fulls[w].at[2 * zz + core]
        return self.p.copy(
            block, block, self.sems.at[self.S_OUT, w, zz], self.sems.at[self.S_IN, w, zz], self.p.sib
        )

    def from_sibling(self, w):
        p = self.p
        pltpu.make_async_copy(
            self.shards[w], self.fulls[w].at[p.s], self.local_sems.at[w]
        ).wait()
        for zz in range(p.planes):
            self.whole(w, zz, 1 - p.c).wait_recv()


def plan_gather(g, count):
    far = g.p.planes - 1
    steps = [lambda: g.start(0)]

    def add(fn, *args):
        step = functools.partial(fn, *args)
        step.whole = fn.__name__ == "from_sibling"
        steps.append(step)

    for w in range(count):
        for d in range(1, far + 1):
            if not (d == 1 and w > 0):
                add(g.from_z, w, d)
            if d == max(far - 1, 1) and w + 1 < count:
                add(g.start, w + 1)
            if d >= 2:
                add(g.from_plane, w, d - 1)
            if d >= 3:
                add(g.from_diagonal, w, d - 2)
        if w + 1 < count:
            add(g.from_z, w + 1, 1)
        add(g.from_plane, w, far)
        if far >= 2:
            add(g.from_diagonal, w, far - 1)
        add(g.from_diagonal, w, far)
        add(g.from_sibling, w)
    return steps


def add_into(dst, src, row, rows):
    cols = dst.shape[-1]
    chunk = max(
        k for k in range(16, rows + 1, 16) if rows % k == 0 and (k * cols <= 49152 or k == 16)
    )

    def body(i, _):
        here = pl.ds(pl.multiple_of(row + i * chunk, 16), chunk)
        there = pl.ds(pl.multiple_of(i * chunk, 16), chunk)
        dst[here, :] = (dst[here, :].astype(F32) + src[there, :].astype(F32)).astype(BF16)
        return 0

    lax.fori_loop(0, rows // chunk, body, 0)


class Reduce:
    (X1_OUT, X1_IN, Y1_OUT, Y1_IN, X2_OUT, X2_IN, Y2_OUT, Y2_IN, X3_OUT, X3_IN, Y3_OUT, Y3_IN) = range(12)
    KINDS = 12
    S_OUT, S_IN = range(2)
    Z_UP, Z_UP_IN, Z_DOWN, Z_DOWN_IN, FETCH = range(5)
    GX_OUT, GX_IN, GY_OUT, GY_IN, FX_OUT, FX_IN, FY_OUT, FY_IN, LOCAL = range(9)
    LAST_KINDS = 9

    def __init__(self, place, wide, z_parts, out, zin_far, refs):
        self.p, self.wide, self.out = place, wide and place.square, out
        self.part, self.x1, self.y1, self.x2, self.y2, zin, self.stage = refs[:7]
        self.core_sems, self.sems, self.z_sems, self.last_sems = refs[7:]
        self.zin = zin if self.wide else zin_far
        self.total = self.part.shape[1]
        self.quarter, self.half = self.total // 4, self.total // 8
        self.z_parts = 1 if self.wide else z_parts

    @staticmethod
    def scratch(square, wide, planes, rows, cols, core_parts, z_parts):
        wide = wide and square
        pieces = planes if wide else 1
        small = (pieces, rows // 8, cols) if square else (1, 16, 128)
        large = (pieces, rows // 4, cols) if square else (1, 16, 128)
        return [
            pltpu.VMEM((planes, rows, cols), BF16),
            pltpu.VMEM(small, BF16),
            pltpu.VMEM(small, BF16),
            pltpu.VMEM(large, BF16),
            pltpu.VMEM(large, BF16),
            pltpu.VMEM((planes + 1, rows // 4, cols) if wide else (1, 16, 128), BF16),
            pltpu.VMEM((16, 128) if wide else (rows // z_parts, cols), BF16),
            pltpu.SemaphoreType.DMA((2, planes, core_parts)),
            pltpu.SemaphoreType.DMA((Reduce.KINDS, pieces)),
            pltpu.SemaphoreType.DMA((5, planes + 1, z_parts)),
            pltpu.SemaphoreType.DMA((Reduce.LAST_KINDS,)),
        ]

    @staticmethod
    def far(square, wide, planes, rows, cols):
        shape = (1, 16, 128) if wide and square else (planes + 1, rows, cols)
        return jax.ShapeDtypeStruct(shape, BF16)

    def at(self, owner, half=None):
        if half is None:
            return pl.ds(pl.multiple_of(owner * self.quarter, 16), self.quarter)
        return pl.ds(pl.multiple_of(owner * self.quarter + half * self.half, 16), self.half)

    def sem(self, kind, k):
        return self.sems.at[kind, k]

    def core_copy(self, zz, src, row, rows, k):
        block = self.part.at[zz, pl.ds(row, rows)]
        return self.p.copy(
            block if src is None else src,
            block,
            self.core_sems.at[self.S_OUT, zz, k],
            self.core_sems.at[self.S_IN, zz, k],
            self.p.sib,
        )

    def slot(self, zz):
        return zz if self.wide else 0

    def hop(self, zz, rows, dst, out, into, device):
        return self.p.copy(
            self.part.at[zz, rows],
            dst,
            self.sem(out, self.slot(zz)),
            self.sem(into, self.slot(zz)),
            device,
        )

    def plane_1(self, zz):
        p, k, h = self.p, self.slot(zz), self.half
        lo, hi = pl.ds(0, h), pl.ds(h, h)
        p.send(lambda: self.hop(zz, self.at(p.bd, 0), self.x1.at[k], self.X1_OUT, self.X1_IN, p.x))
        p.send(lambda: self.hop(zz, self.at(p.bd, 1), self.y1.at[k], self.Y1_OUT, self.Y1_IN, p.y))
        p.send(lambda: self.hop(zz, self.at(p.bx, 0), self.x2.at[k, lo], self.X2_OUT, self.X2_IN, p.x))
        p.send(lambda: self.hop(zz, self.at(p.by, 1), self.y2.at[k, hi], self.Y2_OUT, self.Y2_IN, p.y))

    def plane_2(self, zz):
        p, k, h = self.p, self.slot(zz), self.half
        lo, hi = pl.ds(0, h), pl.ds(h, h)
        self.hop(zz, self.at(p.bd, 0), self.x1.at[k], self.X1_OUT, self.X1_IN, p.x).wait_recv()
        add_into(self.part.at[zz], self.x1.at[k], p.by * self.quarter, h)
        p.send(lambda: self.hop(zz, self.at(p.by, 0), self.y2.at[k, lo], self.Y3_OUT, self.Y3_IN, p.y))
        self.hop(zz, self.at(p.bd, 1), self.y1.at[k], self.Y1_OUT, self.Y1_IN, p.y).wait_recv()
        add_into(self.part.at[zz], self.y1.at[k], p.bx * self.quarter + h, h)
        p.send(lambda: self.hop(zz, self.at(p.bx, 1), self.x2.at[k, hi], self.X3_OUT, self.X3_IN, p.x))

    def plane_3(self, zz):
        p, k, h = self.p, self.slot(zz), self.half
        lo, hi = pl.ds(0, h), pl.ds(h, h)
        self.hop(zz, self.at(p.bx, 0), self.x2.at[k, lo], self.X2_OUT, self.X2_IN, p.x).wait_recv()
        self.hop(zz, self.at(p.by, 1), self.y2.at[k, hi], self.Y2_OUT, self.Y2_IN, p.y).wait_recv()
        self.hop(zz, self.at(p.bx, 1), self.x2.at[k, hi], self.X3_OUT, self.X3_IN, p.x).wait_recv()
        add_into(self.part.at[zz], self.x2.at[k], p.b * self.quarter, self.quarter)
        self.hop(zz, self.at(p.by, 0), self.y2.at[k, lo], self.Y3_OUT, self.Y3_IN, p.y).wait_recv()
        add_into(self.part.at[zz], self.y2.at[k], p.b * self.quarter, self.quarter)

    def z_rows(self, k):
        p = self.p
        rows = self.total // self.z_parts
        return (p.b * self.quarter, self.quarter) if self.wide else (k * rows, rows)

    def z_slot(self, zz, upward, k):
        slot = zz + 1 if upward else zz
        if self.wide:
            return self.zin.at[slot]
        row, rows = self.z_rows(k)
        return self.zin.at[slot, pl.ds(row, rows)]

    def z_hop(self, zz, upward, k):
        p = self.p
        row, rows = self.z_rows(k)
        here = pl.ds(pl.multiple_of(row, 16), rows)
        out, into = (self.Z_UP, self.Z_UP_IN) if upward else (self.Z_DOWN, self.Z_DOWN_IN)
        return p.copy(
            self.part.at[zz, here],
            self.z_slot(zz, upward, k),
            self.z_sems.at[out, zz, k],
            self.z_sems.at[into, zz, k],
            p.up if upward else p.down,
        )

    def z_take(self, zz, upward, k):
        self.z_hop(zz, upward, k).wait_recv()
        row, rows = self.z_rows(k)
        src = self.z_slot(zz, upward, k)
        if not self.wide:
            slot = zz + 1 if upward else zz
            fetch = pltpu.make_async_copy(src, self.stage, self.z_sems.at[self.FETCH, slot, k])
            fetch.start()
            fetch.wait()
            src = self.stage
        add_into(self.part.at[zz], src, row, rows)

    def z_step(self, d, k=0):
        p = self.p
        for upward, there, exists, inner in (
            (True, p.z + d, p.z + d < p.planes, p.has_down),
            (False, p.z - d, p.z >= d, p.has_up),
        ):
            pl.when(jnp.logical_and(exists, inner))(
                lambda there=there, upward=upward: self.z_take(there, upward, k)
            )
            p.send(lambda there=there, upward=upward: self.z_hop(there, upward, k), exists)

    def z_last(self, k=0):
        p = self.p
        pl.when(p.has_down)(lambda: self.z_take(p.z, True, k))
        pl.when(p.has_up)(lambda: self.z_take(p.z, False, k))

    def z_steps(self):
        for k in range(self.z_parts):
            for d in range(self.p.planes - 1, 0, -1):
                yield functools.partial(self.z_step, d, k)
            yield functools.partial(self.z_last, k)

    def plane_steps(self, zz):
        if self.p.square:
            yield functools.partial(self.plane_2, zz)
            yield functools.partial(self.plane_3, zz)

    def spread_steps(self):
        yield self.spread_1
        yield self.spread_2
        yield self.spread_3

    def last_hop(self, src, rows, out, into, device):
        return self.p.copy(
            src, self.out.at[rows], self.last_sems.at[out], self.last_sems.at[into], device
        )

    def spread_1(self):
        p = self.p
        if not p.square:
            pltpu.make_async_copy(self.part.at[p.z], self.out, self.last_sems.at[self.LOCAL]).start()
            return
        rows = self.at(p.b)
        src = self.part.at[p.z, rows]
        p.send(lambda: self.last_hop(src, rows, self.GX_OUT, self.GX_IN, p.x))
        p.send(lambda: self.last_hop(src, rows, self.GY_OUT, self.GY_IN, p.y))
        pltpu.make_async_copy(src, self.out.at[rows], self.last_sems.at[self.LOCAL]).start()

    def spread_2(self):
        p = self.p
        if not p.square:
            return
        from_x, from_y = self.at(p.bx), self.at(p.by)
        half_x, half_y = self.at(p.bx, 0), self.at(p.by, 1)
        self.last_hop(self.out.at[from_x], from_x, self.GX_OUT, self.GX_IN, p.x).wait_recv()
        p.send(lambda: self.last_hop(self.out.at[half_x], half_x, self.FY_OUT, self.FY_IN, p.y))
        self.last_hop(self.out.at[from_y], from_y, self.GY_OUT, self.GY_IN, p.y).wait_recv()
        p.send(lambda: self.last_hop(self.out.at[half_y], half_y, self.FX_OUT, self.FX_IN, p.x))

    def spread_3(self):
        p = self.p
        if not p.square:
            pltpu.make_async_copy(self.part.at[p.z], self.out, self.last_sems.at[self.LOCAL]).wait()
            return
        rows = self.at(p.b)
        half_0, half_1 = self.at(p.bd, 0), self.at(p.bd, 1)
        self.last_hop(self.out.at[half_0], half_0, self.FY_OUT, self.FY_IN, p.y).wait_recv()
        self.last_hop(self.out.at[half_1], half_1, self.FX_OUT, self.FX_IN, p.x).wait_recv()
        pltpu.make_async_copy(
            self.part.at[p.z, rows], self.out.at[rows], self.last_sems.at[self.LOCAL]
        ).wait()


def dot(a, b):
    return jnp.dot(a, b, preferred_element_type=F32)


def dot_nt(a, b):
    return lax.dot_general(a, b, (((1,), (1,)), ((), ())), preferred_element_type=F32)


def dot_tn(a, b):
    return lax.dot_general(a, b, (((0,), (0,)), ((), ())), preferred_element_type=F32)


def row_loop(rows, chunk, body):
    def step(i, _):
        body(pl.ds(pl.multiple_of(i * chunk, chunk), chunk))
        return 0

    lax.fori_loop(0, rows // chunk, step, 0)


def lanes(block, width=128):
    return pl.ds(pl.multiple_of(block * width, width), width)


def tokens(i, span):
    return pl.ds(pl.multiple_of(i * span, span), span)


def transpose(src, dst):
    rows, cols = src.shape
    whole = cols // 128

    def step(j, _):
        at = lanes(j)
        dst[at, :] = src[:, at].T
        return 0

    lax.fori_loop(0, whole, step, 0)
    if cols % 128:
        dst[whole * 128 :, :] = src[:, whole * 128 :].T


def mean_square(v):
    return jnp.mean(v * v, axis=-1, keepdims=True)


class Pump:
    def __init__(self, steps):
        self.steps = list(steps)

    def __call__(self, count=1):
        for step in self.steps[:count]:
            step()
        del self.steps[:count]

    def until(self, left):
        self(len(self.steps) - left)


def pair_masks(span):
    lane = lax.broadcasted_iota(jnp.int32, (span, 128), 1)
    first = (lane < HEAD_DIM).astype(F32)
    row = lax.broadcasted_iota(jnp.int32, (128, 128), 0)
    col = lax.broadcasted_iota(jnp.int32, (128, 128), 1)
    own = ((row < HEAD_DIM) == (col < HEAD_DIM)).astype(F32)
    return first.astype(BF16), (1.0 - first).astype(BF16), own.astype(BF16), own


def by_head(pair, first, second):
    return jnp.concatenate([pair * first, pair * second], axis=0)


def pack_state(state):
    lane = lax.broadcasted_iota(jnp.int32, (HEAD_DIM, 128), 1)
    return jnp.where(lane < HEAD_DIM, state[:HEAD_DIM], state[HEAD_DIM:])


def unpack_state(packed, own):
    return jnp.concatenate([packed, packed], axis=0) * own


def head_sums(v, own):
    high = v.astype(BF16)
    low = (v - high.astype(F32)).astype(BF16)
    return dot(high, own) + dot(low, own)


class Chain:
    S_OUT, S_IN, Z_OUT, Z_IN, P_OUT, P_IN = range(6)

    def __init__(self, place, forward, mine, other, before, out, sems):
        self.p, self.forward = place, forward
        self.mine, self.other, self.before, self.out, self.sems = mine, other, before, out, sems
        self.half = mine.shape[0] // 2
        if forward:
            self.prev, self.next = place.has_down, place.has_up
            self.device, self.counts = place.up, place.c == 1
        else:
            self.prev, self.next = place.has_up, place.has_down
            self.device, self.counts = place.down, place.c == 0

    @staticmethod
    def scratch(count):
        return [pltpu.VMEM((count, HEAD_DIM, 128), BF16)] * 4 + [pltpu.SemaphoreType.DMA((6,))]

    def part(self, core):
        return pl.ds(core * self.half, self.half)

    def sibling_copy(self):
        return self.p.copy(
            self.mine, self.other, self.sems.at[self.S_OUT], self.sems.at[self.S_IN], self.p.sib
        )

    def next_copy(self):
        here = self.part(self.p.c)
        return self.p.copy(
            self.out.at[here], self.before.at[here], self.sems.at[self.Z_OUT],
            self.sems.at[self.Z_IN], self.device,
        )

    def across_copy(self, core):
        here = self.part(core)
        return self.p.copy(
            self.before.at[here], self.before.at[here], self.sems.at[self.P_OUT],
            self.sems.at[self.P_IN], self.p.sib,
        )

    def start(self):
        self.p.send(self.sibling_copy)

        @pl.when(jnp.logical_not(self.prev))
        def _():
            self.before[...] = jnp.zeros_like(self.before)

    def step(self):
        p = self.p
        self.sibling_copy().wait_recv()
        pl.when(self.prev)(lambda: self.next_copy().wait_recv())
        p.send(lambda: self.across_copy(p.c), self.prev)

        @pl.when(self.next)
        def _():
            def body(i, _):
                k = p.c * self.half + i
                total = self.before[k].astype(F32) + self.mine[k].astype(F32)
                self.out[k] = (total + self.other[k].astype(F32)).astype(BF16)
                return 0

            lax.fori_loop(0, self.half, body, 0)

        p.send(self.next_copy, self.next)

    def finish(self, result):
        p = self.p
        pl.when(self.prev)(lambda: self.across_copy(1 - p.c).wait_recv())
        weight = self.counts.astype(F32)

        def body(k, _):
            total = self.before[k].astype(F32) + self.other[k].astype(F32) * weight
            result[k] = total.astype(BF16)
            return 0

        lax.fori_loop(0, result.shape[0], body, 0)


class Locals:
    def __init__(self, sems):
        self.sems, self.used, self.open = sems, 0, []

    def copy(self, src, dst):
        made = pltpu.make_async_copy(src, dst, self.sems.at[self.used])
        self.used += 1
        made.start()
        return made

    def save(self, src, dst):
        self.open.append(self.copy(src, dst))

    def finish(self):
        for made in self.open:
            made.wait()


def load_columns(local, full, rows, dst, stage):
    seq, _, cols = full.shape
    if cols % 128 == 0:
        return [local.copy(full.at[s, rows], dst.at[:, pl.ds(s * cols, cols)]) for s in range(seq)]
    for s in range(seq):
        local.copy(full.at[s, rows], stage.at[pl.ds(0, rows.size)]).wait()
        dst[:, s * cols : (s + 1) * cols] = stage[: rows.size]
    return []


def stream(count, source, slots, sems, body, after=None):
    def fetch(k):
        return pltpu.make_async_copy(source(k), slots.at[lax.rem(k, 2)], sems.at[lax.rem(k, 2)])

    fetch(0).start()

    def step(k, _):
        @pl.when(k + 1 < count)
        def _():
            fetch(k + 1).start()

        fetch(k).wait()
        body(k, lax.rem(k, 2))
        return 0

    if after is None:
        lax.fori_loop(0, count, step, 0)
    else:
        for k in range(count):
            step(jnp.int32(k), 0)
            after(k)


def forward_kernel(batch, seq, spans, *refs):
    (x_hbm, *shards), refs = refs[:5], refs[5:]
    fulls, refs = refs[:4], refs[4:]
    out_hbm, saved, refs = refs[0], refs[1:13], refs[13:]
    (q_out, k_out, v_out, raw_out, att_out, e_out, gated_out, mid_out, nb_out, pair_out, hid_out, na_out) = saved
    (x, na, tmp, q, k, v, raw, att, gated, mid, nb, w_in, w_out, gain, w_pair, tmp_g, tmp_u, pair, hid,
     w_down, res, stage, na_t, gated_t, nb_t, hid_t, mine, other, before, chain_out, early, chain_sems, slot_sems, pair_sems,
     local_sems, gather_sems, gather_local) = refs
    place = Place(batch, seq)
    local = Locals(local_sems)
    load_x = local.copy(x_hbm, x)
    place.barrier()
    gather = Gather(place, shards, fulls, (True, False, True, True), gather_sems, gather_local)
    rows, span = x.shape[0], spans
    per_group = seq // 4
    blocks = rows // span
    pairs = D // 128
    cols_in = w_in.shape[-1]
    half = seq // 2
    first, second, own, own_f = pair_masks(span)
    pump, marks = plan(gather)

    pump(2)
    load_x.wait()

    def norm_rows(r):
        xr = x[r, :].astype(F32)
        na[r, :] = (xr * lax.rsqrt(mean_square(xr) + 1e-6)).astype(BF16)

    row_loop(rows, 32, norm_rows)
    transpose(na, na_t)
    local.save(na_t, na_out)
    pump.until(marks[0])

    dests = (q, k, v, raw)
    for group in range(4):
        dest = dests[group]

        def project(n, slot, group=group, dest=dest):
            tmp[...] = dot(na[...], w_in[slot])
            at = pl.ds(pl.multiple_of(n * cols_in, 128), cols_in)

            def finish_rows(r):
                value = tmp[r, :]
                if group < 2:
                    value = jnp.maximum(value, 0.0) + jnp.log1p(jnp.exp(-jnp.abs(value)))
                dest[r, at] = value.astype(dest.dtype)

            row_loop(rows, 32, finish_rows)

        stream(
            per_group,
            lambda n, group=group: fulls[0].at[group * per_group + n],
            w_in,
            slot_sems,
            project,
        )
        pump(2)

    def state(n, _):
        i, j = lax.div(n, pairs), lax.rem(n, pairs)
        at, block = tokens(i, span), lanes(j)
        mine[n] = pack_state(dot_tn(k[at, block], v[at, block])).astype(BF16)
        return 0

    lax.fori_loop(0, blocks * pairs, state, 0)
    chain = Chain(place, True, mine, other, before, chain_out, chain_sems)
    chain.start()
    for src, dst in ((q, q_out), (k, k_out), (v, v_out)):
        local.save(src, dst)
    pump(2)

    row = lax.rem(lax.broadcasted_iota(jnp.int32, (2 * span, span), 0), span)
    col = lax.broadcasted_iota(jnp.int32, (2 * span, span), 1)
    lane = lax.broadcasted_iota(jnp.int32, (span, 128), 1)

    def inner(n, _):
        i, j = lax.div(n, pairs), lax.rem(n, pairs)
        at, block = tokens(i, span), lanes(j)
        scores = dot_nt(by_head(q[at, block], first, second), k[at, block])
        scores = jnp.where(row >= col, scores, 0.0).astype(BF16)
        both = dot(scores, v[at, block])
        att[at, block] = jnp.where(lane < HEAD_DIM, both[:span], both[span:])
        return 0

    for i in range(blocks):
        lax.fori_loop(i * pairs, (i + 1) * pairs, inner, 0)
        if i == 0:
            chain.step()
        pump(1)

    pump.until(marks[1])
    waits = load_columns(local, fulls[1], pl.ds(0, D), w_out, stage)
    waits += load_columns(local, fulls[1], pl.ds(D, PAD_ROWS), gain, stage)
    chain.finish(early)
    local.save(early, e_out)
    for made in waits:
        made.wait()

    def outer(n, _):
        i, j = lax.div(n, pairs), lax.rem(n, pairs)
        at, block = tokens(i, span), lanes(j)
        a = att[at, block] + dot(q[at, block], unpack_state(early[n], own))
        att[at, block] = a
        unit = a * lax.rsqrt(head_sums(a * a, own) * (1.0 / HEAD_DIM) + 1e-5)
        normed = unit * gain[0:1, block].astype(F32)
        gated[at, block] = (jax.nn.sigmoid(raw[at, block]) * normed).astype(BF16)
        return 0

    lax.fori_loop(0, blocks * pairs, outer, 0)
    pump(1)

    def branch(n, _):
        at = pl.ds(pl.multiple_of(n * 512, 512), 512)
        mid[:, at] = x[:, at].astype(F32) + dot(gated[...], w_out[:, at])
        return 0

    lax.fori_loop(0, D // 512, branch, 0)

    def norm_mid(r):
        m = mid[r, :]
        nb[r, :] = (m * lax.rsqrt(mean_square(m) + 1e-6)).astype(BF16)

    row_loop(rows, 32, norm_mid)
    transpose(gated, gated_t)
    transpose(nb, nb_t)
    for src, dst in ((raw, raw_out), (att, att_out), (gated_t, gated_out), (mid, mid_out), (nb_t, nb_out)):
        local.save(src, dst)
    pump.until(marks[2])

    def fetch_pair(j):
        slot = j % 2
        return [
            pltpu.make_async_copy(
                fulls[2].at[j + side * half], w_pair.at[slot, side], pair_sems.at[slot, side]
            )
            for side in range(2)
        ]

    for made in fetch_pair(0):
        made.start()
    for j in range(half):
        if j + 1 < half:
            for made in fetch_pair(j + 1):
                made.start()
        for made in fetch_pair(j):
            made.wait()
        slot = j % 2
        tmp_g[...] = dot(nb[...], w_pair[slot, 0])
        tmp_u[...] = dot(nb[...], w_pair[slot, 1])

        def finish_pair(r, j=j):
            gate, up = tmp_g[r, :], tmp_u[r, :]
            pair[j, r, :] = gate.astype(BF16)
            pair[j + half, r, :] = up.astype(BF16)
            hid[j, r, :] = (gate * up).astype(BF16)

        row_loop(rows, 32, finish_pair)
        local.save(pair.at[j], pair_out.at[j])
        local.save(pair.at[j + half], pair_out.at[j + half])
        transpose(hid.at[j], hid_t.at[j])
        local.save(hid_t.at[j], hid_out.at[j])
        pump(max(1, (len(pump.steps) - marks[3]) // (half - j)))

    pump.until(marks[3])
    for made in load_columns(local, fulls[3], pl.ds(0, w_down.shape[0]), w_down, stage):
        made.wait()
    width = hid.shape[-1]

    def down(n, _):
        at = pl.ds(pl.multiple_of(n * 512, 512), 512)
        total = mid[:, at]
        for j in range(half):
            total = total + dot(hid[j], w_down[j * width : (j + 1) * width, at])
        res[:, at] = total.astype(BF16)
        return 0

    lax.fori_loop(0, D // 512, down, 0)
    local.save(res, out_hbm)
    pump.until(0)
    local.finish()
    place.finish()


def plan(gather):
    steps = plan_gather(gather, 4)
    marks = []
    kept = []
    for step in steps:
        kept.append(step)
        if getattr(step, "whole", False):
            marks.append(len(kept))
    return Pump(kept), [len(kept) - m for m in marks]


def forward(batch, seq, x, span, shards):
    rows = x.shape[0]
    cols_in, cols_pair = shards[0].shape[1], shards[2].shape[1]
    half = seq // 2
    states = (rows // span) * (D // 128)
    big = jax.ShapeDtypeStruct((rows, D), BF16)
    big_f = jax.ShapeDtypeStruct((rows, D), F32)
    narrow = shards[3].shape[1] % 128 != 0
    any_space = pl.BlockSpec(memory_space=pl.ANY)
    out_shape = [jax.ShapeDtypeStruct((seq, *a.shape), a.dtype) for a in shards]
    out_shape += [big, big, big, big, big, big_f]
    turned = jax.ShapeDtypeStruct((D, rows), BF16)
    out_shape += [jax.ShapeDtypeStruct((states, HEAD_DIM, 128), BF16), turned, big_f, turned]
    out_shape += [
        jax.ShapeDtypeStruct((seq, rows, cols_pair), BF16),
        jax.ShapeDtypeStruct((half, cols_pair, rows), BF16),
        turned,
    ]
    wide, wide_f = pltpu.VMEM((rows, D), BF16), pltpu.VMEM((rows, D), F32)
    pair_f = pltpu.VMEM((rows, cols_pair), F32)
    scratch = [
        wide, wide, pltpu.VMEM((rows, cols_in), F32), wide, wide, wide, wide, wide_f, wide, wide_f, wide,
        pltpu.VMEM((2, D, cols_in), BF16),
        pltpu.VMEM((D, D), BF16),
        pltpu.VMEM((PAD_ROWS, D), BF16),
        pltpu.VMEM((2, 2, D, cols_pair), BF16),
        pair_f, pair_f,
        pltpu.VMEM((seq, rows, cols_pair), BF16),
        pltpu.VMEM((half, rows, cols_pair), BF16),
        pltpu.VMEM((FF, D), BF16),
        wide,
        pltpu.VMEM((FF, shards[3].shape[1]) if narrow else (16, 128), BF16),
        *[pltpu.VMEM((D, rows), BF16)] * 3,
        pltpu.VMEM((half, cols_pair, rows), BF16),
        *[pltpu.VMEM((states, HEAD_DIM, 128), BF16)] * 5,
        pltpu.SemaphoreType.DMA((6,)),
        pltpu.SemaphoreType.DMA((2,)),
        pltpu.SemaphoreType.DMA((2, 2)),
        pltpu.SemaphoreType.DMA((128,)),
        pltpu.SemaphoreType.DMA((Gather.KINDS, 4, half)),
        pltpu.SemaphoreType.DMA((4,)),
    ]
    return pl.pallas_call(
        functools.partial(forward_kernel, batch, seq, span),
        out_shape=out_shape,
        in_specs=[any_space] * 5,
        out_specs=[any_space] * len(out_shape),
        scratch_shapes=scratch,
        compiler_params=pltpu.CompilerParams(
            collective_id=0, has_side_effects=True, vmem_limit_bytes=62 * 1024 * 1024
        ),
        name="forward",
    )(x, *shards)


WIDE = (False, True, False, True)
Z_PARTS = (4, 4, 2, 4)


def slope(plus):
    series = plus * (1.0 - plus * (0.5 - plus * (1.0 / 6.0)))
    return jnp.where(plus < 0.02, series, 1.0 - jnp.exp(-plus))


def backward_kernel(batch, seq, span, *refs):
    g_hbm, x_hbm, *fulls = refs[:6]
    (q_in, k_in, v_in, raw_in, att_in, e_in, gated_in, mid_in, nb_in, pair_in, hid_in, na_in) = refs[6:18]
    grad_hbm, sums, gm_hbm, far = refs[18], refs[19:23], refs[23], refs[24:28]
    refs = list(refs[28:])
    place = Place(batch, seq)
    reds = []
    for w in range(4):
        reds.append(Reduce(place, WIDE[w], Z_PARTS[w], sums[w], far[w], refs[:11]))
        refs = refs[11:]
    (tall, turned, pair, fields, f0, f1, g, split, low, down, slots, wide_out, slim_out, gain, gain_sums, gain_split,
     early, mine, other, before, chain_out, stage, chain_sems, slot_sems, local_sems) = refs
    red_down, red_pair, red_out, red_in = reds
    local = Locals(local_sems)
    rows = g.shape[0]
    half = seq // 2
    planes = half
    width = hid_in.shape[1]
    cols_in, cols_out, cols_pair = fulls[0].shape[2], fulls[1].shape[2], fulls[2].shape[2]
    per_group, per_block = seq // 4, cols_in // 128
    blocks, pairs = rows // span, D // 128
    first, second, own, own_f = pair_masks(span)
    core, sibling = place.c, 1 - place.c
    pending = Pump([])

    load_g = local.copy(g_hbm, g)
    load_hid = [local.copy(hid_in.at[j], tall.at[pl.ds(j * width, width)]) for j in range(half)]
    load_nb = local.copy(nb_in, turned)
    load_pair = [local.copy(pair_in.at[s], pair.at[s]) for s in range(seq)]
    load_mid = local.copy(mid_in, f1)
    load_e = local.copy(e_in, early)
    place.barrier()

    def split_columns(src):
        for s in range(seq):
            to = (s % 2) * (D // 2) + (s // 2) * cols_out
            split[:, to : to + cols_out] = src[:, s * cols_out : (s + 1) * cols_out]

    def by_core(which):
        return pl.ds(pl.multiple_of(which * (D // 2), D // 2), D // 2)

    slim_sent = []

    def slim_send(red, row, count, k, fill):
        slot = len(slim_sent) % 2
        if len(slim_sent) >= 2:
            for made in slim_sent[-2]:
                made().wait_send()
        fill(slot)
        sent = []
        for zz in range(planes):
            src = slim_out.at[slot, zz, pl.ds(0, count)]
            sent.append(functools.partial(red.core_copy, zz, src, row, count, k))
            sent[-1]().start()
        slim_sent.append(sent)

    def slim_theirs(red, lhs, at, row, count, k):
        def fill(slot):
            value = dot(lhs[at : at + count, :], split[:, by_core(sibling)])
            for zz in range(planes):
                slim_out[slot, zz, 0:count, :] = value[:, zz * cols_out : (zz + 1) * cols_out].astype(BF16)

        slim_send(red, row, count, k, fill)

    def slim_mine(red, lhs, at, row, count, k):
        value = dot(lhs[at : at + count, :], split[:, by_core(core)])
        for zz in range(planes):
            red.core_copy(zz, None, row, count, k).wait_recv()
            here = red.part[zz, row : row + count, :].astype(F32)
            here = here + value[:, zz * cols_out : (zz + 1) * cols_out]
            red.part[zz, row : row + count, :] = here.astype(BF16)

    wide_sent = []

    def wide_theirs(red, cols, zz):
        slot = len(wide_sent) % 2
        if len(wide_sent) >= 2:
            wide_sent[-2]().wait_send()
        s = 2 * zz + sibling

        def body(r):
            wide_out[slot, r, 0:cols] = dot(turned[r, :], pair[s, :, 0:cols]).astype(BF16)

        row_loop(D, 256, body)
        src = wide_out.at[slot] if cols == wide_out.shape[2] else wide_out.at[slot, :, pl.ds(0, cols)]
        wide_sent.append(functools.partial(red.core_copy, zz, src, 0, D, 0))
        wide_sent[-1]().start()

    def wide_mine(red, cols, zz):
        s = 2 * zz + core
        red.core_copy(zz, None, 0, D, 0).wait_recv()

        def body(r):
            here = red.part[zz, r, :].astype(F32) + dot(turned[r, :], pair[s, :, 0:cols])
            red.part[zz, r, :] = here.astype(BF16)

        row_loop(D, 256, body)
        if red.wide:
            red.plane_1(zz)

    load_g.wait()
    split_columns(g)
    for made in load_hid:
        made.wait()
    for j in range(half):
        slim_theirs(red_down, tall, j * width, j * width, width, j)
    for j in range(half):
        slim_mine(red_down, tall, j * width, j * width, width, j)
    pending.steps += red_down.z_steps()

    def load_down(j):
        at = pl.ds((j % 2) * width, width)
        return load_columns(local, fulls[3], pl.ds(j * width, width), down.at[at], stage)

    for made in load_pair:
        made.wait()
    waits = load_down(0)
    for j in range(half):
        after = load_down(j + 1) if j + 1 < half else []
        for made in waits:
            made.wait()
        waits = after
        at = (j % 2) * width
        f0[:, 0:width] = dot_nt(g[...], down[at : at + width, :])

        def finish_pair(r, j=j):
            grad = f0[r, 0:width]
            gate, up = pair[j, r, :].astype(F32), pair[j + half, r, :].astype(F32)
            pair[j, r, :] = (grad * up).astype(BF16)
            pair[j + half, r, :] = (grad * gate).astype(BF16)

        row_loop(rows, 32, finish_pair)

    load_nb.wait()
    wide_theirs(red_pair, cols_pair, 0)
    for zz in range(planes):
        if zz + 1 < planes:
            wide_theirs(red_pair, cols_pair, zz + 1)
        wide_mine(red_pair, cols_pair, zz)
        pending.steps += red_pair.plane_steps(zz)
        pending(1)
    load_gated = local.copy(gated_in, turned)
    w_out = down.at[pl.ds(0, D)]
    load_out = load_columns(local, fulls[1], pl.ds(0, D), w_out, stage)
    load_out += load_columns(local, fulls[1], pl.ds(D, PAD_ROWS), gain, stage)
    views = []
    for k, src in enumerate((q_in, k_in, v_in, raw_in)):
        for side in range(2):
            to = tall.at[pl.ds((2 * k + side) * rows, rows)]
            views.append(local.copy(src.at[:, pl.ds(side * (D // 2), D // 2)], to))

    f0[...] = jnp.zeros_like(f0)

    def back_pair(s, slot):
        f0[...] += dot_nt(pair[s], slots[slot])

    stream(seq, lambda s: fulls[2].at[s], slots, slot_sems, back_pair, lambda s: pending(1))
    load_mid.wait()

    def back_mid(r):
        m, grad = f1[r, :], f0[r, :]
        scale = lax.rsqrt(mean_square(m) + 1e-6)
        inner = jnp.mean(grad * m, axis=-1, keepdims=True)
        total = g[r, :].astype(F32) + scale * grad - m * (scale * scale * scale) * inner
        f1[r, :] = total
        low[r, :] = total.astype(BF16)

    row_loop(rows, 32, back_mid)
    save_gm = local.copy(f1, gm_hbm)
    split_columns(low)

    load_gated.wait()
    for k in range(2):
        slim_theirs(red_out, turned, k * (D // 2), k * (D // 2), D // 2, k)
    for k in range(2):
        slim_mine(red_out, turned, k * (D // 2), k * (D // 2), D // 2, k)
    load_na = local.copy(na_in, turned)
    pending(2)
    for made in load_out:
        made.wait()

    def back_branch(n, _):
        at = pl.ds(pl.multiple_of(n * 512, 512), 512)
        f0[:, at] = dot_nt(low[...], w_out[at, :])
        return 0

    lax.fori_loop(0, D // 512, back_branch, 0)
    load_x = local.copy(x_hbm, low)
    save_gm.wait()
    load_att = local.copy(att_in, f1)
    gain_sums[...] = jnp.zeros_like(gain_sums)
    for made in views:
        made.wait()
    load_att.wait()
    load_e.wait()

    def view(k, i, j):
        row = (2 * k + lax.div(j, pairs // 2)) * rows + i * span
        return tokens_at(row, span), lanes(lax.rem(j, pairs // 2))

    def tokens_at(row, count):
        return pl.ds(pl.multiple_of(row, count), count)

    def put(group, i, j, value):
        s = group * per_group + lax.div(j, per_block)
        pair[s, tokens(i, span), lanes(lax.rem(j, per_block))] = value.astype(BF16)

    def back_gate(n, _):
        i, j = lax.div(n, pairs), lax.rem(n, pairs)
        at, block = tokens(i, span), lanes(j)
        a, grad = f1[at, block], f0[at, block]
        scale = lax.rsqrt(head_sums(a * a, own) * (1.0 / HEAD_DIM) + 1e-5)
        unit = a * scale
        gains = gain[0:1, block].astype(F32)
        sig = jax.nn.sigmoid(tall[view(3, i, j)].astype(F32))
        grad_normed = grad * sig
        put(3, i, j, grad * (unit * gains) * sig * (1.0 - sig))
        gain_sums[0:1, block] += jnp.sum(grad_normed * unit, axis=0, keepdims=True)
        grad_unit = grad_normed * gains
        inner = head_sums(grad_unit * a, own) * (1.0 / HEAD_DIM)
        grad_a = (scale * grad_unit - a * (scale * scale * scale) * inner).astype(BF16)
        g[at, block] = grad_a
        mine[n] = pack_state(dot_tn(tall[view(0, i, j)], grad_a)).astype(BF16)
        return 0

    lax.fori_loop(0, blocks * pairs, back_gate, 0)
    chain = Chain(place, False, mine, other, before, chain_out, chain_sems)
    chain.start()

    for s in range(seq):
        to = (s // 2) * cols_out
        gain_split[s % 2, :, to : to + cols_out] = gain_sums[:, s * cols_out : (s + 1) * cols_out]
    top = lax.broadcasted_iota(jnp.int32, (GAIN_ROWS, cols_out), 0) == 0

    def gain_rows(which, zz):
        row = gain_split[which, 0:1, zz * cols_out : (zz + 1) * cols_out]
        return jnp.where(top, row, 0.0)

    def fill_gain(slot):
        for zz in range(planes):
            slim_out[slot, zz, 0:GAIN_ROWS, :] = gain_rows(sibling, zz).astype(BF16)

    slim_send(red_out, D, GAIN_ROWS, 2, fill_gain)
    load_na.wait()
    last = planes - 1
    ready = [zz for zz in range(planes) if zz * 2 >= 3 * per_group]
    for zz in ready:
        wide_theirs(red_in, cols_in, zz)
    for zz in range(planes):
        red_out.core_copy(zz, None, D, GAIN_ROWS, 2).wait_recv()
        here = red_out.part[zz, D : D + GAIN_ROWS, :].astype(F32) + gain_rows(core, zz)
        red_out.part[zz, D : D + GAIN_ROWS, :] = here.astype(BF16)
    for zz in ready:
        wide_mine(red_in, cols_in, zz)
    chain.step()
    pending.steps += red_out.z_steps()

    t_of = lax.rem(lax.broadcasted_iota(jnp.int32, (span, 2 * span), 1), span)
    s_of = lax.broadcasted_iota(jnp.int32, (span, 2 * span), 0)
    t_down = lax.rem(lax.broadcasted_iota(jnp.int32, (2 * span, span), 0), span)
    s_down = lax.broadcasted_iota(jnp.int32, (2 * span, span), 1)
    lane = lax.broadcasted_iota(jnp.int32, (span, 128), 1)

    def back_attention(n, _):
        i, j = lax.div(n, pairs), lax.rem(n, pairs)
        at, block = tokens(i, span), lanes(j)
        qs, ks, vs = (tall[view(k, i, j)] for k in range(3))
        grads = g[at, block]
        q2, g2 = by_head(qs, first, second), by_head(grads, first, second)
        scores = jnp.where(t_of >= s_of, dot_nt(ks, q2), 0.0).astype(BF16)
        grad_t = jnp.where(t_of >= s_of, dot_nt(vs, g2), 0.0).astype(BF16)
        grad_s = jnp.where(t_down >= s_down, dot_nt(g2, vs), 0.0).astype(BF16)
        both = dot(grad_s, ks)
        grad_q = jnp.where(lane < HEAD_DIM, both[:span], both[span:])
        grad_q = grad_q + dot_nt(grads, unpack_state(early[n], own))
        f0[at, block] = dot(grad_t, q2)
        f1[at, block] = dot(scores, g2)
        put(0, i, j, grad_q * slope(qs.astype(F32)))
        return 0

    for i in range(blocks):
        lax.fori_loop(i * pairs, (i + 1) * pairs, back_attention, 0)
        pending(2)
    ready_q = [zz for zz in range(planes) if (zz + 1) * 2 <= per_group]
    for zz in ready_q:
        wide_theirs(red_in, cols_in, zz)
    for zz in ready_q:
        wide_mine(red_in, cols_in, zz)
    chain.finish(other)

    def back_states(n, _):
        i, j = lax.div(n, pairs), lax.rem(n, pairs)
        at, block = tokens(i, span), lanes(j)
        ks, vs = tall[view(1, i, j)], tall[view(2, i, j)]
        later = unpack_state(other[n], own)
        grad_k = f0[at, block] + dot_nt(vs, later)
        put(1, i, j, grad_k * slope(ks.astype(F32)))
        put(2, i, j, f1[at, block] + dot(ks, later))
        return 0

    lax.fori_loop(0, blocks * pairs, back_states, 0)
    load_gm = local.copy(gm_hbm, f1)
    rest = [zz for zz in range(planes) if zz not in ready and zz not in ready_q]
    for n, zz in enumerate(rest):
        wide_theirs(red_in, cols_in, zz)
        if n:
            wide_mine(red_in, cols_in, rest[n - 1])
    if rest:
        wide_mine(red_in, cols_in, rest[-1])
    for red in (red_down, red_out):
        if place.square:
            pending.steps.append(functools.partial(red.plane_1, place.z))
    for red in (red_down, red_out):
        pending.steps += red.plane_steps(place.z)
    for red in (red_down, red_out):
        pending.steps.append(red.spread_1)
    pending.steps += red_pair.z_steps()
    pending.steps.append(red_pair.spread_1)
    for zz in ready + ready_q + rest:
        pending.steps += red_in.plane_steps(zz)
    pending.steps += red_in.z_steps()
    pending.steps.append(red_in.spread_1)
    for name in ("spread_2", "spread_3"):
        for red in (red_down, red_out, red_pair, red_in):
            pending.steps.append(getattr(red, name))

    f0[...] = jnp.zeros_like(f0)
    w_in = slots if cols_in == slots.shape[2] else slots.at[:, :, pl.ds(0, cols_in)]

    def back_in(s, slot):
        f0[...] += dot_nt(pair[s, :, 0:cols_in], w_in[slot])

    stream(seq, lambda s: fulls[0].at[s], w_in, slot_sems, back_in, lambda s: pending(3))
    load_gm.wait()
    load_x.wait()

    def back_x(r):
        x, grad = low[r, :].astype(F32), f0[r, :]
        scale = lax.rsqrt(mean_square(x) + 1e-6)
        inner = jnp.mean(grad * x, axis=-1, keepdims=True)
        f1[r, :] += scale * grad - x * (scale * scale * scale) * inner

    row_loop(rows, 32, back_x)
    local.save(f1, grad_hbm)
    pending.until(0)
    local.finish()
    for sent in slim_sent[-2:]:
        for made in sent:
            made().wait_send()
    for made in wide_sent[-2:]:
        made().wait_send()
    place.finish()


def backward(batch, seq, span, grad, x, fulls, saved):
    rows = x.shape[0]
    half = seq // 2
    cols_in, cols_out, cols_pair = fulls[0].shape[2], fulls[1].shape[2], fulls[2].shape[2]
    width = saved[10].shape[1]
    square = batch == 4
    shapes = ((FF, cols_out), (D, cols_pair), (D + GAIN_ROWS, cols_out), (D, cols_in))
    states = (rows // span) * (D // 128)
    any_space = pl.BlockSpec(memory_space=pl.ANY)
    big_f = jax.ShapeDtypeStruct((rows, D), F32)
    out_shape = [big_f] + [jax.ShapeDtypeStruct(shape, BF16) for shape in shapes] + [big_f]
    out_shape += [Reduce.far(square, WIDE[w], half, *shapes[w]) for w in range(4)]
    scratch = []
    core_parts = (half, 1, 3, 1)
    for w in range(4):
        scratch += Reduce.scratch(square, WIDE[w], half, *shapes[w], core_parts[w], Z_PARTS[w])
    narrow = cols_out % 128 != 0
    state = pltpu.VMEM((states, HEAD_DIM, 128), BF16)
    scratch += [
        pltpu.VMEM((max(FF, 8 * rows), D // 2), BF16),
        pltpu.VMEM((D, rows), BF16),
        pltpu.VMEM((seq, rows, cols_pair), BF16),
        pltpu.VMEM((16, 128), BF16),
        pltpu.VMEM((rows, D), F32),
        pltpu.VMEM((rows, D), F32),
        pltpu.VMEM((rows, D), BF16),
        pltpu.VMEM((rows, D), BF16),
        pltpu.VMEM((rows, D), BF16),
        pltpu.VMEM((max(2 * width, D), D), BF16),
        pltpu.VMEM((2, D, cols_pair), BF16),
        pltpu.VMEM((2, D, cols_pair), BF16),
        pltpu.VMEM((2, half, max(width, D // 2), cols_out), BF16),
        pltpu.VMEM((PAD_ROWS, D), BF16),
        pltpu.VMEM((8, D), F32),
        pltpu.VMEM((2, 8, D // 2), F32),
        state, state, state, state, state,
        pltpu.VMEM((D, cols_out) if narrow else (16, 128), BF16),
        pltpu.SemaphoreType.DMA((6,)),
        pltpu.SemaphoreType.DMA((2,)),
        pltpu.SemaphoreType.DMA((192,)),
    ]
    return pl.pallas_call(
        functools.partial(backward_kernel, batch, seq, span),
        out_shape=out_shape,
        in_specs=[any_space] * 18,
        out_specs=[any_space] * len(out_shape),
        scratch_shapes=scratch,
        compiler_params=pltpu.CompilerParams(
            collective_id=1, has_side_effects=True, vmem_limit_bytes=63 * 1024 * 1024
        ),
        name="backward",
    )(grad, x, *fulls, *saved)


def local(block_in, attn_in, attn_out, out_gain, glu_in, glu_out, block_grad):
    seq_count, span = block_in.shape[:2]
    rows = seq_count * span
    batch, seq = lax.axis_size("batch"), lax.axis_size("seq")
    x = block_in.reshape(rows, D)
    with_gain = jnp.concatenate([attn_out, jnp.broadcast_to(out_gain, (PAD_ROWS, out_gain.shape[0]))])
    parts = forward(batch, seq, x, span, (attn_in, with_gain, glu_in, glu_out))
    fulls, block_out, saved = parts[:4], parts[4], parts[5:]
    grads = backward(batch, seq, span, block_grad.reshape(rows, D), x, fulls, saved)
    input_grad, sums = grads[0], list(grads[1:5])
    if batch != 4:
        sums = [lax.psum(a, "batch") for a in sums]
    down, pair, out, into = (a.astype(F32) for a in sums)
    return (
        block_out.reshape(block_in.shape),
        input_grad.reshape(block_in.shape),
        into,
        out[:D],
        out[D],
        pair,
        down,
    )


def solution(mesh):
    rows, columns = P("batch", "seq", None), P(None, "seq")
    return jax.shard_map(
        local,
        mesh=mesh,
        in_specs=(rows, columns, columns, P("seq"), columns, columns, rows),
        out_specs=(rows, rows, columns, columns, P("seq"), columns, columns),
        check_vma=False,
    )
```

```python
import functools

import jax
import jax.numpy as jnp
from jax import lax
from jax.experimental import pallas as pl
from jax.experimental.pallas import tpu as pltpu
from jax.sharding import PartitionSpec as P

HEADS = 16
HEAD_DIM = 64
D = 1024
FF = 2816
MESH = pl.DeviceIdType.MESH
BF16 = jnp.bfloat16
F32 = jnp.float32
PAD_ROWS = 16
GAIN_ROWS = 128


def run_if(cond, fn):
    if cond is None:
        fn()
    else:
        pl.when(cond)(fn)


class Place:
    def __init__(self, batch, seq):
        self.planes = seq // 2
        self.square = batch == 4
        self.b = lax.axis_index("batch")
        self.s = lax.axis_index("seq")
        self.z = lax.div(self.s, 2)
        self.c = lax.rem(self.s, 2)
        self.bx = self.b + 1 - 2 * lax.rem(self.b, 2)
        self.by = lax.rem(self.b + 2, 4)
        self.bd = lax.rem(self.bx + 2, 4)
        self.sib = (self.b, self.s + 1 - 2 * self.c)
        self.up = (self.b, self.s + 2)
        self.down = (self.b, self.s - 2)
        self.x = (self.bx, self.s)
        self.y = (self.by, self.s)
        self.has_up = self.z < self.planes - 1
        self.has_down = self.z > 0
        self.sent = []

    def barrier(self):
        sem = pltpu.get_barrier_semaphore()
        always = [self.sib] + ([self.x, self.y] if self.square else [])
        for device in always:
            pl.semaphore_signal(sem, inc=1, device_id=device, device_id_type=MESH)
        for cond, device in ((self.has_up, self.up), (self.has_down, self.down)):
            pl.when(cond)(
                lambda device=device: pl.semaphore_signal(
                    sem, inc=1, device_id=device, device_id_type=MESH
                )
            )
        ends = self.has_up.astype(jnp.int32) + self.has_down.astype(jnp.int32)
        pl.semaphore_wait(sem, len(always) + ends)

    def copy(self, src, dst, send_sem, recv_sem, device):
        return pltpu.make_async_remote_copy(
            src_ref=src,
            dst_ref=dst,
            send_sem=send_sem,
            recv_sem=recv_sem,
            device_id=device,
            device_id_type=MESH,
        )

    def send(self, make, cond=None):
        run_if(cond, lambda: make().start())
        self.sent.append((cond, make))

    def finish(self):
        for cond, make in self.sent:
            run_if(cond, lambda make=make: make().wait_send())
        self.sent = []


class Gather:
    Z_UP, Z_DOWN, Z_IN, X_OUT, X_IN, Y_OUT, Y_IN, FX_OUT, FX_IN, FY_OUT, FY_IN = range(11)
    S_OUT, S_IN = 11, 15
    KINDS = 19

    def __init__(self, place, shards, held, fulls, quartered, sems, local_sems):
        self.p, self.shards, self.held, self.fulls, self.sems = place, shards, held, fulls, sems
        self.local_sems = local_sems
        for w, shard in enumerate(shards):
            pltpu.make_async_copy(shard, held[w], local_sems.at[0, w]).start()
        self.quartered = [q and place.square for q in quartered]

    def rows(self, w, owner, half=None):
        rows = self.shards[w].shape[0]
        if not self.quartered[w]:
            return pl.ds(0, rows)
        part = rows // 4
        if half is None:
            return pl.ds(pl.multiple_of(owner * part, 16), part)
        return pl.ds(pl.multiple_of(owner * part + half * (part // 2), 16), part // 2)

    def move(self, w, zz, rows, out, into, device, core=None):
        core = self.p.c if core is None else core
        block = self.fulls[w].at[2 * zz + core, rows]
        return self.p.copy(
            block, block, self.sems.at[out, w, zz], self.sems.at[into, w, zz], device
        )

    def across(self, w, zz, piece, core=None):
        p = self.p
        rows = self.rows(w, (p.b, p.bx, p.by, p.bd)[piece])
        return self.move(w, zz, rows, self.S_OUT + piece, self.S_IN + piece, p.sib, core)

    def whole(self, w):
        p = self.p
        here = self.fulls[w].at[p.s]
        return p.copy(
            self.held[w], here, self.sems.at[self.S_OUT, w, p.z], self.sems.at[self.S_IN, w, p.z], p.sib
        )

    def start(self, w):
        p, own = self.p, self.held[w]
        here = self.fulls[w].at[p.s]
        pltpu.make_async_copy(self.shards[w], own, self.local_sems.at[0, w]).wait()
        rows = self.rows(w, p.b)
        for cond, device, out in (
            (p.has_up, p.up, self.Z_UP),
            (p.has_down, p.down, self.Z_DOWN),
        ):
            p.send(
                lambda device=device, out=out: p.copy(
                    own.at[rows],
                    here.at[rows],
                    self.sems.at[out, w, p.z],
                    self.sems.at[self.Z_IN, w, p.z],
                    device,
                ),
                cond,
            )
        p.send(lambda: self.whole(w))
        pltpu.make_async_copy(own, here, self.local_sems.at[1, w]).start()

    def sides(self, d):
        p = self.p
        return (
            (p.z >= d, p.z - d, p.has_up, p.up, self.Z_UP),
            (p.z + d < p.planes, p.z + d, p.has_down, p.down, self.Z_DOWN),
        )

    def from_z(self, w, d):
        p = self.p
        rows = self.rows(w, p.b)
        for cond, zz, more, device, out in self.sides(d):
            run_if(
                cond, lambda zz=zz: self.move(w, zz, rows, self.Z_UP, self.Z_IN, p.up).wait_recv()
            )
            p.send(
                lambda zz=zz, device=device, out=out: self.move(
                    w, zz, rows, out, self.Z_IN, device
                ),
                jnp.logical_and(cond, more),
            )
            p.send(lambda zz=zz: self.across(w, zz, 0), cond)

    def to_plane(self, w, d):
        p = self.p
        rows = self.rows(w, p.b)
        for cond, zz, *_ in self.sides(d):
            p.send(lambda zz=zz: self.move(w, zz, rows, self.X_OUT, self.X_IN, p.x), cond)
            p.send(lambda zz=zz: self.move(w, zz, rows, self.Y_OUT, self.Y_IN, p.y), cond)

    def from_plane(self, w, d):
        p = self.p
        from_x, from_y = self.rows(w, p.bx), self.rows(w, p.by)
        half_x, half_y = self.rows(w, p.bx, 0), self.rows(w, p.by, 1)
        for cond, zz, *_ in self.sides(d):
            run_if(
                cond, lambda zz=zz: self.move(w, zz, from_x, self.X_OUT, self.X_IN, p.x).wait_recv()
            )
            p.send(lambda zz=zz: self.move(w, zz, half_x, self.FY_OUT, self.FY_IN, p.y), cond)
            run_if(
                cond, lambda zz=zz: self.move(w, zz, from_y, self.Y_OUT, self.Y_IN, p.y).wait_recv()
            )
            p.send(lambda zz=zz: self.move(w, zz, half_y, self.FX_OUT, self.FX_IN, p.x), cond)
            p.send(lambda zz=zz: self.across(w, zz, 1), cond)
            p.send(lambda zz=zz: self.across(w, zz, 2), cond)

    def from_diagonal(self, w, d):
        p = self.p
        half_0, half_1 = self.rows(w, p.bd, 0), self.rows(w, p.bd, 1)
        for cond, zz, *_ in self.sides(d):
            run_if(
                cond,
                lambda zz=zz: self.move(w, zz, half_0, self.FY_OUT, self.FY_IN, p.y).wait_recv(),
            )
            run_if(
                cond,
                lambda zz=zz: self.move(w, zz, half_1, self.FX_OUT, self.FX_IN, p.x).wait_recv(),
            )
            p.send(lambda zz=zz: self.across(w, zz, 3), cond)

    def nearest(self, k):
        planes = self.p.planes
        found = jnp.int32(0)
        for z in range(planes):
            order = sorted(range(planes), key=lambda t: (abs(t - z), t))
            found = jnp.where(self.p.z == z, order[k], found)
        return found

    def have(self, w, k):
        p = self.p
        if k == 0:
            pltpu.make_async_copy(
                self.held[w], self.fulls[w].at[p.s], self.local_sems.at[1, w]
            ).wait()
            self.whole(w).wait_recv()
            return p.z
        zz = self.nearest(k)
        for piece in range(4 if self.quartered[w] else 1):
            self.across(w, zz, piece, 1 - p.c).wait_recv()
        return zz


class Steps:
    def __init__(self, table):
        self.table, self.todo, self.ticks = table, {}, 0

    def add(self, name, fn, *args):
        self.todo[name] = functools.partial(fn, *args)

    def run(self, name):
        step = self.todo.pop(name, None)
        if step is not None:
            step()

    def tick(self):
        for name in self.table.get(self.ticks, ()):
            self.run(name)
        self.ticks += 1

    def finish(self, wanted=lambda name: True):
        for name in [name for name in self.todo if wanted(name)]:
            self.run(name)


def plan_gather(steps, g, count):
    far = g.p.planes - 1
    for w in range(count):
        steps.add(("start", w), g.start, w)
        for d in range(1, far + 1):
            steps.add(("z", w, d), g.from_z, w, d)
        if g.quartered[w]:
            for name, step in (("x", g.to_plane), ("p", g.from_plane), ("g", g.from_diagonal)):
                for d in range(1, far + 1):
                    steps.add((name, w, d), step, w, d)


def add_into(dst, src, row, rows):
    cols = dst.shape[-1]
    chunk = max(
        k for k in range(16, rows + 1, 16) if rows % k == 0 and (k * cols <= 49152 or k == 16)
    )

    def body(i, _):
        here = pl.ds(pl.multiple_of(row + i * chunk, 16), chunk)
        there = pl.ds(pl.multiple_of(i * chunk, 16), chunk)
        dst[here, :] = (dst[here, :].astype(F32) + src[there, :].astype(F32)).astype(BF16)
        return 0

    lax.fori_loop(0, rows // chunk, body, 0)


class Reduce:
    (X1_OUT, X1_IN, Y1_OUT, Y1_IN, X2_OUT, X2_IN, Y2_OUT, Y2_IN, X3_OUT, X3_IN, Y3_OUT, Y3_IN) = range(12)
    KINDS = 12
    S_OUT, S_IN = range(2)
    Z_UP, Z_UP_IN, Z_DOWN, Z_DOWN_IN, FETCH = range(5)
    GX_OUT, GX_IN, GY_OUT, GY_IN, FX_OUT, FX_IN, FY_OUT, FY_IN, LOCAL = range(9)
    LAST_KINDS = 9

    def __init__(self, place, wide, z_parts, out, zin_far, refs):
        self.p, self.wide, self.out = place, wide and place.square, out
        self.part, self.x1, self.y1, self.x2, self.y2, zin, self.stage = refs[:7]
        self.core_sems, self.sems, self.z_sems, self.last_sems = refs[7:]
        self.zin = zin if self.wide else zin_far
        self.total = self.part.shape[1]
        self.quarter, self.half = self.total // 4, self.total // 8
        self.z_parts = 1 if self.wide else z_parts

    @staticmethod
    def scratch(square, wide, planes, rows, cols, core_parts, z_parts):
        wide = wide and square
        pieces = planes if wide else 1
        small = (pieces, rows // 8, cols) if square else (1, 16, 128)
        large = (pieces, rows // 4, cols) if square else (1, 16, 128)
        return [
            pltpu.VMEM((planes, rows, cols), BF16),
            pltpu.VMEM(small, BF16),
            pltpu.VMEM(small, BF16),
            pltpu.VMEM(large, BF16),
            pltpu.VMEM(large, BF16),
            pltpu.VMEM((planes + 1, rows // 4, cols) if wide else (1, 16, 128), BF16),
            pltpu.VMEM((16, 128) if wide else (rows // z_parts, cols), BF16),
            pltpu.SemaphoreType.DMA((2, planes, core_parts)),
            pltpu.SemaphoreType.DMA((Reduce.KINDS, pieces)),
            pltpu.SemaphoreType.DMA((5, planes + 1, z_parts)),
            pltpu.SemaphoreType.DMA((Reduce.LAST_KINDS,)),
        ]

    @staticmethod
    def far(square, wide, planes, rows, cols):
        shape = (1, 16, 128) if wide and square else (planes + 1, rows, cols)
        return jax.ShapeDtypeStruct(shape, BF16)

    def at(self, owner, half=None):
        if half is None:
            return pl.ds(pl.multiple_of(owner * self.quarter, 16), self.quarter)
        return pl.ds(pl.multiple_of(owner * self.quarter + half * self.half, 16), self.half)

    def sem(self, kind, k):
        return self.sems.at[kind, k]

    def core_copy(self, zz, src, row, rows, k):
        block = self.part.at[zz, pl.ds(row, rows)]
        return self.p.copy(
            block if src is None else src,
            block,
            self.core_sems.at[self.S_OUT, zz, k],
            self.core_sems.at[self.S_IN, zz, k],
            self.p.sib,
        )

    def slot(self, zz):
        return zz if self.wide else 0

    def hop(self, zz, rows, dst, out, into, device):
        return self.p.copy(
            self.part.at[zz, rows],
            dst,
            self.sem(out, self.slot(zz)),
            self.sem(into, self.slot(zz)),
            device,
        )

    def plane_1(self, zz):
        p, k, h = self.p, self.slot(zz), self.half
        lo, hi = pl.ds(0, h), pl.ds(h, h)
        p.send(lambda: self.hop(zz, self.at(p.bd, 0), self.x1.at[k], self.X1_OUT, self.X1_IN, p.x))
        p.send(lambda: self.hop(zz, self.at(p.bd, 1), self.y1.at[k], self.Y1_OUT, self.Y1_IN, p.y))
        p.send(lambda: self.hop(zz, self.at(p.bx, 0), self.x2.at[k, lo], self.X2_OUT, self.X2_IN, p.x))
        p.send(lambda: self.hop(zz, self.at(p.by, 1), self.y2.at[k, hi], self.Y2_OUT, self.Y2_IN, p.y))

    def plane_2(self, zz):
        p, k, h = self.p, self.slot(zz), self.half
        lo, hi = pl.ds(0, h), pl.ds(h, h)
        self.hop(zz, self.at(p.bd, 0), self.x1.at[k], self.X1_OUT, self.X1_IN, p.x).wait_recv()
        add_into(self.part.at[zz], self.x1.at[k], p.by * self.quarter, h)
        p.send(lambda: self.hop(zz, self.at(p.by, 0), self.y2.at[k, lo], self.Y3_OUT, self.Y3_IN, p.y))
        self.hop(zz, self.at(p.bd, 1), self.y1.at[k], self.Y1_OUT, self.Y1_IN, p.y).wait_recv()
        add_into(self.part.at[zz], self.y1.at[k], p.bx * self.quarter + h, h)
        p.send(lambda: self.hop(zz, self.at(p.bx, 1), self.x2.at[k, hi], self.X3_OUT, self.X3_IN, p.x))

    def plane_3(self, zz):
        p, k, h = self.p, self.slot(zz), self.half
        lo, hi = pl.ds(0, h), pl.ds(h, h)
        self.hop(zz, self.at(p.bx, 0), self.x2.at[k, lo], self.X2_OUT, self.X2_IN, p.x).wait_recv()
        self.hop(zz, self.at(p.by, 1), self.y2.at[k, hi], self.Y2_OUT, self.Y2_IN, p.y).wait_recv()
        self.hop(zz, self.at(p.bx, 1), self.x2.at[k, hi], self.X3_OUT, self.X3_IN, p.x).wait_recv()
        add_into(self.part.at[zz], self.x2.at[k], p.b * self.quarter, self.quarter)
        self.hop(zz, self.at(p.by, 0), self.y2.at[k, lo], self.Y3_OUT, self.Y3_IN, p.y).wait_recv()
        add_into(self.part.at[zz], self.y2.at[k], p.b * self.quarter, self.quarter)

    def z_rows(self, k):
        p = self.p
        rows = self.total // self.z_parts
        return (p.b * self.quarter, self.quarter) if self.wide else (k * rows, rows)

    def z_slot(self, zz, upward, k):
        slot = zz + 1 if upward else zz
        if self.wide:
            return self.zin.at[slot]
        row, rows = self.z_rows(k)
        return self.zin.at[slot, pl.ds(row, rows)]

    def z_hop(self, zz, upward, k):
        p = self.p
        row, rows = self.z_rows(k)
        here = pl.ds(pl.multiple_of(row, 16), rows)
        out, into = (self.Z_UP, self.Z_UP_IN) if upward else (self.Z_DOWN, self.Z_DOWN_IN)
        return p.copy(
            self.part.at[zz, here],
            self.z_slot(zz, upward, k),
            self.z_sems.at[out, zz, k],
            self.z_sems.at[into, zz, k],
            p.up if upward else p.down,
        )

    def z_take(self, zz, upward, k):
        self.z_hop(zz, upward, k).wait_recv()
        row, rows = self.z_rows(k)
        src = self.z_slot(zz, upward, k)
        if not self.wide:
            slot = zz + 1 if upward else zz
            fetch = pltpu.make_async_copy(src, self.stage, self.z_sems.at[self.FETCH, slot, k])
            fetch.start()
            fetch.wait()
            src = self.stage
        add_into(self.part.at[zz], src, row, rows)

    def z_step(self, zz, d, k):
        p = self.p
        for upward, at in ((True, zz - d), (False, zz + d)):
            if not 0 <= at < p.planes:
                continue

            @pl.when(p.z == at)
            def _(upward=upward, at=at):
                if at != (0 if upward else p.planes - 1):
                    self.z_take(zz, upward, k)
                self.z_hop(zz, upward, k).start()

            p.sent.append((p.z == at, functools.partial(self.z_hop, zz, upward, k)))

    def z_last(self, zz, k):
        @pl.when(self.p.z == zz)
        def _():
            if zz > 0:
                self.z_take(zz, True, k)
            if zz < self.p.planes - 1:
                self.z_take(zz, False, k)

    def z_plan(self, steps, r, zz):
        for k in range(self.z_parts):
            for d in range(max(zz, self.p.planes - 1 - zz), 0, -1):
                steps.add(("z", r, zz, d, k), self.z_step, zz, d, k)
            steps.add(("zl", r, zz, k), self.z_last, zz, k)

    def plane_plan(self, steps, r, zz):
        if self.p.square:
            steps.add(("p2", r, zz), self.plane_2, zz)
            steps.add(("p3", r, zz), self.plane_3, zz)

    def late_plan(self, steps, r):
        if self.p.square:
            for n, step in enumerate((self.plane_1, self.plane_2, self.plane_3)):
                steps.add(("p%d" % (n + 1), r, -1), step, self.p.z)

    def spread_plan(self, steps, r):
        for n, step in enumerate((self.spread_1, self.spread_2, self.spread_3)):
            steps.add(("s%d" % (n + 1), r), step)

    def last_hop(self, src, rows, out, into, device):
        return self.p.copy(
            src, self.out.at[rows], self.last_sems.at[out], self.last_sems.at[into], device
        )

    def spread_1(self):
        p = self.p
        if not p.square:
            pltpu.make_async_copy(self.part.at[p.z], self.out, self.last_sems.at[self.LOCAL]).start()
            return
        rows = self.at(p.b)
        src = self.part.at[p.z, rows]
        p.send(lambda: self.last_hop(src, rows, self.GX_OUT, self.GX_IN, p.x))
        p.send(lambda: self.last_hop(src, rows, self.GY_OUT, self.GY_IN, p.y))
        pltpu.make_async_copy(src, self.out.at[rows], self.last_sems.at[self.LOCAL]).start()

    def spread_2(self):
        p = self.p
        if not p.square:
            return
        from_x, from_y = self.at(p.bx), self.at(p.by)
        half_x, half_y = self.at(p.bx, 0), self.at(p.by, 1)
        self.last_hop(self.out.at[from_x], from_x, self.GX_OUT, self.GX_IN, p.x).wait_recv()
        p.send(lambda: self.last_hop(self.out.at[half_x], half_x, self.FY_OUT, self.FY_IN, p.y))
        self.last_hop(self.out.at[from_y], from_y, self.GY_OUT, self.GY_IN, p.y).wait_recv()
        p.send(lambda: self.last_hop(self.out.at[half_y], half_y, self.FX_OUT, self.FX_IN, p.x))

    def spread_3(self):
        p = self.p
        if not p.square:
            pltpu.make_async_copy(self.part.at[p.z], self.out, self.last_sems.at[self.LOCAL]).wait()
            return
        rows = self.at(p.b)
        half_0, half_1 = self.at(p.bd, 0), self.at(p.bd, 1)
        self.last_hop(self.out.at[half_0], half_0, self.FY_OUT, self.FY_IN, p.y).wait_recv()
        self.last_hop(self.out.at[half_1], half_1, self.FX_OUT, self.FX_IN, p.x).wait_recv()
        pltpu.make_async_copy(
            self.part.at[p.z, rows], self.out.at[rows], self.last_sems.at[self.LOCAL]
        ).wait()


FORWARD_STEPS = {
    0: (('start', 0), ('z', 0, 1), ('x', 0, 1), ('start', 3), ('z', 0, 2), ('start', 2), ('x', 0, 2), ('start', 1), ('p', 0, 1),),
    1: (('p', 0, 2), ('z', 0, 3), ('x', 0, 3), ('z', 3, 1),),
    2: (('x', 3, 1), ('g', 0, 1),),
    4: (('g', 0, 2), ('z', 2, 1),),
    5: (('p', 0, 3), ('x', 2, 1),),
    6: (('g', 0, 3),),
    7: (('z', 3, 2), ('z', 1, 1), ('x', 3, 2),),
    10: (('z', 2, 2), ('p', 3, 1),),
    11: (('c', 0), ('x', 2, 2), ('z', 3, 3), ('z', 1, 2),),
    12: (('c', 1), ('g', 3, 1), ('x', 3, 3),),
    13: (('z', 2, 3), ('c', 2), ('x', 2, 3),),
    14: (('p', 3, 3), ('p', 2, 1), ('p', 2, 2),),
    15: (('p', 3, 2), ('z', 1, 3), ('c', 3), ('p', 2, 3),),
    16: (('g', 3, 3),),
    18: (('g', 2, 1),),
    22: (('g', 2, 2),),
    24: (('g', 2, 3),),
    37: (('g', 3, 2),),
}
BACKWARD_STEPS = {
    0: (('z', 0, 1, 2, 0), ('z', 0, 3, 3, 0),),
    4: (('z', 0, 0, 3, 0),),
    5: (('z', 0, 3, 3, 1), ('z', 0, 0, 3, 1),),
    6: (('z', 0, 3, 2, 0), ('z', 0, 1, 1, 0), ('z', 0, 2, 2, 1), ('z', 0, 1, 2, 1),),
    7: (('z', 0, 2, 2, 0),),
    9: (('z', 0, 0, 2, 0),),
    10: (('p2', 1, 0),),
    11: (('z', 0, 3, 1, 0),),
    12: (('z', 0, 0, 2, 1),),
    13: (('z', 0, 3, 2, 1),),
    14: (('z', 0, 0, 1, 0),),
    16: (('z', 0, 1, 1, 1),),
    18: (('p3', 1, 0), ('zl', 0, 3, 0),),
    19: (('z', 0, 0, 1, 1), ('z', 0, 2, 1, 1),),
    20: (('p2', 1, 2), ('z', 1, 0, 3, 0),),
    22: (('z', 0, 2, 1, 0),),
    23: (('p2', 1, 1),),
    24: (('z', 0, 3, 1, 1),),
    26: (('z', 1, 0, 2, 0), ('c', 0), ('zl', 0, 2, 1),),
    27: (('p2', 1, 3), ('p3', 1, 2), ('zl', 0, 2, 0), ('zl', 0, 1, 0),),
    28: (('zl', 0, 0, 1), ('zl', 0, 1, 1),),
    29: (('z', 2, 0, 3, 0), ('zl', 0, 3, 1), ('p3', 1, 3), ('c', 1),),
    30: (('z', 1, 2, 2, 0), ('z', 1, 3, 3, 0),),
    31: (('p2', 3, 3),),
    32: (('z', 2, 1, 2, 0), ('zl', 0, 0, 0), ('c', 2), ('z', 1, 2, 1, 0), ('p1', 0, -1),),
    33: (('z', 2, 2, 2, 0),),
    34: (('p3', 1, 1), ('z', 1, 3, 2, 0), ('z', 2, 0, 2, 0), ('p2', 0, -1), ('p3', 3, 3),),
    35: (('c', 3),),
    36: (('z', 1, 1, 2, 0), ('z', 2, 3, 3, 0), ('z', 2, 2, 1, 0),),
    37: (('p2', 3, 0),),
    38: (('p3', 0, -1), ('s1', 0), ('z', 1, 0, 1, 0),),
    39: (('z', 1, 3, 1, 0), ('z', 2, 3, 2, 0), ('z', 3, 3, 3, 0),),
    40: (('z', 3, 3, 2, 0), ('p3', 3, 0), ('z', 3, 0, 3, 0),),
    41: (('z', 1, 1, 1, 0),),
    42: (('z', 2, 1, 1, 0), ('z', 2, 0, 1, 0), ('zl', 1, 2, 0),),
    43: (('p2', 3, 1), ('zl', 1, 3, 0), ('zl', 1, 0, 0), ('z', 2, 3, 1, 0),),
    44: (('z', 3, 0, 2, 0), ('zl', 1, 1, 0),),
    45: (('p2', 3, 2),),
    46: (('p3', 3, 1), ('z', 3, 1, 2, 0), ('s1', 1), ('zl', 2, 1, 0), ('z', 3, 3, 1, 0),),
    47: (('p3', 3, 2), ('zl', 2, 2, 0), ('z', 3, 2, 2, 0),),
    48: (('zl', 2, 0, 0), ('z', 3, 0, 1, 0), ('zl', 2, 3, 0), ('p1', 2, -1),),
    49: (('z', 3, 1, 1, 0), ('s2', 0), ('z', 3, 2, 1, 0), ('p2', 2, -1), ('s2', 1),),
    50: (('zl', 3, 3, 0), ('p3', 2, -1), ('s3', 0), ('s1', 2), ('zl', 3, 0, 0), ('zl', 3, 1, 0), ('zl', 3, 2, 0), ('s1', 3),),
    51: (('s2', 2), ('s2', 3), ('s3', 1), ('s3', 2), ('s3', 3),),
}


def dot(a, b):
    return jnp.dot(a, b, preferred_element_type=F32)


def dot_nt(a, b):
    return lax.dot_general(a, b, (((1,), (1,)), ((), ())), preferred_element_type=F32)


def dot_tn(a, b):
    return lax.dot_general(a, b, (((0,), (0,)), ((), ())), preferred_element_type=F32)


def row_loop(rows, chunk, body):
    def step(i, _):
        body(pl.ds(pl.multiple_of(i * chunk, chunk), chunk))
        return 0

    lax.fori_loop(0, rows // chunk, step, 0)


def lanes(block, width=128):
    return pl.ds(pl.multiple_of(block * width, width), width)


def tokens(i, span):
    return pl.ds(pl.multiple_of(i * span, span), span)


def transpose(src, dst):
    rows, cols = src.shape
    whole = cols // 128

    def step(j, _):
        at = lanes(j)
        dst[at, :] = src[:, at].T
        return 0

    lax.fori_loop(0, whole, step, 0)
    if cols % 128:
        dst[whole * 128 :, :] = src[:, whole * 128 :].T


def mean_square(v):
    return jnp.mean(v * v, axis=-1, keepdims=True)


def pair_masks(span):
    lane = lax.broadcasted_iota(jnp.int32, (span, 128), 1)
    first = (lane < HEAD_DIM).astype(F32)
    row = lax.broadcasted_iota(jnp.int32, (128, 128), 0)
    col = lax.broadcasted_iota(jnp.int32, (128, 128), 1)
    own = ((row < HEAD_DIM) == (col < HEAD_DIM)).astype(F32)
    return first.astype(BF16), (1.0 - first).astype(BF16), own.astype(BF16), own


def by_head(pair, first, second):
    return jnp.concatenate([pair * first, pair * second], axis=0)


def pack_state(state):
    lane = lax.broadcasted_iota(jnp.int32, (HEAD_DIM, 128), 1)
    return jnp.where(lane < HEAD_DIM, state[:HEAD_DIM], state[HEAD_DIM:])


def unpack_state(packed, own):
    return jnp.concatenate([packed, packed], axis=0) * own


def head_sums(v, own):
    return dot(v.astype(BF16), own)


def grouped(lo, hi, compute, store, size=4):
    def step(m, _):
        first = lo + m * size
        results = [compute(first + u) for u in range(size)]
        for u in range(size):
            store(first + u, results[u])
        return 0

    lax.fori_loop(0, (hi - lo) // size, step, 0)


class Chain:
    S_OUT, S_IN, Z_OUT, Z_IN, P_OUT, P_IN = range(6)

    def __init__(self, place, forward, mine, other, before, out, sems):
        self.p, self.forward = place, forward
        self.mine, self.other, self.before, self.out, self.sems = mine, other, before, out, sems
        self.half = mine.shape[0] // 2
        if forward:
            self.prev, self.next = place.has_down, place.has_up
            self.device, self.counts = place.up, place.c == 1
        else:
            self.prev, self.next = place.has_up, place.has_down
            self.device, self.counts = place.down, place.c == 0

    @staticmethod
    def scratch(count):
        return [pltpu.VMEM((count, HEAD_DIM, 128), BF16)] * 4 + [pltpu.SemaphoreType.DMA((6,))]

    def part(self, core):
        return pl.ds(core * self.half, self.half)

    def sibling_copy(self):
        return self.p.copy(
            self.mine, self.other, self.sems.at[self.S_OUT], self.sems.at[self.S_IN], self.p.sib
        )

    def next_copy(self):
        here = self.part(self.p.c)
        return self.p.copy(
            self.out.at[here], self.before.at[here], self.sems.at[self.Z_OUT],
            self.sems.at[self.Z_IN], self.device,
        )

    def across_copy(self, core):
        here = self.part(core)
        return self.p.copy(
            self.before.at[here], self.before.at[here], self.sems.at[self.P_OUT],
            self.sems.at[self.P_IN], self.p.sib,
        )

    def start(self):
        self.p.send(self.sibling_copy)

        @pl.when(jnp.logical_not(self.prev))
        def _():
            self.before[...] = jnp.zeros_like(self.before)

    def step(self, h):
        p = self.p
        here = p.z == (h if self.forward else p.planes - 1 - h)

        @pl.when(here)
        def _():
            self.sibling_copy().wait_recv()
            if h > 0:
                self.next_copy().wait_recv()
                self.across_copy(p.c).start()
            if h < p.planes - 1:

                def body(i, _):
                    k = p.c * self.half + i
                    total = self.before[k].astype(F32) + self.mine[k].astype(F32)
                    self.out[k] = (total + self.other[k].astype(F32)).astype(BF16)
                    return 0

                lax.fori_loop(0, self.half, body, 0)
                self.next_copy().start()

        if h > 0:
            p.sent.append((here, lambda: self.across_copy(p.c)))
        if h < p.planes - 1:
            p.sent.append((here, self.next_copy))

    def plan(self, steps):
        for h in range(self.p.planes):
            steps.add(("c", h), self.step, h)

    def finish(self, result):
        p = self.p
        pl.when(self.prev)(lambda: self.across_copy(1 - p.c).wait_recv())
        weight = self.counts.astype(F32)

        def body(k, _):
            total = self.before[k].astype(F32) + self.other[k].astype(F32) * weight
            result[k] = total.astype(BF16)
            return 0

        lax.fori_loop(0, result.shape[0], body, 0)


class Locals:
    def __init__(self, sems):
        self.sems, self.used, self.open = sems, 0, []

    def copy(self, src, dst):
        made = pltpu.make_async_copy(src, dst, self.sems.at[self.used])
        self.used += 1
        made.start()
        return made

    def save(self, src, dst):
        self.open.append(self.copy(src, dst))

    def finish(self):
        for made in self.open:
            made.wait()


def load_columns(local, full, rows, dst, stage):
    seq, _, cols = full.shape
    if cols % 128 == 0:
        return [local.copy(full.at[s, rows], dst.at[:, pl.ds(s * cols, cols)]) for s in range(seq)]
    for s in range(seq):
        local.copy(full.at[s, rows], stage.at[pl.ds(0, rows.size)]).wait()
        dst[:, s * cols : (s + 1) * cols] = stage[: rows.size]
    return []


def load_plane(local, full, rows, zz, dst, stage):
    cols = full.shape[2]
    if cols % 128 == 0:
        return [
            local.copy(full.at[2 * zz + core, rows], dst.at[:, pl.ds(core * cols, cols)])
            for core in range(2)
        ]
    for core in range(2):
        local.copy(full.at[2 * zz + core, rows], stage.at[core, pl.ds(0, rows.size)]).wait()
    dst[...] = jnp.concatenate([stage[0, 0 : rows.size], stage[1, 0 : rows.size]], axis=1)
    return []


def stream(order, source, slots, sems, body, after):
    def fetch(n):
        return pltpu.make_async_copy(source(order[n]), slots.at[n % 2], sems.at[n % 2])

    fetch(0).start()
    for n, s in enumerate(order):
        if n + 1 < len(order):
            fetch(n + 1).start()
        fetch(n).wait()
        body(s, n % 2)
        after()


def forward_kernel(batch, seq, spans, *refs):
    (x_hbm, *shards), refs = refs[:5], refs[5:]
    fulls, refs = refs[:4], refs[4:]
    out_hbm, saved, refs = refs[0], refs[1:13], refs[13:]
    (q_out, k_out, v_out, raw_out, att_out, e_out, gated_out, mid_out, nb_out, pair_out, hid_out, na_out) = saved
    (x, na, tmp, qkvr, att, gated, mid, nb, w_in, w_out, gain, w_pair, tmp_g, tmp_u, pair, hid,
     w_down, res, stage, na_t, gated_t, nb_t, hid_t, mine, other, before, chain_out, early, chain_sems, slot_sems, pair_sems,
     local_sems, gather_sems, gather_local, *held) = refs
    place = Place(batch, seq)
    local = Locals(local_sems)
    gather = Gather(place, shards, held, fulls, (True, False, True, True), gather_sems, gather_local)
    load_x = local.copy(x_hbm, x)
    place.barrier()
    rows, span = x.shape[0], spans
    per_group = seq // 4
    blocks = rows // span
    pairs = D // 128
    cols_in = w_in.shape[-1]
    half = seq // 2
    planes = place.planes
    cols_two = 2 * fulls[1].shape[2]
    q, k, v, raw = (qkvr.at[n] for n in range(4))
    first, second, own, own_f = pair_masks(span)
    steps = Steps(FORWARD_STEPS if place.square and place.planes == 4 else {})
    plan_gather(steps, gather, 4)

    def have(w, n):
        steps.finish(lambda name: not steps.table and name[0] != "c" and name[1] <= w)
        return gather.have(w, n)

    steps.tick()
    load_x.wait()

    def norm_rows(r):
        xr = x[r, :].astype(F32)
        na[r, :] = (xr * lax.rsqrt(mean_square(xr) + 1e-6)).astype(BF16)

    row_loop(rows, 64, norm_rows)
    steps.tick()

    def project(s, slot):
        group, n = lax.div(s, per_group), lax.rem(s, per_group)
        tmp[...] = dot(na[...], w_in[slot])
        at = pl.ds(pl.multiple_of(n * cols_in, 128), cols_in)

        @pl.when(s < 2 * per_group)
        def _():
            def finish_rows(r):
                value = tmp[r, :]
                value = jnp.maximum(value, 0.0) + jnp.log1p(jnp.exp(-jnp.abs(value)))
                qkvr[group, r, at] = value.astype(BF16)

            row_loop(rows, 64, finish_rows)

        @pl.when(s >= 2 * per_group)
        def _():
            def finish_rows(r):
                qkvr[group, r, at] = tmp[r, :].astype(BF16)

            row_loop(rows, 64, finish_rows)

    for n in range(planes):
        zz = have(0, n)
        blocks_in = [
            pltpu.make_async_copy(fulls[0].at[2 * zz + c], w_in.at[c], slot_sems.at[c]) for c in range(2)
        ]
        for made in blocks_in:
            made.start()
        for c, made in enumerate(blocks_in):
            made.wait()
            project(2 * zz + c, c)
            steps.tick()

    def state(n):
        i, j = lax.div(n, pairs), lax.rem(n, pairs)
        at, block = tokens(i, span), lanes(j)
        return pack_state(dot_tn(k[at, block], v[at, block])).astype(BF16)

    def keep_state(n, value):
        mine[n] = value

    grouped(0, blocks * pairs, state, keep_state)
    chain = Chain(place, True, mine, other, before, chain_out, chain_sems)
    chain.start()
    chain.plan(steps)
    for src, dst in ((q, q_out), (k, k_out), (v, v_out), (raw, raw_out)):
        local.save(src, dst)
    steps.tick()

    row = lax.rem(lax.broadcasted_iota(jnp.int32, (2 * span, span), 0), span)
    col = lax.broadcasted_iota(jnp.int32, (2 * span, span), 1)
    lane = lax.broadcasted_iota(jnp.int32, (span, 128), 1)

    def inner(n):
        i, j = lax.div(n, pairs), lax.rem(n, pairs)
        at, block = tokens(i, span), lanes(j)
        scores = dot_nt(by_head(q[at, block], first, second), k[at, block])
        scores = jnp.where(row >= col, scores, 0.0).astype(BF16)
        both = dot(scores, v[at, block])
        return jnp.where(lane < HEAD_DIM, both[:span], both[span:])

    def keep_inner(n, value):
        att[tokens(lax.div(n, pairs), span), lanes(lax.rem(n, pairs))] = value

    for i in range(blocks):
        grouped(i * pairs, (i + 1) * pairs, inner, keep_inner)
        steps.tick()

    transpose(na, na_t)
    local.save(na_t, na_out)
    steps.tick()
    steps.finish(lambda name: name[0] == "c")
    chain.finish(early)
    local.save(early, e_out)
    loads = []
    for n in range(planes):
        zz = have(1, n)
        to = pl.ds(pl.multiple_of(zz * cols_two, 128), cols_two)
        loads += load_plane(local, fulls[1], pl.ds(0, D), zz, w_out.at[:, to], stage)
        loads += load_plane(local, fulls[1], pl.ds(D, PAD_ROWS), zz, gain.at[:, to], stage)
    for made in loads:
        made.wait()
    steps.tick()

    def outer(n):
        i, j = lax.div(n, pairs), lax.rem(n, pairs)
        at, block = tokens(i, span), lanes(j)
        a = att[at, block] + dot(q[at, block], unpack_state(early[n], own))
        unit = a * lax.rsqrt(head_sums(a * a, own) * (1.0 / HEAD_DIM) + 1e-5)
        normed = unit * gain[0:1, block].astype(F32)
        return a, (jax.nn.sigmoid(raw[at, block].astype(F32)) * normed).astype(BF16)

    def keep_outer(n, value):
        at, block = tokens(lax.div(n, pairs), span), lanes(lax.rem(n, pairs))
        att[at, block], gated[at, block] = value

    for i in range(blocks):
        grouped(i * pairs, (i + 1) * pairs, outer, keep_outer)
        steps.tick()
    local.save(att, att_out)

    for n in range(D // 512):
        at = pl.ds(n * 512, 512)
        mid[:, at] = x[:, at].astype(F32) + dot(gated[...], w_out[:, at])
        steps.tick()

    def norm_mid(r):
        m = mid[r, :]
        nb[r, :] = (m * lax.rsqrt(mean_square(m) + 1e-6)).astype(BF16)

    row_loop(rows, 64, norm_mid)
    local.save(mid, mid_out)
    steps.tick()

    def fetch_pair(j, slot):
        return [
            pltpu.make_async_copy(
                fulls[2].at[j + side * half], w_pair.at[slot, side], pair_sems.at[slot, side]
            )
            for side in range(2)
        ]

    early_half = planes == 4
    away = jnp.where(place.z < 2, 0, 2) if early_half else 0
    for n in range(planes - 1 if early_half else planes):
        have(2, n)
    for made in fetch_pair(away, 0):
        made.start()
    for n in range(half):
        j, slot = lax.rem(n + away, half), n % 2
        if early_half and n == 1:
            have(2, planes - 1)
        if n + 1 < half:
            for made in fetch_pair(lax.rem(n + 1 + away, half), 1 - slot):
                made.start()
        for made in fetch_pair(j, slot):
            made.wait()
        tmp_g[...] = dot(nb[...], w_pair[slot, 0])
        steps.tick()
        tmp_u[...] = dot(nb[...], w_pair[slot, 1])
        steps.tick()

        def finish_pair(r, j=j):
            gate, up = tmp_g[r, :], tmp_u[r, :]
            pair[j, r, :] = gate.astype(BF16)
            pair[j + half, r, :] = up.astype(BF16)
            hid[j, r, :] = (gate * up).astype(BF16)

        row_loop(rows, 64, finish_pair)
        local.save(pair.at[j], pair_out.at[j])
        local.save(pair.at[j + half], pair_out.at[j + half])
        steps.tick()

    transpose(gated, gated_t)
    local.save(gated_t, gated_out)
    transpose(nb, nb_t)
    local.save(nb_t, nb_out)
    steps.tick()
    for j in range(half):
        transpose(hid.at[j], hid_t.at[j])
        local.save(hid_t.at[j], hid_out.at[j])
    steps.tick()

    width = hid.shape[-1]

    def down(zz, slot):
        at = pl.ds(pl.multiple_of(zz * cols_two, 128), cols_two)
        total = mid[:, at]
        for j in range(half):
            total = total + dot(hid[j], w_down[slot, j * width : (j + 1) * width, :])
        res[:, at] = total.astype(BF16)

    before_it = None
    for n in range(planes):
        zz = have(3, n)
        loads = load_plane(local, fulls[3], pl.ds(0, FF), zz, w_down.at[n % 2], stage)
        if before_it is not None:
            down(*before_it)
            steps.tick()
        for made in loads:
            made.wait()
        before_it = (zz, n % 2)
    down(*before_it)
    local.save(res, out_hbm)
    steps.tick()
    steps.finish()
    local.finish()
    place.finish()


def forward(batch, seq, x, span, shards):
    rows = x.shape[0]
    cols_in, cols_pair = shards[0].shape[1], shards[2].shape[1]
    half = seq // 2
    states = (rows // span) * (D // 128)
    big = jax.ShapeDtypeStruct((rows, D), BF16)
    big_f = jax.ShapeDtypeStruct((rows, D), F32)
    narrow = shards[3].shape[1] % 128 != 0
    any_space = pl.BlockSpec(memory_space=pl.ANY)
    out_shape = [jax.ShapeDtypeStruct((seq, *a.shape), a.dtype) for a in shards]
    out_shape += [big, big, big, big, big, big_f]
    turned = jax.ShapeDtypeStruct((D, rows), BF16)
    out_shape += [jax.ShapeDtypeStruct((states, HEAD_DIM, 128), BF16), turned, big_f, turned]
    out_shape += [
        jax.ShapeDtypeStruct((seq, rows, cols_pair), BF16),
        jax.ShapeDtypeStruct((half, cols_pair, rows), BF16),
        turned,
    ]
    wide, wide_f = pltpu.VMEM((rows, D), BF16), pltpu.VMEM((rows, D), F32)
    pair_f = pltpu.VMEM((rows, cols_pair), F32)
    scratch = [
        wide, wide, pltpu.VMEM((rows, cols_in), F32), pltpu.VMEM((4, rows, D), BF16), wide_f, wide, wide_f, wide,
        pltpu.VMEM((2, D, cols_in), BF16),
        pltpu.VMEM((D, D), BF16),
        pltpu.VMEM((PAD_ROWS, D), BF16),
        pltpu.VMEM((2, 2, D, cols_pair), BF16),
        pair_f, pair_f,
        pltpu.VMEM((seq, rows, cols_pair), BF16),
        pltpu.VMEM((half, rows, cols_pair), BF16),
        pltpu.VMEM((2, FF, 2 * shards[3].shape[1]), BF16),
        wide,
        pltpu.VMEM((2, FF, shards[3].shape[1]) if narrow else (2, 16, 128), BF16),
        *[pltpu.VMEM((D, rows), BF16)] * 3,
        pltpu.VMEM((half, cols_pair, rows), BF16),
        *[pltpu.VMEM((states, HEAD_DIM, 128), BF16)] * 5,
        pltpu.SemaphoreType.DMA((6,)),
        pltpu.SemaphoreType.DMA((2,)),
        pltpu.SemaphoreType.DMA((2, 2)),
        pltpu.SemaphoreType.DMA((128,)),
        pltpu.SemaphoreType.DMA((Gather.KINDS, 4, half)),
        pltpu.SemaphoreType.DMA((2, 4)),
        *[pltpu.VMEM(a.shape, a.dtype) for a in shards],
    ]
    return pl.pallas_call(
        functools.partial(forward_kernel, batch, seq, span),
        out_shape=out_shape,
        in_specs=[any_space] * 5,
        out_specs=[any_space] * len(out_shape),
        scratch_shapes=scratch,
        compiler_params=pltpu.CompilerParams(
            collective_id=0, has_side_effects=True, vmem_limit_bytes=62 * 1024 * 1024
        ),
        name="forward",
    )(x, *shards)


WIDE = (False, True, False, True)
Z_PARTS = (2, 4, 1, 4)


def slope(plus):
    series = plus * (1.0 - plus * (0.5 - plus * (1.0 / 6.0)))
    return jnp.where(plus < 0.02, series, 1.0 - jnp.exp(-plus))


def backward_kernel(batch, seq, span, *refs):
    g_hbm, x_hbm, *fulls = refs[:6]
    (q_in, k_in, v_in, raw_in, att_in, e_in, gated_in, mid_in, nb_in, pair_in, hid_in, na_in) = refs[6:18]
    grad_hbm, sums, gm_hbm, far = refs[18], refs[19:23], refs[23], refs[24:28]
    refs = list(refs[28:])
    place = Place(batch, seq)
    reds = []
    for w in range(4):
        reds.append(Reduce(place, WIDE[w], Z_PARTS[w], sums[w], far[w], refs[:11]))
        refs = refs[11:]
    (tall, turned, pair, fields, f0, f1, g, split, low, down, slots, wide_out, slim_out, gain, gain_sums, gain_split,
     early, mine, other, before, chain_out, stage, chain_sems, slot_sems, local_sems) = refs
    red_down, red_pair, red_out, red_in = reds
    local = Locals(local_sems)
    rows = g.shape[0]
    half = seq // 2
    planes = half
    width = hid_in.shape[1]
    cols_in, cols_out, cols_pair = fulls[0].shape[2], fulls[1].shape[2], fulls[2].shape[2]
    per_group, per_block = seq // 4, cols_in // 128
    blocks, pairs = rows // span, D // 128
    first, second, own, own_f = pair_masks(span)
    core, sibling = place.c, 1 - place.c
    steps = Steps(BACKWARD_STEPS if place.square and place.planes == 4 else {})

    load_g = local.copy(g_hbm, g)
    load_hid = [local.copy(hid_in.at[j], tall.at[pl.ds(j * width, width)]) for j in range(half)]
    load_nb = local.copy(nb_in, turned)
    load_pair = [local.copy(pair_in.at[s], pair.at[s]) for s in range(seq)]
    load_mid = local.copy(mid_in, f1)
    load_e = local.copy(e_in, early)
    place.barrier()

    def split_columns(src):
        for s in range(seq):
            to = (s % 2) * (D // 2) + (s // 2) * cols_out
            split[:, to : to + cols_out] = src[:, s * cols_out : (s + 1) * cols_out]

    def by_core(which):
        return pl.ds(pl.multiple_of(which * (D // 2), D // 2), D // 2)

    slim_sent = []

    def slim_send(red, row, count, k, fill):
        slot = len(slim_sent) % 2
        if len(slim_sent) >= 2:
            for made in slim_sent[-2]:
                made().wait_send()
        fill(slot)
        sent = []
        for zz in range(planes):
            src = slim_out.at[slot, zz, pl.ds(0, count)]
            sent.append(functools.partial(red.core_copy, zz, src, row, count, k))
            sent[-1]().start()
        slim_sent.append(sent)

    def slim_theirs(red, lhs, at, row, count, k):
        def fill(slot):
            value = dot(lhs[at : at + count, :], split[:, by_core(sibling)])
            for zz in range(planes):
                slim_out[slot, zz, 0:count, :] = value[:, zz * cols_out : (zz + 1) * cols_out].astype(BF16)

        slim_send(red, row, count, k, fill)

    def slim_mine(red, lhs, at, row, count, k):
        value = dot(lhs[at : at + count, :], split[:, by_core(core)])
        for zz in range(planes):
            red.core_copy(zz, None, row, count, k).wait_recv()
            here = red.part[zz, row : row + count, :].astype(F32)
            here = here + value[:, zz * cols_out : (zz + 1) * cols_out]
            red.part[zz, row : row + count, :] = here.astype(BF16)

    wide_sent = []

    def wide_theirs(red, cols, zz):
        slot = len(wide_sent) % 2
        if len(wide_sent) >= 2:
            wide_sent[-2]().wait_send()
        s = 2 * zz + sibling

        def body(r):
            wide_out[slot, r, 0:cols] = dot(turned[r, :], pair[s, :, 0:cols]).astype(BF16)

        row_loop(D, 256, body)
        src = wide_out.at[slot] if cols == wide_out.shape[2] else wide_out.at[slot, :, pl.ds(0, cols)]
        wide_sent.append(functools.partial(red.core_copy, zz, src, 0, D, 0))
        wide_sent[-1]().start()
        steps.tick()

    def wide_mine(red, r, cols, zz):
        s = 2 * zz + core
        red.core_copy(zz, None, 0, D, 0).wait_recv()

        def body(at):
            here = red.part[zz, at, :].astype(F32) + dot(turned[at, :], pair[s, :, 0:cols])
            red.part[zz, at, :] = here.astype(BF16)

        row_loop(D, 256, body)
        if red.wide:
            red.plane_1(zz)
        red.plane_plan(steps, r, zz)
        red.z_plan(steps, r, zz)
        steps.tick()

    load_g.wait()
    split_columns(g)
    for made in load_hid:
        made.wait()
    for j in range(half):
        slim_theirs(red_down, tall, j * width, j * width, width, j)
    for j in range(half):
        slim_mine(red_down, tall, j * width, j * width, width, j)
    for zz in range(planes):
        red_down.z_plan(steps, 0, zz)
    red_down.late_plan(steps, 0)
    red_down.spread_plan(steps, 0)
    steps.tick()

    def load_down(j):
        at = pl.ds((j % 2) * width, width)
        return load_columns(local, fulls[3], pl.ds(j * width, width), down.at[at], stage)

    for made in load_pair:
        made.wait()
    waits = load_down(0)
    for j in range(half):
        after = load_down(j + 1) if j + 1 < half else []
        for made in waits:
            made.wait()
        waits = after
        at = (j % 2) * width
        f0[:, 0:width] = dot_nt(g[...], down[at : at + width, :])

        def finish_pair(r, j=j):
            grad = f0[r, 0:width]
            gate, up = pair[j, r, :].astype(F32), pair[j + half, r, :].astype(F32)
            pair[j, r, :] = (grad * up).astype(BF16)
            pair[j + half, r, :] = (grad * gate).astype(BF16)

        row_loop(rows, 64, finish_pair)
        steps.tick()

    load_nb.wait()
    wide_theirs(red_pair, cols_pair, 0)
    for zz in range(planes):
        if zz + 1 < planes:
            wide_theirs(red_pair, cols_pair, zz + 1)
        wide_mine(red_pair, 1, cols_pair, zz)
    red_pair.spread_plan(steps, 1)
    load_gated = local.copy(gated_in, turned)
    w_out = down.at[pl.ds(0, D)]
    load_out = load_columns(local, fulls[1], pl.ds(0, D), w_out, stage)
    load_out += load_columns(local, fulls[1], pl.ds(D, PAD_ROWS), gain, stage)
    views = []
    for k, src in enumerate((q_in, k_in, v_in, raw_in)):
        for side in range(2):
            to = tall.at[pl.ds((2 * k + side) * rows, rows)]
            views.append(local.copy(src.at[:, pl.ds(side * (D // 2), D // 2)], to))

    def back_pair(s, slot):
        value = dot_nt(pair[s], slots[slot])
        f0[...] = value if s == 0 else f0[...] + value

    stream(list(range(seq)), lambda s: fulls[2].at[s], slots, slot_sems, back_pair, steps.tick)
    load_mid.wait()

    def back_mid(r):
        m, grad = f1[r, :], f0[r, :]
        scale = lax.rsqrt(mean_square(m) + 1e-6)
        inner = jnp.mean(grad * m, axis=-1, keepdims=True)
        total = g[r, :].astype(F32) + scale * grad - m * (scale * scale * scale) * inner
        f1[r, :] = total
        low[r, :] = total.astype(BF16)

    row_loop(rows, 64, back_mid)
    save_gm = local.copy(f1, gm_hbm)
    split_columns(low)
    steps.tick()

    load_gated.wait()
    for k in range(2):
        slim_theirs(red_out, turned, k * (D // 2), k * (D // 2), D // 2, k)
    for made in load_out:
        made.wait()
    for n in range(D // 512):
        at = pl.ds(n * 512, 512)
        f0[:, at] = dot_nt(low[...], w_out[at, :])
    for k in range(2):
        slim_mine(red_out, turned, k * (D // 2), k * (D // 2), D // 2, k)
    load_na = local.copy(na_in, turned)
    load_x = local.copy(x_hbm, low)
    save_gm.wait()
    load_att = local.copy(att_in, f1)
    gain_sums[...] = jnp.zeros_like(gain_sums)
    for made in views:
        made.wait()
    load_e.wait()
    load_att.wait()
    steps.tick()

    def view(k, i, j):
        row = pl.multiple_of((2 * k + lax.div(j, pairs // 2)) * rows + i * span, span)
        return pl.ds(row, span), lanes(lax.rem(j, pairs // 2))

    def put(group, i, j, value):
        s = group * per_group + lax.div(j, per_block)
        pair[s, tokens(i, span), lanes(lax.rem(j, per_block))] = value

    def place_of(n):
        return lax.div(n, pairs), lax.rem(n, pairs)

    def back_gate(n):
        i, j = place_of(n)
        at, block = tokens(i, span), lanes(j)
        a, grad = f1[at, block], f0[at, block]
        scale = lax.rsqrt(head_sums(a * a, own) * (1.0 / HEAD_DIM) + 1e-5)
        unit = a * scale
        gains = gain[0:1, block].astype(F32)
        sig = jax.nn.sigmoid(tall[view(3, i, j)].astype(F32))
        grad_normed = grad * sig
        grad_gate = (grad * (unit * gains) * sig * (1.0 - sig)).astype(BF16)
        gain_sum = jnp.sum(grad_normed * unit, axis=0, keepdims=True)
        grad_unit = grad_normed * gains
        inner = head_sums(grad_unit * a, own) * (1.0 / HEAD_DIM)
        grad_a = (scale * grad_unit - a * (scale * scale * scale) * inner).astype(BF16)
        state = pack_state(dot_tn(tall[view(0, i, j)], grad_a)).astype(BF16)
        return grad_gate, gain_sum, grad_a, state

    def keep_gate(n, value):
        i, j = place_of(n)
        put(3, i, j, value[0])
        gain_sums[0:1, lanes(j)] += value[1]
        g[tokens(i, span), lanes(j)] = value[2]
        mine[n] = value[3]

    for i in range(blocks):
        grouped(i * pairs, (i + 1) * pairs, back_gate, keep_gate)
        if i == blocks - 1:
            chain = Chain(place, False, mine, other, before, chain_out, chain_sems)
            chain.start()
            chain.plan(steps)
        steps.tick()

    for s in range(seq):
        to = (s // 2) * cols_out
        gain_split[s % 2, :, to : to + cols_out] = gain_sums[:, s * cols_out : (s + 1) * cols_out]
    top = lax.broadcasted_iota(jnp.int32, (GAIN_ROWS, cols_out), 0) == 0

    def gain_rows(which, zz):
        row = gain_split[which, 0:1, zz * cols_out : (zz + 1) * cols_out]
        return jnp.where(top, row, 0.0)

    def fill_gain(slot):
        for zz in range(planes):
            slim_out[slot, zz, 0:GAIN_ROWS, :] = gain_rows(sibling, zz).astype(BF16)

    slim_send(red_out, D, GAIN_ROWS, 2, fill_gain)
    load_na.wait()
    ready = [zz for zz in range(planes) if zz * 2 >= 3 * per_group]
    for zz in ready:
        wide_theirs(red_in, cols_in, zz)
    for zz in range(planes):
        red_out.core_copy(zz, None, D, GAIN_ROWS, 2).wait_recv()
        here = red_out.part[zz, D : D + GAIN_ROWS, :].astype(F32) + gain_rows(core, zz)
        red_out.part[zz, D : D + GAIN_ROWS, :] = here.astype(BF16)
    for zz in range(planes):
        red_out.z_plan(steps, 2, zz)
    red_out.late_plan(steps, 2)
    red_out.spread_plan(steps, 2)
    steps.tick()
    for zz in ready:
        wide_mine(red_in, 3, cols_in, zz)

    t_of = lax.rem(lax.broadcasted_iota(jnp.int32, (span, 2 * span), 1), span)
    s_of = lax.broadcasted_iota(jnp.int32, (span, 2 * span), 0)
    t_down = lax.rem(lax.broadcasted_iota(jnp.int32, (2 * span, span), 0), span)
    s_down = lax.broadcasted_iota(jnp.int32, (2 * span, span), 1)
    lane = lax.broadcasted_iota(jnp.int32, (span, 128), 1)

    def back_attention(n):
        i, j = place_of(n)
        qs, ks, vs = (tall[view(k, i, j)] for k in range(3))
        grads = g[tokens(i, span), lanes(j)]
        q2, g2 = by_head(qs, first, second), by_head(grads, first, second)
        scores = jnp.where(t_of >= s_of, dot_nt(ks, q2), 0.0).astype(BF16)
        grad_t = jnp.where(t_of >= s_of, dot_nt(vs, g2), 0.0).astype(BF16)
        grad_s = jnp.where(t_down >= s_down, dot_nt(g2, vs), 0.0).astype(BF16)
        both = dot(grad_s, ks)
        grad_q = jnp.where(lane < HEAD_DIM, both[:span], both[span:])
        grad_q = grad_q + dot_nt(grads, unpack_state(early[n], own))
        return dot(grad_t, q2), dot(scores, g2), (grad_q * slope(qs.astype(F32))).astype(BF16)

    def keep_attention(n, value):
        i, j = place_of(n)
        at, block = tokens(i, span), lanes(j)
        f0[at, block], f1[at, block] = value[:2]
        put(0, i, j, value[2])

    for i in range(blocks):
        grouped(i * pairs, (i + 1) * pairs, back_attention, keep_attention, 2)
        steps.tick()
    ready_q = [zz for zz in range(planes) if (zz + 1) * 2 <= per_group]
    for zz in ready_q:
        wide_theirs(red_in, cols_in, zz)
    for zz in ready_q:
        wide_mine(red_in, 3, cols_in, zz)
    steps.finish(lambda name: name[0] == "c")
    chain.finish(other)

    def back_states(n):
        i, j = place_of(n)
        at, block = tokens(i, span), lanes(j)
        ks, vs = tall[view(1, i, j)], tall[view(2, i, j)]
        later = unpack_state(other[n], own)
        grad_k = (f0[at, block] + dot_nt(vs, later)) * slope(ks.astype(F32))
        return grad_k.astype(BF16), (f1[at, block] + dot(ks, later)).astype(BF16)

    def keep_states(n, value):
        put(1, *place_of(n), value[0])
        put(2, *place_of(n), value[1])

    for i in range(blocks):
        grouped(i * pairs, (i + 1) * pairs, back_states, keep_states)
        if i % 2:
            steps.tick()
    load_gm = local.copy(gm_hbm, f1)
    rest = [zz for zz in range(planes) if zz not in ready and zz not in ready_q]
    for n, zz in enumerate(rest):
        if n >= 2:
            wide_mine(red_in, 3, cols_in, rest[n - 2])
        wide_theirs(red_in, cols_in, zz)
    for zz in rest[-2:]:
        wide_mine(red_in, 3, cols_in, zz)
    red_in.spread_plan(steps, 3)

    w_in = slots if cols_in == slots.shape[2] else slots.at[:, :, pl.ds(0, cols_in)]

    def back_in(s, slot):
        value = dot_nt(pair[s, :, 0:cols_in], w_in[slot])
        f0[...] = value if s == 0 else f0[...] + value

    stream(list(range(seq)), lambda s: fulls[0].at[s], w_in, slot_sems, back_in, steps.tick)
    load_gm.wait()
    load_x.wait()

    def back_x(r):
        x, grad = low[r, :].astype(F32), f0[r, :]
        scale = lax.rsqrt(mean_square(x) + 1e-6)
        inner = jnp.mean(grad * x, axis=-1, keepdims=True)
        f1[r, :] += scale * grad - x * (scale * scale * scale) * inner

    row_loop(rows, 64, back_x)
    local.save(f1, grad_hbm)
    steps.tick()
    steps.finish()
    local.finish()
    for sent in slim_sent[-2:]:
        for made in sent:
            made().wait_send()
    for made in wide_sent[-2:]:
        made().wait_send()
    place.finish()


def backward(batch, seq, span, grad, x, fulls, saved):
    rows = x.shape[0]
    half = seq // 2
    cols_in, cols_out, cols_pair = fulls[0].shape[2], fulls[1].shape[2], fulls[2].shape[2]
    width = saved[10].shape[1]
    square = batch == 4
    shapes = ((FF, cols_out), (D, cols_pair), (D + GAIN_ROWS, cols_out), (D, cols_in))
    states = (rows // span) * (D // 128)
    any_space = pl.BlockSpec(memory_space=pl.ANY)
    big_f = jax.ShapeDtypeStruct((rows, D), F32)
    out_shape = [big_f] + [jax.ShapeDtypeStruct(shape, BF16) for shape in shapes] + [big_f]
    out_shape += [Reduce.far(square, WIDE[w], half, *shapes[w]) for w in range(4)]
    scratch = []
    core_parts = (half, 1, 3, 1)
    for w in range(4):
        scratch += Reduce.scratch(square, WIDE[w], half, *shapes[w], core_parts[w], Z_PARTS[w])
    narrow = cols_out % 128 != 0
    state = pltpu.VMEM((states, HEAD_DIM, 128), BF16)
    scratch += [
        pltpu.VMEM((max(FF, 8 * rows), D // 2), BF16),
        pltpu.VMEM((D, rows), BF16),
        pltpu.VMEM((seq, rows, cols_pair), BF16),
        pltpu.VMEM((16, 128), BF16),
        pltpu.VMEM((rows, D), F32),
        pltpu.VMEM((rows, D), F32),
        pltpu.VMEM((rows, D), BF16),
        pltpu.VMEM((rows, D), BF16),
        pltpu.VMEM((rows, D), BF16),
        pltpu.VMEM((max(2 * width, D), D), BF16),
        pltpu.VMEM((2, D, cols_pair), BF16),
        pltpu.VMEM((2, D, cols_pair), BF16),
        pltpu.VMEM((2, half, max(width, D // 2), cols_out), BF16),
        pltpu.VMEM((PAD_ROWS, D), BF16),
        pltpu.VMEM((8, D), F32),
        pltpu.VMEM((2, 8, D // 2), F32),
        state, state, state, state, state,
        pltpu.VMEM((D, cols_out) if narrow else (16, 128), BF16),
        pltpu.SemaphoreType.DMA((6,)),
        pltpu.SemaphoreType.DMA((2,)),
        pltpu.SemaphoreType.DMA((192,)),
    ]
    return pl.pallas_call(
        functools.partial(backward_kernel, batch, seq, span),
        out_shape=out_shape,
        in_specs=[any_space] * 18,
        out_specs=[any_space] * len(out_shape),
        scratch_shapes=scratch,
        compiler_params=pltpu.CompilerParams(
            collective_id=1, has_side_effects=True, vmem_limit_bytes=63 * 1024 * 1024
        ),
        name="backward",
    )(grad, x, *fulls, *saved)


def local(block_in, attn_in, attn_out, out_gain, glu_in, glu_out, block_grad):
    seq_count, span = block_in.shape[:2]
    rows = seq_count * span
    batch, seq = lax.axis_size("batch"), lax.axis_size("seq")
    x = block_in.reshape(rows, D)
    with_gain = jnp.concatenate([attn_out, jnp.broadcast_to(out_gain, (PAD_ROWS, out_gain.shape[0]))])
    parts = forward(batch, seq, x, span, (attn_in, with_gain, glu_in, glu_out))
    fulls, block_out, saved = parts[:4], parts[4], parts[5:]
    grads = backward(batch, seq, span, block_grad.reshape(rows, D), x, fulls, saved)
    input_grad, sums = grads[0], list(grads[1:5])
    if batch != 4:
        sums = [lax.psum(a, "batch") for a in sums]
    down, pair, out, into = (a.astype(F32) for a in sums)
    return (
        block_out.reshape(block_in.shape),
        input_grad.reshape(block_in.shape),
        into,
        out[:D],
        out[D],
        pair,
        down,
    )


def solution(mesh):
    rows, columns = P("batch", "seq", None), P(None, "seq")
    return jax.shard_map(
        local,
        mesh=mesh,
        in_specs=(rows, columns, columns, P("seq"), columns, columns, rows),
        out_specs=(rows, rows, columns, columns, P("seq"), columns, columns),
        check_vma=False,
    )
```

```python
import functools

import jax
import jax.numpy as jnp
from jax import lax
from jax.experimental import pallas as pl
from jax.experimental.pallas import tpu as pltpu
from jax.sharding import PartitionSpec as P

HEADS = 16
HEAD_DIM = 64
D = 1024
FF = 2816
MESH = pl.DeviceIdType.MESH
BF16 = jnp.bfloat16
F32 = jnp.float32
GAIN_ROWS = 128


def run_if(cond, fn):
    if cond is None:
        fn()
    else:
        pl.when(cond)(fn)


class Place:
    def __init__(self, batch, seq):
        self.planes = seq // 2
        self.square = batch == 4
        self.b = lax.axis_index("batch")
        self.s = lax.axis_index("seq")
        self.z = lax.div(self.s, 2)
        self.c = lax.rem(self.s, 2)
        self.bx = self.b + 1 - 2 * lax.rem(self.b, 2)
        self.by = lax.rem(self.b + 2, 4)
        self.bd = lax.rem(self.bx + 2, 4)
        self.sib = (self.b, self.s + 1 - 2 * self.c)
        self.up = (self.b, self.s + 2)
        self.down = (self.b, self.s - 2)
        self.x = (self.bx, self.s)
        self.y = (self.by, self.s)
        self.has_up = self.z < self.planes - 1
        self.has_down = self.z > 0
        self.sent = []

    def barrier(self):
        sem = pltpu.get_barrier_semaphore()
        always = [self.sib] + ([self.x, self.y] if self.square else [])
        for device in always:
            pl.semaphore_signal(sem, inc=1, device_id=device, device_id_type=MESH)
        for cond, device in ((self.has_up, self.up), (self.has_down, self.down)):
            pl.when(cond)(
                lambda device=device: pl.semaphore_signal(
                    sem, inc=1, device_id=device, device_id_type=MESH
                )
            )
        ends = self.has_up.astype(jnp.int32) + self.has_down.astype(jnp.int32)
        pl.semaphore_wait(sem, len(always) + ends)

    def copy(self, src, dst, send_sem, recv_sem, device):
        return pltpu.make_async_remote_copy(
            src_ref=src,
            dst_ref=dst,
            send_sem=send_sem,
            recv_sem=recv_sem,
            device_id=device,
            device_id_type=MESH,
        )

    def send(self, make, cond=None):
        run_if(cond, lambda: make().start())
        self.sent.append((cond, make))

    def finish(self):
        for cond, make in self.sent:
            run_if(cond, lambda make=make: make().wait_send())
        self.sent = []


class Gather:
    Z_UP, Z_DOWN, Z_IN, X_OUT, X_IN, Y_OUT, Y_IN, FX_OUT, FX_IN, FY_OUT, FY_IN = range(11)
    S_OUT, S_IN = 11, 15
    KINDS = 19

    def __init__(self, place, held, fulls, quartered, sems, local_sems):
        self.p, self.held, self.fulls, self.sems = place, held, fulls, sems
        self.local_sems = local_sems
        self.quartered = [q and place.square for q in quartered]

    def rows(self, w, owner, half=None):
        rows = self.held[w].shape[0]
        if not self.quartered[w]:
            return pl.ds(0, rows)
        part = rows // 4
        if half is None:
            return pl.ds(pl.multiple_of(owner * part, 16), part)
        return pl.ds(pl.multiple_of(owner * part + half * (part // 2), 16), part // 2)

    def move(self, w, zz, rows, out, into, device, core=None):
        core = self.p.c if core is None else core
        block = self.fulls[w].at[2 * zz + core, rows]
        return self.p.copy(
            block, block, self.sems.at[out, w, zz], self.sems.at[into, w, zz], device
        )

    def across(self, w, zz, piece, core=None):
        p = self.p
        rows = self.rows(w, (p.b, p.bx, p.by, p.bd)[piece])
        return self.move(w, zz, rows, self.S_OUT + piece, self.S_IN + piece, p.sib, core)

    def whole(self, w):
        p = self.p
        here = self.fulls[w].at[p.s]
        return p.copy(
            self.held[w], here, self.sems.at[self.S_OUT, w, p.z], self.sems.at[self.S_IN, w, p.z], p.sib
        )

    def start(self, w):
        p, own = self.p, self.held[w]
        here = self.fulls[w].at[p.s]
        rows = self.rows(w, p.b)
        for cond, device, out in (
            (p.has_up, p.up, self.Z_UP),
            (p.has_down, p.down, self.Z_DOWN),
        ):
            p.send(
                lambda device=device, out=out: p.copy(
                    own.at[rows],
                    here.at[rows],
                    self.sems.at[out, w, p.z],
                    self.sems.at[self.Z_IN, w, p.z],
                    device,
                ),
                cond,
            )
        p.send(lambda: self.whole(w))
        pltpu.make_async_copy(own, here, self.local_sems.at[w]).start()

    def sides(self, d):
        p = self.p
        return (
            (p.z >= d, p.z - d, p.has_up, p.up, self.Z_UP),
            (p.z + d < p.planes, p.z + d, p.has_down, p.down, self.Z_DOWN),
        )

    def from_z(self, w, d):
        p = self.p
        rows = self.rows(w, p.b)
        for cond, zz, more, device, out in self.sides(d):
            run_if(
                cond, lambda zz=zz: self.move(w, zz, rows, self.Z_UP, self.Z_IN, p.up).wait_recv()
            )
            p.send(
                lambda zz=zz, device=device, out=out: self.move(
                    w, zz, rows, out, self.Z_IN, device
                ),
                jnp.logical_and(cond, more),
            )
            p.send(lambda zz=zz: self.across(w, zz, 0), cond)

    def to_plane(self, w, d):
        p = self.p
        rows = self.rows(w, p.b)
        for cond, zz, *_ in self.sides(d):
            p.send(lambda zz=zz: self.move(w, zz, rows, self.X_OUT, self.X_IN, p.x), cond)
            p.send(lambda zz=zz: self.move(w, zz, rows, self.Y_OUT, self.Y_IN, p.y), cond)

    def from_plane(self, w, d):
        p = self.p
        from_x, from_y = self.rows(w, p.bx), self.rows(w, p.by)
        half_x, half_y = self.rows(w, p.bx, 0), self.rows(w, p.by, 1)
        for cond, zz, *_ in self.sides(d):
            run_if(
                cond, lambda zz=zz: self.move(w, zz, from_x, self.X_OUT, self.X_IN, p.x).wait_recv()
            )
            p.send(lambda zz=zz: self.move(w, zz, half_x, self.FY_OUT, self.FY_IN, p.y), cond)
            run_if(
                cond, lambda zz=zz: self.move(w, zz, from_y, self.Y_OUT, self.Y_IN, p.y).wait_recv()
            )
            p.send(lambda zz=zz: self.move(w, zz, half_y, self.FX_OUT, self.FX_IN, p.x), cond)
            p.send(lambda zz=zz: self.across(w, zz, 1), cond)
            p.send(lambda zz=zz: self.across(w, zz, 2), cond)

    def from_diagonal(self, w, d):
        p = self.p
        half_0, half_1 = self.rows(w, p.bd, 0), self.rows(w, p.bd, 1)
        for cond, zz, *_ in self.sides(d):
            run_if(
                cond,
                lambda zz=zz: self.move(w, zz, half_0, self.FY_OUT, self.FY_IN, p.y).wait_recv(),
            )
            run_if(
                cond,
                lambda zz=zz: self.move(w, zz, half_1, self.FX_OUT, self.FX_IN, p.x).wait_recv(),
            )
            p.send(lambda zz=zz: self.across(w, zz, 3), cond)

    def nearest(self, k):
        planes = self.p.planes
        found = jnp.int32(0)
        for z in range(planes):
            order = sorted(range(planes), key=lambda t: (abs(t - z), t))
            found = jnp.where(self.p.z == z, order[k], found)
        return found

    def have(self, w, k):
        p = self.p
        if k == 0:
            pltpu.make_async_copy(
                self.held[w], self.fulls[w].at[p.s], self.local_sems.at[w]
            ).wait()
            self.whole(w).wait_recv()
            return p.z
        zz = self.nearest(k)
        for piece in range(4 if self.quartered[w] else 1):
            self.across(w, zz, piece, 1 - p.c).wait_recv()
        return zz


class Steps:
    def __init__(self, table):
        self.table, self.todo, self.ticks = table, {}, 0

    def add(self, name, fn, *args):
        self.todo[name] = functools.partial(fn, *args)

    def run(self, name):
        step = self.todo.pop(name, None)
        if step is not None:
            step()

    def tick(self):
        for name in self.table.get(self.ticks, ()):
            self.run(name)
        self.ticks += 1

    def finish(self, wanted=lambda name: True):
        for name in [name for name in self.todo if wanted(name)]:
            self.run(name)


def plan_gather(steps, g, count):
    far = g.p.planes - 1
    for w in range(count):
        steps.add(("start", w), g.start, w)
        for d in range(1, far + 1):
            steps.add(("z", w, d), g.from_z, w, d)
        if g.quartered[w]:
            for name, step in (("x", g.to_plane), ("p", g.from_plane), ("g", g.from_diagonal)):
                for d in range(1, far + 1):
                    steps.add((name, w, d), step, w, d)


def add_into(dst, src, row, rows):
    cols = dst.shape[-1]
    chunk = max(
        k for k in range(16, rows + 1, 16) if rows % k == 0 and (k * cols <= 49152 or k == 16)
    )

    def body(i, _):
        here = pl.ds(pl.multiple_of(row + i * chunk, 16), chunk)
        there = pl.ds(pl.multiple_of(i * chunk, 16), chunk)
        dst[here, :] = (dst[here, :].astype(F32) + src[there, :].astype(F32)).astype(BF16)
        return 0

    lax.fori_loop(0, rows // chunk, body, 0)


class Reduce:
    (X1_OUT, X1_IN, Y1_OUT, Y1_IN, X2_OUT, X2_IN, Y2_OUT, Y2_IN, X3_OUT, X3_IN, Y3_OUT, Y3_IN) = range(12)
    KINDS = 12
    S_OUT, S_IN = range(2)
    Z_UP, Z_UP_IN, Z_DOWN, Z_DOWN_IN, FETCH = range(5)
    GX_OUT, GX_IN, GY_OUT, GY_IN, FX_OUT, FX_IN, FY_OUT, FY_IN, LOCAL = range(9)
    LAST_KINDS = 9

    def __init__(self, place, wide, z_parts, out, zin_far, refs):
        self.p, self.wide, self.out = place, wide and place.square, out
        self.part, self.x1, self.y1, self.x2, self.y2, zin, self.stage = refs[:7]
        self.core_sems, self.sems, self.z_sems, self.last_sems = refs[7:]
        self.zin = zin if self.wide else zin_far
        self.total = self.part.shape[1]
        self.quarter, self.half = self.total // 4, self.total // 8
        self.z_parts = 1 if self.wide else z_parts

    @staticmethod
    def scratch(square, wide, planes, rows, cols, core_parts, z_parts):
        wide = wide and square
        pieces = planes if wide else 1
        small = (pieces, rows // 8, cols) if square else (1, 16, 128)
        large = (pieces, rows // 4, cols) if square else (1, 16, 128)
        return [
            pltpu.VMEM((planes, rows, cols), BF16),
            pltpu.VMEM(small, BF16),
            pltpu.VMEM(small, BF16),
            pltpu.VMEM(large, BF16),
            pltpu.VMEM(large, BF16),
            pltpu.VMEM((planes + 1, rows // 4, cols) if wide else (1, 16, 128), BF16),
            pltpu.VMEM((16, 128) if wide else (rows // z_parts, cols), BF16),
            pltpu.SemaphoreType.DMA((2, planes, core_parts)),
            pltpu.SemaphoreType.DMA((Reduce.KINDS, pieces)),
            pltpu.SemaphoreType.DMA((5, planes + 1, z_parts)),
            pltpu.SemaphoreType.DMA((Reduce.LAST_KINDS,)),
        ]

    @staticmethod
    def far(square, wide, planes, rows, cols):
        shape = (1, 16, 128) if wide and square else (planes + 1, rows, cols)
        return jax.ShapeDtypeStruct(shape, BF16)

    def at(self, owner, half=None):
        if half is None:
            return pl.ds(pl.multiple_of(owner * self.quarter, 16), self.quarter)
        return pl.ds(pl.multiple_of(owner * self.quarter + half * self.half, 16), self.half)

    def sem(self, kind, k):
        return self.sems.at[kind, k]

    def core_copy(self, zz, src, row, rows, k):
        block = self.part.at[zz, pl.ds(row, rows)]
        return self.p.copy(
            block if src is None else src,
            block,
            self.core_sems.at[self.S_OUT, zz, k],
            self.core_sems.at[self.S_IN, zz, k],
            self.p.sib,
        )

    def slot(self, zz):
        return zz if self.wide else 0

    def hop(self, zz, rows, dst, out, into, device):
        return self.p.copy(
            self.part.at[zz, rows],
            dst,
            self.sem(out, self.slot(zz)),
            self.sem(into, self.slot(zz)),
            device,
        )

    def plane_1(self, zz):
        p, k, h = self.p, self.slot(zz), self.half
        lo, hi = pl.ds(0, h), pl.ds(h, h)
        p.send(lambda: self.hop(zz, self.at(p.bd, 0), self.x1.at[k], self.X1_OUT, self.X1_IN, p.x))
        p.send(lambda: self.hop(zz, self.at(p.bd, 1), self.y1.at[k], self.Y1_OUT, self.Y1_IN, p.y))
        p.send(lambda: self.hop(zz, self.at(p.bx, 0), self.x2.at[k, lo], self.X2_OUT, self.X2_IN, p.x))
        p.send(lambda: self.hop(zz, self.at(p.by, 1), self.y2.at[k, hi], self.Y2_OUT, self.Y2_IN, p.y))

    def plane_2(self, zz):
        p, k, h = self.p, self.slot(zz), self.half
        lo, hi = pl.ds(0, h), pl.ds(h, h)
        self.hop(zz, self.at(p.bd, 0), self.x1.at[k], self.X1_OUT, self.X1_IN, p.x).wait_recv()
        add_into(self.part.at[zz], self.x1.at[k], p.by * self.quarter, h)
        p.send(lambda: self.hop(zz, self.at(p.by, 0), self.y2.at[k, lo], self.Y3_OUT, self.Y3_IN, p.y))
        self.hop(zz, self.at(p.bd, 1), self.y1.at[k], self.Y1_OUT, self.Y1_IN, p.y).wait_recv()
        add_into(self.part.at[zz], self.y1.at[k], p.bx * self.quarter + h, h)
        p.send(lambda: self.hop(zz, self.at(p.bx, 1), self.x2.at[k, hi], self.X3_OUT, self.X3_IN, p.x))

    def plane_3(self, zz):
        p, k, h = self.p, self.slot(zz), self.half
        lo, hi = pl.ds(0, h), pl.ds(h, h)
        self.hop(zz, self.at(p.bx, 0), self.x2.at[k, lo], self.X2_OUT, self.X2_IN, p.x).wait_recv()
        self.hop(zz, self.at(p.by, 1), self.y2.at[k, hi], self.Y2_OUT, self.Y2_IN, p.y).wait_recv()
        self.hop(zz, self.at(p.bx, 1), self.x2.at[k, hi], self.X3_OUT, self.X3_IN, p.x).wait_recv()
        add_into(self.part.at[zz], self.x2.at[k], p.b * self.quarter, self.quarter)
        self.hop(zz, self.at(p.by, 0), self.y2.at[k, lo], self.Y3_OUT, self.Y3_IN, p.y).wait_recv()
        add_into(self.part.at[zz], self.y2.at[k], p.b * self.quarter, self.quarter)

    def z_rows(self, k):
        p = self.p
        rows = self.total // self.z_parts
        return (p.b * self.quarter, self.quarter) if self.wide else (k * rows, rows)

    def z_slot(self, zz, upward, k):
        slot = zz + 1 if upward else zz
        if self.wide:
            return self.zin.at[slot]
        row, rows = self.z_rows(k)
        return self.zin.at[slot, pl.ds(row, rows)]

    def z_hop(self, zz, upward, k):
        p = self.p
        row, rows = self.z_rows(k)
        here = pl.ds(pl.multiple_of(row, 16), rows)
        out, into = (self.Z_UP, self.Z_UP_IN) if upward else (self.Z_DOWN, self.Z_DOWN_IN)
        return p.copy(
            self.part.at[zz, here],
            self.z_slot(zz, upward, k),
            self.z_sems.at[out, zz, k],
            self.z_sems.at[into, zz, k],
            p.up if upward else p.down,
        )

    def z_take(self, zz, upward, k):
        self.z_hop(zz, upward, k).wait_recv()
        row, rows = self.z_rows(k)
        src = self.z_slot(zz, upward, k)
        if not self.wide:
            slot = zz + 1 if upward else zz
            fetch = pltpu.make_async_copy(src, self.stage, self.z_sems.at[self.FETCH, slot, k])
            fetch.start()
            fetch.wait()
            src = self.stage
        add_into(self.part.at[zz], src, row, rows)

    def z_step(self, zz, d, k):
        p = self.p
        for upward, at in ((True, zz - d), (False, zz + d)):
            if not 0 <= at < p.planes:
                continue

            @pl.when(p.z == at)
            def _(upward=upward, at=at):
                if at != (0 if upward else p.planes - 1):
                    self.z_take(zz, upward, k)
                self.z_hop(zz, upward, k).start()

            p.sent.append((p.z == at, functools.partial(self.z_hop, zz, upward, k)))

    def z_last(self, zz, k):
        @pl.when(self.p.z == zz)
        def _():
            if zz > 0:
                self.z_take(zz, True, k)
            if zz < self.p.planes - 1:
                self.z_take(zz, False, k)

    def z_plan(self, steps, r, zz):
        for k in range(self.z_parts):
            for d in range(max(zz, self.p.planes - 1 - zz), 0, -1):
                steps.add(("z", r, zz, d, k), self.z_step, zz, d, k)
            steps.add(("zl", r, zz, k), self.z_last, zz, k)

    def plane_plan(self, steps, r, zz):
        if self.p.square:
            steps.add(("p2", r, zz), self.plane_2, zz)
            steps.add(("p3", r, zz), self.plane_3, zz)

    def late_plan(self, steps, r):
        if self.p.square:
            for n, step in enumerate((self.plane_1, self.plane_2, self.plane_3)):
                steps.add(("p%d" % (n + 1), r, -1), step, self.p.z)

    def spread_plan(self, steps, r):
        for n, step in enumerate((self.spread_1, self.spread_2, self.spread_3)):
            steps.add(("s%d" % (n + 1), r), step)

    def last_hop(self, src, rows, out, into, device):
        return self.p.copy(
            src, self.out.at[rows], self.last_sems.at[out], self.last_sems.at[into], device
        )

    def spread_1(self):
        p = self.p
        if not p.square:
            pltpu.make_async_copy(self.part.at[p.z], self.out, self.last_sems.at[self.LOCAL]).start()
            return
        rows = self.at(p.b)
        src = self.part.at[p.z, rows]
        p.send(lambda: self.last_hop(src, rows, self.GX_OUT, self.GX_IN, p.x))
        p.send(lambda: self.last_hop(src, rows, self.GY_OUT, self.GY_IN, p.y))
        pltpu.make_async_copy(src, self.out.at[rows], self.last_sems.at[self.LOCAL]).start()

    def spread_2(self):
        p = self.p
        if not p.square:
            return
        from_x, from_y = self.at(p.bx), self.at(p.by)
        half_x, half_y = self.at(p.bx, 0), self.at(p.by, 1)
        self.last_hop(self.out.at[from_x], from_x, self.GX_OUT, self.GX_IN, p.x).wait_recv()
        p.send(lambda: self.last_hop(self.out.at[half_x], half_x, self.FY_OUT, self.FY_IN, p.y))
        self.last_hop(self.out.at[from_y], from_y, self.GY_OUT, self.GY_IN, p.y).wait_recv()
        p.send(lambda: self.last_hop(self.out.at[half_y], half_y, self.FX_OUT, self.FX_IN, p.x))

    def spread_3(self):
        p = self.p
        if not p.square:
            pltpu.make_async_copy(self.part.at[p.z], self.out, self.last_sems.at[self.LOCAL]).wait()
            return
        rows = self.at(p.b)
        half_0, half_1 = self.at(p.bd, 0), self.at(p.bd, 1)
        self.last_hop(self.out.at[half_0], half_0, self.FY_OUT, self.FY_IN, p.y).wait_recv()
        self.last_hop(self.out.at[half_1], half_1, self.FX_OUT, self.FX_IN, p.x).wait_recv()
        pltpu.make_async_copy(
            self.part.at[p.z, rows], self.out.at[rows], self.last_sems.at[self.LOCAL]
        ).wait()


FORWARD_STEPS = {
    0: (('z', 0, 1), ('x', 0, 1),),
    1: (('start', 1), ('z', 0, 2), ('x', 0, 2), ('z', 1, 1), ('start', 2),),
    3: (('p', 0, 1), ('z', 0, 3), ('x', 0, 3), ('p', 0, 2), ('x', 1, 1), ('start', 3), ('g', 0, 1), ('z', 1, 2), ('x', 1, 2),),
    4: (('p', 0, 3), ('z', 2, 1), ('x', 2, 1),),
    5: (('g', 0, 2), ('z', 3, 1),),
    6: (('z', 1, 3),),
    7: (('g', 0, 3), ('p', 1, 2), ('x', 1, 3),),
    10: (('z', 2, 2), ('p', 1, 1), ('x', 2, 2), ('c', 0, 0), ('c', 0, 1),),
    12: (('p', 1, 3), ('c', 1, 0),),
    13: (('c', 1, 1),),
    14: (('c', 0, 2), ('g', 1, 2), ('g', 1, 1), ('p', 2, 1),),
    15: (('g', 1, 3), ('z', 2, 3), ('c', 1, 2), ('x', 2, 3),),
    16: (('c', 0, 3), ('z', 3, 2), ('p', 2, 2),),
    17: (('c', 1, 3),),
    21: (('g', 2, 1),),
    22: (('p', 2, 3),),
    23: (('x', 3, 1),),
    24: (('g', 2, 2), ('z', 3, 3), ('x', 3, 3),),
    25: (('g', 2, 3), ('x', 3, 2),),
    28: (('p', 3, 1),),
    29: (('p', 3, 3),),
    30: (('p', 3, 2),),
    31: (('g', 3, 1),),
    32: (('g', 3, 3),),
    33: (('g', 3, 2),),
}
BACKWARD_STEPS = {
    0: (('z', 0, 3, 3, 0), ('z', 0, 0, 3, 0),),
    7: (('z', 0, 1, 2, 0),),
    8: (('z', 0, 2, 2, 0),),
    10: (('z', 0, 0, 2, 0), ('z', 0, 3, 2, 0),),
    11: (('p2', 1, 0),),
    16: (('z', 0, 2, 1, 0), ('z', 0, 1, 1, 0),),
    17: (('z', 0, 3, 1, 0), ('z', 0, 0, 1, 0),),
    18: (('p2', 1, 1),),
    21: (('c', 0, 0), ('p2', 1, 3),),
    23: (('p2', 1, 2), ('p3', 1, 0), ('c', 1, 0), ('zl', 0, 1, 0),),
    24: (('zl', 0, 2, 0), ('z', 2, 3, 3, 0),),
    25: (('c', 0, 1), ('z', 2, 1, 2, 0), ('c', 1, 1),),
    26: (('z', 2, 2, 2, 0), ('zl', 0, 0, 0), ('zl', 0, 3, 0),),
    27: (('c', 0, 2), ('z', 1, 0, 3, 0), ('p1', 0, -1),),
    28: (('c', 1, 2),),
    29: (('p2', 3, 3),),
    30: (('z', 2, 0, 3, 0), ('p3', 1, 3), ('z', 1, 3, 3, 0), ('p2', 0, -1), ('z', 2, 2, 1, 0), ('c', 0, 3), ('c', 1, 3),),
    32: (('z', 1, 0, 2, 0),),
    33: (('z', 1, 3, 2, 0),),
    34: (('p3', 1, 2), ('z', 1, 2, 2, 0), ('p2', 3, 0),),
    35: (('p3', 1, 1), ('z', 1, 1, 2, 0),),
    36: (('z', 2, 0, 2, 0), ('zl', 2, 2, 0), ('p3', 3, 3), ('z', 3, 3, 3, 0),),
    37: (('z', 1, 3, 1, 0), ('z', 2, 3, 2, 0), ('z', 1, 1, 1, 0), ('z', 2, 1, 1, 0), ('z', 1, 2, 1, 0), ('p2', 3, 1), ('z', 1, 0, 1, 0), ('p3', 0, -1), ('z', 2, 0, 1, 0), ('p2', 3, 2),),
    38: (('p3', 3, 0), ('s1', 0), ('z', 3, 0, 3, 0),),
    39: (('zl', 1, 0, 0), ('p3', 3, 1), ('z', 3, 1, 2, 0), ('zl', 1, 1, 0), ('z', 2, 3, 1, 0), ('p3', 3, 2), ('z', 3, 3, 2, 0), ('zl', 1, 3, 0), ('zl', 1, 2, 0), ('s1', 1), ('z', 3, 2, 2, 0), ('z', 3, 0, 2, 0),),
    40: (('zl', 2, 1, 0), ('s2', 0), ('zl', 2, 3, 0),),
    41: (('z', 3, 1, 1, 0), ('zl', 2, 0, 0), ('z', 3, 2, 1, 0), ('z', 3, 3, 1, 0), ('z', 3, 0, 1, 0), ('p1', 2, -1), ('s2', 1),),
    42: (('p2', 2, -1), ('zl', 3, 1, 0), ('zl', 3, 3, 0),),
    43: (('zl', 3, 2, 0), ('zl', 3, 0, 0), ('s1', 3), ('p3', 2, -1), ('s1', 2), ('s3', 0), ('s2', 3), ('s2', 2), ('s3', 1), ('s3', 3), ('s3', 2),),
}


def dot(a, b):
    return jnp.dot(a, b, preferred_element_type=F32)


def dot_nt(a, b):
    return lax.dot_general(a, b, (((1,), (1,)), ((), ())), preferred_element_type=F32)


def dot_tn(a, b):
    return lax.dot_general(a, b, (((0,), (0,)), ((), ())), preferred_element_type=F32)


def row_loop(rows, chunk, body):
    def step(i, _):
        body(pl.ds(pl.multiple_of(i * chunk, chunk), chunk))
        return 0

    lax.fori_loop(0, rows // chunk, step, 0)


def lanes(block, width=128):
    return pl.ds(pl.multiple_of(block * width, width), width)


def tokens(i, span):
    return pl.ds(pl.multiple_of(i * span, span), span)


def transpose(src, dst):
    rows, cols = src.shape
    whole = cols // 128

    def step(j, _):
        at = lanes(j)
        dst[at, :] = src[:, at].T
        return 0

    lax.fori_loop(0, whole, step, 0)
    if cols % 128:
        dst[whole * 128 :, :] = src[:, whole * 128 :].T


def mean_square(v):
    return jnp.mean(v * v, axis=-1, keepdims=True)


def pair_masks(span):
    lane = lax.broadcasted_iota(jnp.int32, (span, 128), 1)
    first = (lane < HEAD_DIM).astype(F32)
    row = lax.broadcasted_iota(jnp.int32, (128, 128), 0)
    col = lax.broadcasted_iota(jnp.int32, (128, 128), 1)
    own = ((row < HEAD_DIM) == (col < HEAD_DIM)).astype(F32)
    return first.astype(BF16), (1.0 - first).astype(BF16), own.astype(BF16), own


def by_head(pair, first, second):
    return jnp.concatenate([pair * first, pair * second], axis=0)


def pack_state(state):
    lane = lax.broadcasted_iota(jnp.int32, (HEAD_DIM, 128), 1)
    return jnp.where(lane < HEAD_DIM, state[:HEAD_DIM], state[HEAD_DIM:])


def unpack_state(packed, own):
    return jnp.concatenate([packed, packed], axis=0) * own


def head_sums(v, own):
    return dot(v.astype(BF16), own)


def grouped(lo, hi, compute, store, size=4):
    def step(m, _):
        first = lo + m * size
        results = [compute(first + u) for u in range(size)]
        for u in range(size):
            store(first + u, results[u])
        return 0

    lax.fori_loop(0, (hi - lo) // size, step, 0)


class Chain:
    S_OUT, S_IN, Z_OUT, Z_IN, P_OUT, P_IN = range(6)
    PARTS = 2

    def __init__(self, place, forward, mine, other, before, out, sems):
        self.p, self.forward = place, forward
        self.mine, self.other, self.before, self.out, self.sems = mine, other, before, out, sems
        self.count = mine.shape[0] // self.PARTS
        self.half = self.count // 2
        if forward:
            self.prev, self.next = place.has_down, place.has_up
            self.device, self.counts = place.up, place.c == 1
        else:
            self.prev, self.next = place.has_up, place.has_down
            self.device, self.counts = place.down, place.c == 0

    @staticmethod
    def scratch(count):
        return [pltpu.VMEM((count, HEAD_DIM, 128), BF16)] * 4 + [pltpu.SemaphoreType.DMA((6, Chain.PARTS))]

    def part(self, k, core):
        return pl.ds(k * self.count + core * self.half, self.half)

    def sibling_copy(self, k):
        here = pl.ds(k * self.count, self.count)
        return self.p.copy(
            self.mine.at[here], self.other.at[here], self.sems.at[self.S_OUT, k],
            self.sems.at[self.S_IN, k], self.p.sib,
        )

    def next_copy(self, k):
        here = self.part(k, self.p.c)
        return self.p.copy(
            self.out.at[here], self.before.at[here], self.sems.at[self.Z_OUT, k],
            self.sems.at[self.Z_IN, k], self.device,
        )

    def across_copy(self, k, core):
        here = self.part(k, core)
        return self.p.copy(
            self.before.at[here], self.before.at[here], self.sems.at[self.P_OUT, k],
            self.sems.at[self.P_IN, k], self.p.sib,
        )

    def start(self, k, steps):
        self.p.send(lambda: self.sibling_copy(k))

        @pl.when(jnp.logical_not(self.prev))
        def _():
            def body(n, _):
                self.before[k * self.count + n] = jnp.zeros(self.before.shape[1:], BF16)
                return 0

            lax.fori_loop(0, self.count, body, 0)

        for h in range(self.p.planes):
            steps.add(("c", k, h), self.step, k, h)

    def step(self, k, h):
        p = self.p
        here = p.z == (h if self.forward else p.planes - 1 - h)

        @pl.when(here)
        def _():
            self.sibling_copy(k).wait_recv()
            if h > 0:
                self.next_copy(k).wait_recv()
                self.across_copy(k, p.c).start()
            if h < p.planes - 1:

                def body(i, _):
                    n = k * self.count + p.c * self.half + i
                    total = self.before[n].astype(F32) + self.mine[n].astype(F32)
                    self.out[n] = (total + self.other[n].astype(F32)).astype(BF16)
                    return 0

                lax.fori_loop(0, self.half, body, 0)
                self.next_copy(k).start()

        if h > 0:
            p.sent.append((here, lambda: self.across_copy(k, p.c)))
        if h < p.planes - 1:
            p.sent.append((here, lambda: self.next_copy(k)))

    def finish(self, k, steps, result):
        p = self.p
        steps.finish(lambda name: name[:2] == ("c", k))
        pl.when(self.prev)(lambda: self.across_copy(k, 1 - p.c).wait_recv())
        weight = self.counts.astype(F32)

        def body(i, _):
            n = k * self.count + i
            total = self.before[n].astype(F32) + self.other[n].astype(F32) * weight
            result[n] = total.astype(BF16)
            return 0

        lax.fori_loop(0, self.count, body, 0)


class Locals:
    def __init__(self, sems):
        self.sems, self.used, self.open = sems, 0, []

    def copy(self, src, dst):
        made = pltpu.make_async_copy(src, dst, self.sems.at[self.used])
        self.used += 1
        made.start()
        return made

    def save(self, src, dst):
        self.open.append(self.copy(src, dst))

    def finish(self):
        for made in self.open:
            made.wait()


def load_columns(local, full, rows, dst, stage):
    seq, _, cols = full.shape
    if cols % 128 == 0:
        return [local.copy(full.at[s, rows], dst.at[:, pl.ds(s * cols, cols)]) for s in range(seq)]
    for s in range(seq):
        local.copy(full.at[s, rows], stage.at[pl.ds(0, rows.size)]).wait()
        dst[:, s * cols : (s + 1) * cols] = stage[: rows.size]
    return []


def load_plane(local, full, rows, zz, dst, stage):
    cols = full.shape[2]
    if cols % 128 == 0:
        return [
            local.copy(full.at[2 * zz + core, rows], dst.at[:, pl.ds(core * cols, cols)])
            for core in range(2)
        ]
    for core in range(2):
        local.copy(full.at[2 * zz + core, rows], stage.at[core, pl.ds(0, rows.size)]).wait()
    dst[...] = jnp.concatenate([stage[0, 0 : rows.size], stage[1, 0 : rows.size]], axis=1)
    return []


def stream(order, source, slots, sems, body, after):
    def fetch(n):
        return pltpu.make_async_copy(source(order[n]), slots.at[n % 2], sems.at[n % 2])

    fetch(0).start()
    for n, s in enumerate(order):
        if n + 1 < len(order):
            fetch(n + 1).start()
        fetch(n).wait()
        body(s, n % 2)
        after()


def forward_kernel(batch, seq, spans, *refs):
    (x_hbm, in_hbm, out_w_hbm, gain_hbm, pair_hbm, down_hbm), refs = refs[:6], refs[6:]
    fulls, refs = refs[:4], refs[4:]
    out_hbm, saved, refs = refs[0], refs[1:13], refs[13:]
    (q_out, k_out, v_out, raw_out, att_out, e_out, gated_out, mid_out, nb_out, pair_out, hid_out, na_out) = saved
    (x, na, tmp, qkvr, att, gated, mid, nb, w_in, w_out, gain, w_pair, tmp_g, tmp_u, pair, hid,
     w_down, res, stage, turned_pair, gain_own, na_t, gated_t, nb_t, hid_t, mine, other, before, chain_out, early, chain_sems, slot_sems, pair_sems,
     local_sems, gather_sems, gather_local, *held) = refs
    place = Place(batch, seq)
    local = Locals(local_sems)
    load_in = local.copy(in_hbm, held[0])
    load_x = local.copy(x_hbm, x)
    load_gain = local.copy(gain_hbm, gain_own)
    load_out = local.copy(out_w_hbm, held[1].at[pl.ds(0, D)])
    load_turned = local.copy(pair_hbm, turned_pair)
    load_down = local.copy(down_hbm, held[3])
    gather = Gather(place, held, fulls, (True, True, True, True), gather_sems, gather_local)
    place.barrier()
    rows, span = x.shape[0], spans
    per_group = seq // 4
    blocks = rows // span
    pairs = D // 128
    cols_in = w_in.shape[-1]
    half = seq // 2
    planes = place.planes
    cols_two = 2 * fulls[1].shape[2]
    q, k, v, raw = (qkvr.at[n] for n in range(4))
    first, second, own, own_f = pair_masks(span)
    steps = Steps(FORWARD_STEPS if place.square and place.planes == 4 else {})
    plan_gather(steps, gather, 4)

    def have(w, n):
        steps.finish(lambda name: not steps.table and name[0] != "c" and name[1] <= w)
        return gather.have(w, n)

    load_in.wait()
    steps.run(("start", 0))
    steps.tick()
    load_x.wait()

    def norm_rows(r):
        xr = x[r, :].astype(F32)
        na[r, :] = (xr * lax.rsqrt(mean_square(xr) + 1e-6)).astype(BF16)

    row_loop(rows, 64, norm_rows)
    load_gain.wait()
    load_out.wait()
    top = lax.broadcasted_iota(jnp.int32, (GAIN_ROWS, gain_own.shape[1]), 0) == 0
    held[1][D : D + GAIN_ROWS, :] = jnp.where(top, gain_own[...].astype(F32), 0.0).astype(BF16)
    load_turned.wait()
    transpose(turned_pair, held[2])
    load_down.wait()
    steps.tick()

    def project(s, slot):
        group, n = lax.div(s, per_group), lax.rem(s, per_group)
        tmp[...] = dot(na[...], w_in[slot])
        at = pl.ds(pl.multiple_of(n * cols_in, 128), cols_in)

        @pl.when(s < 2 * per_group)
        def _():
            def finish_rows(r):
                value = tmp[r, :]
                value = jnp.maximum(value, 0.0) + jnp.log1p(jnp.exp(-jnp.abs(value)))
                qkvr[group, r, at] = value.astype(BF16)

            row_loop(rows, 64, finish_rows)

        @pl.when(s >= 2 * per_group)
        def _():
            def finish_rows(r):
                qkvr[group, r, at] = tmp[r, :].astype(BF16)

            row_loop(rows, 64, finish_rows)

    for n in range(planes):
        zz = have(0, n)
        blocks_in = [
            pltpu.make_async_copy(fulls[0].at[2 * zz + c], w_in.at[c], slot_sems.at[c]) for c in range(2)
        ]
        for made in blocks_in:
            made.start()
        for c, made in enumerate(blocks_in):
            made.wait()
            project(2 * zz + c, c)
            steps.tick()

    def state(n):
        i, j = lax.div(n, pairs), lax.rem(n, pairs)
        at, block = tokens(i, span), lanes(j)
        return pack_state(dot_tn(k[at, block], v[at, block])).astype(BF16)

    def keep_state(n, value):
        mine[n] = value

    chain = Chain(place, True, mine, other, before, chain_out, chain_sems)
    for part in range(Chain.PARTS):
        grouped(part * chain.count, (part + 1) * chain.count, state, keep_state)
        chain.start(part, steps)
        steps.tick()
    for src, dst in ((q, q_out), (k, k_out), (v, v_out), (raw, raw_out)):
        local.save(src, dst)

    row = lax.rem(lax.broadcasted_iota(jnp.int32, (2 * span, span), 0), span)
    col = lax.broadcasted_iota(jnp.int32, (2 * span, span), 1)
    lane = lax.broadcasted_iota(jnp.int32, (span, 128), 1)

    def inner(n):
        i, j = lax.div(n, pairs), lax.rem(n, pairs)
        at, block = tokens(i, span), lanes(j)
        scores = dot_nt(by_head(q[at, block], first, second), k[at, block])
        scores = jnp.where(row >= col, scores, 0.0).astype(BF16)
        both = dot(scores, v[at, block])
        return jnp.where(lane < HEAD_DIM, both[:span], both[span:])

    def keep_inner(n, value):
        att[tokens(lax.div(n, pairs), span), lanes(lax.rem(n, pairs))] = value

    for i in range(blocks):
        grouped(i * pairs, (i + 1) * pairs, inner, keep_inner)
        steps.tick()

    transpose(na, na_t)
    local.save(na_t, na_out)
    steps.tick()
    chain.finish(0, steps, early)
    loads = []
    for n in range(planes):
        zz = have(1, n)
        to = pl.ds(pl.multiple_of(zz * cols_two, 128), cols_two)
        loads += load_plane(local, fulls[1], pl.ds(0, D), zz, w_out.at[:, to], stage)
        loads += load_plane(local, fulls[1], pl.ds(D, 16), zz, gain.at[:, to], stage)
    for made in loads:
        made.wait()
    steps.tick()

    def outer(n):
        i, j = lax.div(n, pairs), lax.rem(n, pairs)
        at, block = tokens(i, span), lanes(j)
        a = att[at, block] + dot(q[at, block], unpack_state(early[n], own))
        unit = a * lax.rsqrt(head_sums(a * a, own) * (1.0 / HEAD_DIM) + 1e-5)
        normed = unit * gain[0:1, block].astype(F32)
        return a, (jax.nn.sigmoid(raw[at, block].astype(F32)) * normed).astype(BF16)

    def keep_outer(n, value):
        at, block = tokens(lax.div(n, pairs), span), lanes(lax.rem(n, pairs))
        att[at, block], gated[at, block] = value

    for i in range(blocks):
        if i == blocks // 2:
            chain.finish(1, steps, early)
        grouped(i * pairs, (i + 1) * pairs, outer, keep_outer)
        steps.tick()
    local.save(early, e_out)
    local.save(att, att_out)

    def turn(src, dst, blocks_of):
        for block in blocks_of:
            at = slice(block * 128, min((block + 1) * 128, src.shape[1]))
            dst[at, :] = src[:, at].T

    for n in range(D // 512):
        at = pl.ds(n * 512, 512)
        mid[:, at] = x[:, at].astype(F32) + dot(gated[...], w_out[:, at])
        turn(gated, gated_t, range(n * 4, n * 4 + 4))
        steps.tick()
    local.save(gated_t, gated_out)

    def norm_mid(r):
        m = mid[r, :]
        nb[r, :] = (m * lax.rsqrt(mean_square(m) + 1e-6)).astype(BF16)

    row_loop(rows, 64, norm_mid)
    local.save(mid, mid_out)
    steps.tick()

    def fetch_pair(j, slot):
        return [
            pltpu.make_async_copy(
                fulls[2].at[j + side * half], w_pair.at[slot, side], pair_sems.at[slot, side]
            )
            for side in range(2)
        ]

    early_half = planes == 4
    away = jnp.where(place.z < 2, 0, 2) if early_half else 0
    for n in range(planes - 1 if early_half else planes):
        have(2, n)
    for made in fetch_pair(away, 0):
        made.start()
    count_t = -(-hid.shape[-1] // 128)

    def finish_pair(n, part):
        j, slot = lax.rem(n + away, half), n % 2
        for row in range(part * rows // 2, (part + 1) * rows // 2, 64):
            r = slice(row, row + 64)
            gate, up = tmp_g[slot, r, :], tmp_u[slot, r, :]
            pair[j, r, :] = gate.astype(BF16)
            pair[j + half, r, :] = up.astype(BF16)
            hid[j, r, :] = (gate * up).astype(BF16)

    def save_pair(n):
        j = lax.rem(n + away, half)
        local.save(pair.at[j], pair_out.at[j])
        local.save(pair.at[j + half], pair_out.at[j + half])

    def turn_hid(n):
        j = lax.rem(n + away, half)
        turn(hid.at[j], hid_t.at[j], range(count_t))
        local.save(hid_t.at[j], hid_out.at[j])

    for n in range(half):
        j, slot = lax.rem(n + away, half), n % 2
        if early_half and n == 1:
            have(2, planes - 1)
        if n + 1 < half:
            for made in fetch_pair(lax.rem(n + 1 + away, half), 1 - slot):
                made.start()
        for made in fetch_pair(j, slot):
            made.wait()
        tmp_g[slot] = dot(nb[...], w_pair[slot, 0])
        if n > 0:
            finish_pair(n - 1, 0)
        else:
            turn(nb, nb_t, range(D // 256))
        steps.tick()
        tmp_u[slot] = dot(nb[...], w_pair[slot, 1])
        if n > 0:
            finish_pair(n - 1, 1)
            save_pair(n - 1)
        else:
            turn(nb, nb_t, range(D // 256, D // 128))
            local.save(nb_t, nb_out)
        if n > 1:
            turn_hid(n - 2)
        steps.tick()
    finish_pair(half - 1, 0)
    finish_pair(half - 1, 1)
    save_pair(half - 1)
    steps.tick()

    width = hid.shape[-1]

    def down(zz, slot):
        at = pl.ds(pl.multiple_of(zz * cols_two, 128), cols_two)
        total = mid[:, at]
        for j in range(half):
            total = total + dot(hid[j], w_down[slot, j * width : (j + 1) * width, :])
        res[:, at] = total.astype(BF16)

    later = [half - 2, half - 1]
    before_it = None
    for n in range(planes):
        zz = have(3, n)
        loads = load_plane(local, fulls[3], pl.ds(0, FF), zz, w_down.at[n % 2], stage)
        if before_it is not None:
            down(*before_it)
            if later:
                turn_hid(later.pop(0))
            steps.tick()
        for made in loads:
            made.wait()
        before_it = (zz, n % 2)
    down(*before_it)
    local.save(res, out_hbm)
    steps.tick()
    steps.finish()
    local.finish()
    place.finish()


def forward(batch, seq, x, span, shards):
    attn_in, attn_out, out_gain, glu_in, glu_out = shards
    shards = (attn_in, jax.ShapeDtypeStruct((D + GAIN_ROWS, attn_out.shape[1]), BF16), glu_in, glu_out)
    rows = x.shape[0]
    cols_in, cols_pair = shards[0].shape[1], shards[2].shape[1]
    half = seq // 2
    states = (rows // span) * (D // 128)
    big = jax.ShapeDtypeStruct((rows, D), BF16)
    big_f = jax.ShapeDtypeStruct((rows, D), F32)
    narrow = shards[3].shape[1] % 128 != 0
    any_space = pl.BlockSpec(memory_space=pl.ANY)
    out_shape = [jax.ShapeDtypeStruct((seq, *a.shape), a.dtype) for a in shards]
    out_shape += [big, big, big, big, big, big_f]
    turned = jax.ShapeDtypeStruct((D, rows), BF16)
    out_shape += [jax.ShapeDtypeStruct((states, HEAD_DIM, 128), BF16), turned, big_f, turned]
    out_shape += [
        jax.ShapeDtypeStruct((seq, rows, cols_pair), BF16),
        jax.ShapeDtypeStruct((half, cols_pair, rows), BF16),
        turned,
    ]
    wide, wide_f = pltpu.VMEM((rows, D), BF16), pltpu.VMEM((rows, D), F32)
    pair_f = pltpu.VMEM((2, rows, cols_pair), F32)
    scratch = [
        wide, wide, pltpu.VMEM((rows, cols_in), F32), pltpu.VMEM((4, rows, D), BF16), wide_f, wide, wide_f, wide,
        pltpu.VMEM((2, D, cols_in), BF16),
        pltpu.VMEM((D, D), BF16),
        pltpu.VMEM((16, D), BF16),
        pltpu.VMEM((2, 2, D, cols_pair), BF16),
        pair_f, pair_f,
        pltpu.VMEM((seq, rows, cols_pair), BF16),
        pltpu.VMEM((half, rows, cols_pair), BF16),
        pltpu.VMEM((2, FF, 2 * shards[3].shape[1]), BF16),
        wide,
        pltpu.VMEM((2, FF, shards[3].shape[1]) if narrow else (2, 16, 128), BF16),
        pltpu.VMEM((cols_pair, D), BF16),
        pltpu.VMEM((1, attn_out.shape[1]), BF16),
        *[pltpu.VMEM((D, rows), BF16)] * 3,
        pltpu.VMEM((half, cols_pair, rows), BF16),
        *[pltpu.VMEM((states, HEAD_DIM, 128), BF16)] * 5,
        pltpu.SemaphoreType.DMA((6, Chain.PARTS)),
        pltpu.SemaphoreType.DMA((2,)),
        pltpu.SemaphoreType.DMA((2, 2)),
        pltpu.SemaphoreType.DMA((128,)),
        pltpu.SemaphoreType.DMA((Gather.KINDS, 4, half)),
        pltpu.SemaphoreType.DMA((4,)),
        *[pltpu.VMEM(a.shape, a.dtype) for a in shards],
    ]
    return pl.pallas_call(
        functools.partial(forward_kernel, batch, seq, span),
        out_shape=out_shape,
        in_specs=[any_space] * 6,
        out_specs=[any_space] * len(out_shape),
        scratch_shapes=scratch,
        compiler_params=pltpu.CompilerParams(
            collective_id=0, has_side_effects=True, vmem_limit_bytes=62 * 1024 * 1024
        ),
        name="forward",
    )(x, attn_in, attn_out, out_gain.reshape(1, -1), glu_in.T, glu_out)


WIDE = (False, True, False, True)
Z_PARTS = (1, 4, 1, 4)


def slope(plus):
    series = plus * (1.0 - plus * (0.5 - plus * (1.0 / 6.0)))
    return jnp.where(plus < 0.02, series, 1.0 - jnp.exp(-plus))


def backward_kernel(batch, seq, span, *refs):
    g_hbm, x_hbm, *fulls = refs[:6]
    (q_in, k_in, v_in, raw_in, att_in, e_in, gated_in, mid_in, nb_in, pair_in, hid_in, na_in) = refs[6:18]
    grad_hbm, sums, gm_hbm, far = refs[18], refs[19:23], refs[23], refs[24:28]
    refs = list(refs[28:])
    place = Place(batch, seq)
    reds = []
    for w in range(4):
        reds.append(Reduce(place, WIDE[w], Z_PARTS[w], sums[w], far[w], refs[:11]))
        refs = refs[11:]
    (tall, turned, pair, fields, f0, f1, g, split, low, down, slots, wide_out, slim_out, gain, gain_sums, gain_split,
     early, mine, other, before, chain_out, stage, chain_sems, slot_sems, local_sems) = refs
    red_down, red_pair, red_out, red_in = reds
    local = Locals(local_sems)
    rows = g.shape[0]
    half = seq // 2
    planes = half
    width = hid_in.shape[1]
    cols_in, cols_out, cols_pair = fulls[0].shape[2], fulls[1].shape[2], fulls[2].shape[2]
    per_group, per_block = seq // 4, cols_in // 128
    blocks, pairs = rows // span, D // 128
    first, second, own, own_f = pair_masks(span)
    core, sibling = place.c, 1 - place.c
    steps = Steps(BACKWARD_STEPS if place.square and place.planes == 4 else {})

    load_g = local.copy(g_hbm, g)
    load_hid = [local.copy(hid_in.at[j], tall.at[pl.ds(j * width, width)]) for j in range(half)]
    load_nb = local.copy(nb_in, turned)
    load_pair = [local.copy(pair_in.at[s], pair.at[s]) for s in range(seq)]
    load_e = local.copy(e_in, early)
    place.barrier()

    def split_columns(src):
        for s in range(seq):
            to = (s % 2) * (D // 2) + (s // 2) * cols_out
            split[:, to : to + cols_out] = src[:, s * cols_out : (s + 1) * cols_out]

    def by_core(which):
        return pl.ds(pl.multiple_of(which * (D // 2), D // 2), D // 2)

    slim_sent = []

    def slim_send(red, row, count, k, fill):
        slot = len(slim_sent) % 2
        if len(slim_sent) >= 2:
            for made in slim_sent[-2]:
                made().wait_send()
        fill(slot)
        sent = []
        for zz in range(planes):
            src = slim_out.at[slot, zz, pl.ds(0, count)]
            sent.append(functools.partial(red.core_copy, zz, src, row, count, k))
            sent[-1]().start()
        slim_sent.append(sent)

    def slim_theirs(red, lhs, at, row, count, k):
        def fill(slot):
            value = dot(lhs[at : at + count, :], split[:, by_core(sibling)])
            for zz in range(planes):
                slim_out[slot, zz, 0:count, :] = value[:, zz * cols_out : (zz + 1) * cols_out].astype(BF16)

        slim_send(red, row, count, k, fill)

    def slim_mine(red, lhs, at, row, count, k):
        value = dot(lhs[at : at + count, :], split[:, by_core(core)])
        for zz in range(planes):
            red.core_copy(zz, None, row, count, k).wait_recv()
            here = red.part[zz, row : row + count, :].astype(F32)
            here = here + value[:, zz * cols_out : (zz + 1) * cols_out]
            red.part[zz, row : row + count, :] = here.astype(BF16)

    wide_sent = []

    def wide_theirs(red, cols, zz):
        slot = len(wide_sent) % 2
        if len(wide_sent) >= 2:
            wide_sent[-2]().wait_send()
        s = 2 * zz + sibling

        for row in range(0, D, 256):
            r = slice(row, row + 256)
            wide_out[slot, r, 0:cols] = dot(turned[r, :], pair[s, :, 0:cols]).astype(BF16)
        src = wide_out.at[slot] if cols == wide_out.shape[2] else wide_out.at[slot, :, pl.ds(0, cols)]
        wide_sent.append(functools.partial(red.core_copy, zz, src, 0, D, 0))
        wide_sent[-1]().start()
        steps.tick()

    def wide_mine(red, r, cols, zz):
        s = 2 * zz + core
        red.core_copy(zz, None, 0, D, 0).wait_recv()

        for row in range(0, D, 256):
            at = slice(row, row + 256)
            here = red.part[zz, at, :].astype(F32) + dot(turned[at, :], pair[s, :, 0:cols])
            red.part[zz, at, :] = here.astype(BF16)
        if red.wide:
            red.plane_1(zz)
        red.plane_plan(steps, r, zz)
        red.z_plan(steps, r, zz)
        steps.tick()

    load_g.wait()
    split_columns(g)
    for made in load_hid:
        made.wait()
    for j in range(half):
        slim_theirs(red_down, tall, j * width, j * width, width, j)
    for j in range(half):
        slim_mine(red_down, tall, j * width, j * width, width, j)
    for zz in range(planes):
        red_down.z_plan(steps, 0, zz)
    red_down.late_plan(steps, 0)
    red_down.spread_plan(steps, 0)
    steps.tick()

    def load_down(j):
        at = pl.ds((j % 2) * width, width)
        return load_columns(local, fulls[3], pl.ds(j * width, width), down.at[at], stage)

    for made in load_pair:
        made.wait()
    waits = load_down(0)
    grads = (f0, f1)

    def finish_pair(j):
        for row in range(0, rows, 64):
            r = slice(row, row + 64)
            grad = grads[j % 2][r, 0:width]
            gate, up = pair[j, r, :].astype(F32), pair[j + half, r, :].astype(F32)
            pair[j, r, :] = (grad * up).astype(BF16)
            pair[j + half, r, :] = (grad * gate).astype(BF16)

    for j in range(half):
        after = load_down(j + 1) if j + 1 < half else []
        for made in waits:
            made.wait()
        waits = after
        at = (j % 2) * width
        grads[j % 2][:, 0:width] = dot_nt(g[...], down[at : at + width, :])
        if j > 0:
            finish_pair(j - 1)
        steps.tick()
    finish_pair(half - 1)
    load_mid = local.copy(mid_in, f1)

    load_nb.wait()
    wide_theirs(red_pair, cols_pair, 0)
    for zz in range(planes):
        if zz + 1 < planes:
            wide_theirs(red_pair, cols_pair, zz + 1)
        wide_mine(red_pair, 1, cols_pair, zz)
    red_pair.spread_plan(steps, 1)
    load_gated = local.copy(gated_in, turned)
    w_out = down.at[pl.ds(0, D)]
    load_out = load_columns(local, fulls[1], pl.ds(0, D), w_out, stage)
    load_out += load_columns(local, fulls[1], pl.ds(D, 16), gain, stage)
    views = []
    for k, src in enumerate((q_in, k_in, v_in, raw_in)):
        for side in range(2):
            to = tall.at[pl.ds((2 * k + side) * rows, rows)]
            views.append(local.copy(src.at[:, pl.ds(side * (D // 2), D // 2)], to))

    for made in wide_sent[-2:]:
        made().wait_send()
    wide_sent.clear()
    places = (slots.at[0], slots.at[1], wide_out.at[0], wide_out.at[1])

    def fetch_pair(n):
        return [
            pltpu.make_async_copy(fulls[2].at[s], places[s % 4], slot_sems.at[s % 4])
            for s in (2 * n, 2 * n + 1)
        ]

    for made in fetch_pair(0):
        made.start()
    for n in range(half):
        if n + 1 < half:
            for made in fetch_pair(n + 1):
                made.start()
        for made in fetch_pair(n):
            made.wait()
        value = sum(dot_nt(pair[s], places[s % 4][...]) for s in (2 * n, 2 * n + 1))
        f0[...] = value if n == 0 else f0[...] + value
        steps.tick()
    load_mid.wait()

    def back_mid(r):
        m, grad = f1[r, :], f0[r, :]
        scale = lax.rsqrt(mean_square(m) + 1e-6)
        inner = jnp.mean(grad * m, axis=-1, keepdims=True)
        total = g[r, :].astype(F32) + scale * grad - m * (scale * scale * scale) * inner
        f1[r, :] = total
        low[r, :] = total.astype(BF16)

    row_loop(rows, 64, back_mid)
    save_gm = local.copy(f1, gm_hbm)
    split_columns(low)
    steps.tick()

    load_gated.wait()
    for k in range(2):
        slim_theirs(red_out, turned, k * (D // 2), k * (D // 2), D // 2, k)
    for made in load_out:
        made.wait()
    for n in range(D // 512):
        at = pl.ds(n * 512, 512)
        f0[:, at] = dot_nt(low[...], w_out[at, :])
    for k in range(2):
        slim_mine(red_out, turned, k * (D // 2), k * (D // 2), D // 2, k)
    load_na = local.copy(na_in, turned)
    load_x = local.copy(x_hbm, low)
    save_gm.wait()
    load_att = local.copy(att_in, f1)
    gain_sums[...] = jnp.zeros_like(gain_sums)
    for made in views:
        made.wait()
    load_e.wait()
    load_att.wait()
    steps.tick()

    def view(k, i, j):
        row = pl.multiple_of((2 * k + lax.div(j, pairs // 2)) * rows + i * span, span)
        return pl.ds(row, span), lanes(lax.rem(j, pairs // 2))

    def put(group, i, j, value):
        s = group * per_group + lax.div(j, per_block)
        pair[s, tokens(i, span), lanes(lax.rem(j, per_block))] = value

    def place_of(n):
        return lax.div(n, pairs), lax.rem(n, pairs)

    def back_gate(n):
        i, j = place_of(n)
        at, block = tokens(i, span), lanes(j)
        a, grad = f1[at, block], f0[at, block]
        scale = lax.rsqrt(head_sums(a * a, own) * (1.0 / HEAD_DIM) + 1e-5)
        unit = a * scale
        gains = gain[0:1, block].astype(F32)
        sig = jax.nn.sigmoid(tall[view(3, i, j)].astype(F32))
        grad_normed = grad * sig
        grad_gate = (grad * (unit * gains) * sig * (1.0 - sig)).astype(BF16)
        gain_sum = jnp.sum(grad_normed * unit, axis=0, keepdims=True)
        grad_unit = grad_normed * gains
        inner = head_sums(grad_unit * a, own) * (1.0 / HEAD_DIM)
        grad_a = (scale * grad_unit - a * (scale * scale * scale) * inner).astype(BF16)
        state = pack_state(dot_tn(tall[view(0, i, j)], grad_a)).astype(BF16)
        return grad_gate, gain_sum, grad_a, state

    def keep_gate(n, value):
        i, j = place_of(n)
        put(3, i, j, value[0])
        gain_sums[0:1, lanes(j)] += value[1]
        g[tokens(i, span), lanes(j)] = value[2]
        mine[n] = value[3]

    chain = Chain(place, False, mine, other, before, chain_out, chain_sems)
    for i in range(blocks):
        grouped(i * pairs, (i + 1) * pairs, back_gate, keep_gate)
        if (i + 1) % (blocks // Chain.PARTS) == 0:
            chain.start(i // (blocks // Chain.PARTS), steps)
        steps.tick()

    for s in range(seq):
        to = (s // 2) * cols_out
        gain_split[s % 2, :, to : to + cols_out] = gain_sums[:, s * cols_out : (s + 1) * cols_out]
    top = lax.broadcasted_iota(jnp.int32, (GAIN_ROWS, cols_out), 0) == 0

    def gain_rows(which, zz):
        row = gain_split[which, 0:1, zz * cols_out : (zz + 1) * cols_out]
        return jnp.where(top, row, 0.0)

    def fill_gain(slot):
        for zz in range(planes):
            slim_out[slot, zz, 0:GAIN_ROWS, :] = gain_rows(sibling, zz).astype(BF16)

    slim_send(red_out, D, GAIN_ROWS, 2, fill_gain)
    load_na.wait()
    ready = [zz for zz in range(planes) if zz * 2 >= 3 * per_group]
    for zz in ready:
        wide_theirs(red_in, cols_in, zz)
    for zz in range(planes):
        red_out.core_copy(zz, None, D, GAIN_ROWS, 2).wait_recv()
        here = red_out.part[zz, D : D + GAIN_ROWS, :].astype(F32) + gain_rows(core, zz)
        red_out.part[zz, D : D + GAIN_ROWS, :] = here.astype(BF16)
    for zz in range(planes):
        red_out.z_plan(steps, 2, zz)
    red_out.late_plan(steps, 2)
    red_out.spread_plan(steps, 2)
    steps.tick()
    for zz in ready:
        wide_mine(red_in, 3, cols_in, zz)

    t_of = lax.rem(lax.broadcasted_iota(jnp.int32, (span, 2 * span), 1), span)
    s_of = lax.broadcasted_iota(jnp.int32, (span, 2 * span), 0)
    t_down = lax.rem(lax.broadcasted_iota(jnp.int32, (2 * span, span), 0), span)
    s_down = lax.broadcasted_iota(jnp.int32, (2 * span, span), 1)
    lane = lax.broadcasted_iota(jnp.int32, (span, 128), 1)

    def back_attention(n):
        i, j = place_of(n)
        qs, ks, vs = (tall[view(k, i, j)] for k in range(3))
        grads = g[tokens(i, span), lanes(j)]
        q2, g2 = by_head(qs, first, second), by_head(grads, first, second)
        scores = jnp.where(t_of >= s_of, dot_nt(ks, q2), 0.0).astype(BF16)
        grad_t = jnp.where(t_of >= s_of, dot_nt(vs, g2), 0.0).astype(BF16)
        grad_s = jnp.where(t_down >= s_down, dot_nt(g2, vs), 0.0).astype(BF16)
        both = dot(grad_s, ks)
        grad_q = jnp.where(lane < HEAD_DIM, both[:span], both[span:])
        grad_q = grad_q + dot_nt(grads, unpack_state(early[n], own))
        return dot(grad_t, q2), dot(scores, g2), (grad_q * slope(qs.astype(F32))).astype(BF16)

    def keep_attention(n, value):
        i, j = place_of(n)
        at, block = tokens(i, span), lanes(j)
        f0[at, block], f1[at, block] = value[:2]
        put(0, i, j, value[2])

    for i in range(blocks):
        grouped(i * pairs, (i + 1) * pairs, back_attention, keep_attention, 2)
        steps.tick()
    ready_q = [zz for zz in range(planes) if (zz + 1) * 2 <= per_group]
    for zz in ready_q:
        wide_theirs(red_in, cols_in, zz)
    for zz in ready_q:
        wide_mine(red_in, 3, cols_in, zz)

    def back_states(n):
        i, j = place_of(n)
        at, block = tokens(i, span), lanes(j)
        ks, vs = tall[view(1, i, j)], tall[view(2, i, j)]
        later = unpack_state(other[n], own)
        grad_k = (f0[at, block] + dot_nt(vs, later)) * slope(ks.astype(F32))
        return grad_k.astype(BF16), (f1[at, block] + dot(ks, later)).astype(BF16)

    def keep_states(n, value):
        put(1, *place_of(n), value[0])
        put(2, *place_of(n), value[1])

    for part in range(Chain.PARTS):
        chain.finish(part, steps, other)
        grouped(part * chain.count, (part + 1) * chain.count, back_states, keep_states)
        steps.tick()
    load_gm = local.copy(gm_hbm, f1)
    rest = [zz for zz in range(planes) if zz not in ready and zz not in ready_q]
    for n, zz in enumerate(rest):
        if n >= 2:
            wide_mine(red_in, 3, cols_in, rest[n - 2])
        wide_theirs(red_in, cols_in, zz)
    for zz in rest[-2:]:
        wide_mine(red_in, 3, cols_in, zz)
    red_in.spread_plan(steps, 3)

    places_in = [slots.at[k, :, pl.ds(0, cols_in)] for k in range(2)]
    places_in += [down.at[pl.ds(0, D), pl.ds(k * (D // 2), cols_in)] for k in range(2)]

    def fetch_in(n):
        return [
            pltpu.make_async_copy(fulls[0].at[s], places_in[s % 4], slot_sems.at[s % 4])
            for s in (2 * n, 2 * n + 1)
        ]

    for made in fetch_in(0):
        made.start()
    for n in range(half):
        if n + 1 < half:
            for made in fetch_in(n + 1):
                made.start()
        for made in fetch_in(n):
            made.wait()
        value = sum(dot_nt(pair[s, :, 0:cols_in], places_in[s % 4][...]) for s in (2 * n, 2 * n + 1))
        f0[...] = value if n == 0 else f0[...] + value
        steps.tick()
    load_gm.wait()
    load_x.wait()

    def back_x(r):
        x, grad = low[r, :].astype(F32), f0[r, :]
        scale = lax.rsqrt(mean_square(x) + 1e-6)
        inner = jnp.mean(grad * x, axis=-1, keepdims=True)
        f1[r, :] += scale * grad - x * (scale * scale * scale) * inner

    row_loop(rows, 64, back_x)
    local.save(f1, grad_hbm)
    steps.tick()
    steps.finish()
    local.finish()
    for sent in slim_sent[-2:]:
        for made in sent:
            made().wait_send()
    for made in wide_sent[-2:]:
        made().wait_send()
    place.finish()


def backward(batch, seq, span, grad, x, fulls, saved):
    rows = x.shape[0]
    half = seq // 2
    cols_in, cols_out, cols_pair = fulls[0].shape[2], fulls[1].shape[2], fulls[2].shape[2]
    width = saved[10].shape[1]
    square = batch == 4
    shapes = ((FF, cols_out), (D, cols_pair), (D + GAIN_ROWS, cols_out), (D, cols_in))
    states = (rows // span) * (D // 128)
    any_space = pl.BlockSpec(memory_space=pl.ANY)
    big_f = jax.ShapeDtypeStruct((rows, D), F32)
    out_shape = [big_f] + [jax.ShapeDtypeStruct(shape, BF16) for shape in shapes] + [big_f]
    out_shape += [Reduce.far(square, WIDE[w], half, *shapes[w]) for w in range(4)]
    scratch = []
    core_parts = (half, 1, 3, 1)
    for w in range(4):
        scratch += Reduce.scratch(square, WIDE[w], half, *shapes[w], core_parts[w], Z_PARTS[w])
    narrow = cols_out % 128 != 0
    state = pltpu.VMEM((states, HEAD_DIM, 128), BF16)
    scratch += [
        pltpu.VMEM((max(FF, 8 * rows), D // 2), BF16),
        pltpu.VMEM((D, rows), BF16),
        pltpu.VMEM((seq, rows, cols_pair), BF16),
        pltpu.VMEM((16, 128), BF16),
        pltpu.VMEM((rows, D), F32),
        pltpu.VMEM((rows, D), F32),
        pltpu.VMEM((rows, D), BF16),
        pltpu.VMEM((rows, D), BF16),
        pltpu.VMEM((rows, D), BF16),
        pltpu.VMEM((max(2 * width, D), D), BF16),
        pltpu.VMEM((2, D, cols_pair), BF16),
        pltpu.VMEM((2, D, cols_pair), BF16),
        pltpu.VMEM((2, half, max(width, D // 2), cols_out), BF16),
        pltpu.VMEM((16, D), BF16),
        pltpu.VMEM((8, D), F32),
        pltpu.VMEM((2, 8, D // 2), F32),
        state, state, state, state, state,
        pltpu.VMEM((D, cols_out) if narrow else (16, 128), BF16),
        pltpu.SemaphoreType.DMA((6, Chain.PARTS)),
        pltpu.SemaphoreType.DMA((4,)),
        pltpu.SemaphoreType.DMA((192,)),
    ]
    return pl.pallas_call(
        functools.partial(backward_kernel, batch, seq, span),
        out_shape=out_shape,
        in_specs=[any_space] * 18,
        out_specs=[any_space] * len(out_shape),
        scratch_shapes=scratch,
        compiler_params=pltpu.CompilerParams(
            collective_id=1, has_side_effects=True, vmem_limit_bytes=63 * 1024 * 1024
        ),
        name="backward",
    )(grad, x, *fulls, *saved)


def local(block_in, attn_in, attn_out, out_gain, glu_in, glu_out, block_grad):
    seq_count, span = block_in.shape[:2]
    rows = seq_count * span
    batch, seq = lax.axis_size("batch"), lax.axis_size("seq")
    x = block_in.reshape(rows, D)
    parts = forward(batch, seq, x, span, (attn_in, attn_out, out_gain, glu_in, glu_out))
    fulls, block_out, saved = parts[:4], parts[4], parts[5:]
    grads = backward(batch, seq, span, block_grad.reshape(rows, D), x, fulls, saved)
    input_grad, sums = grads[0], list(grads[1:5])
    if batch != 4:
        sums = [lax.psum(a, "batch") for a in sums]
    down, pair, out, into = (a.astype(F32) for a in sums)
    return (
        block_out.reshape(block_in.shape),
        input_grad.reshape(block_in.shape),
        into,
        out[:D],
        out[D],
        pair,
        down,
    )


def solution(mesh):
    rows, columns = P("batch", "seq", None), P(None, "seq")
    return jax.shard_map(
        local,
        mesh=mesh,
        in_specs=(rows, columns, columns, P("seq"), columns, columns, rows),
        out_specs=(rows, rows, columns, columns, P("seq"), columns, columns),
        check_vma=False,
    )
```

```python
import functools

import jax
import jax.numpy as jnp
from jax import lax
from jax.experimental import pallas as pl
from jax.experimental.pallas import tpu as pltpu
from jax.sharding import PartitionSpec as P

HEADS = 16
HEAD_DIM = 64
D = 1024
FF = 2816
MESH = pl.DeviceIdType.MESH
BF16 = jnp.bfloat16
F32 = jnp.float32
GAIN_ROWS = 128


def run_if(cond, fn):
    if cond is None:
        fn()
    else:
        pl.when(cond)(fn)


class Place:
    def __init__(self, batch, seq):
        self.planes = seq // 2
        self.square = batch == 4
        self.b = lax.axis_index("batch")
        self.s = lax.axis_index("seq")
        self.z = lax.div(self.s, 2)
        self.c = lax.rem(self.s, 2)
        self.bx = self.b + 1 - 2 * lax.rem(self.b, 2)
        self.by = lax.rem(self.b + 2, 4)
        self.bd = lax.rem(self.bx + 2, 4)
        self.sib = (self.b, self.s + 1 - 2 * self.c)
        self.up = (self.b, self.s + 2)
        self.down = (self.b, self.s - 2)
        self.x = (self.bx, self.s)
        self.y = (self.by, self.s)
        self.has_up = self.z < self.planes - 1
        self.has_down = self.z > 0
        self.sent = []

    def barrier(self):
        sem = pltpu.get_barrier_semaphore()
        always = [self.sib] + ([self.x, self.y] if self.square else [])
        for device in always:
            pl.semaphore_signal(sem, inc=1, device_id=device, device_id_type=MESH)
        for cond, device in ((self.has_up, self.up), (self.has_down, self.down)):
            pl.when(cond)(
                lambda device=device: pl.semaphore_signal(
                    sem, inc=1, device_id=device, device_id_type=MESH
                )
            )
        ends = self.has_up.astype(jnp.int32) + self.has_down.astype(jnp.int32)
        pl.semaphore_wait(sem, len(always) + ends)

    def copy(self, src, dst, send_sem, recv_sem, device):
        return pltpu.make_async_remote_copy(
            src_ref=src,
            dst_ref=dst,
            send_sem=send_sem,
            recv_sem=recv_sem,
            device_id=device,
            device_id_type=MESH,
        )

    def send(self, make, cond=None):
        run_if(cond, lambda: make().start())
        self.sent.append((cond, make))

    def finish(self):
        for cond, make in self.sent:
            run_if(cond, lambda make=make: make().wait_send())
        self.sent = []


def first_half(quarter):
    return -(-quarter // 32) * 16


def quarter_rows(owner, quarter, half=None):
    if half is None:
        return pl.ds(pl.multiple_of(owner * quarter, 16), quarter)
    cut = first_half(quarter)
    start, rows = ((0, cut), (cut, quarter - cut))[half]
    return pl.ds(pl.multiple_of(owner * quarter + start, 16), rows)


class Gather:
    Z_UP, Z_DOWN, Z_IN, X_OUT, X_IN, Y_OUT, Y_IN, FX_OUT, FX_IN, FY_OUT, FY_IN = range(11)
    S_OUT, S_IN = 11, 15
    KINDS = 19

    def __init__(self, place, held, fulls, quartered, sems, local_sems):
        self.p, self.held, self.fulls, self.sems = place, held, fulls, sems
        self.local_sems = local_sems
        self.quartered = [q and place.square for q in quartered]

    def rows(self, w, owner, half=None):
        rows = self.held[w].shape[0]
        if not self.quartered[w]:
            return pl.ds(0, rows)
        return quarter_rows(owner, rows // 4, half)

    def move(self, w, zz, rows, out, into, device, core=None):
        core = self.p.c if core is None else core
        block = self.fulls[w].at[2 * zz + core, rows]
        return self.p.copy(
            block, block, self.sems.at[out, w, zz], self.sems.at[into, w, zz], device
        )

    def across(self, w, zz, piece, core=None):
        p = self.p
        rows = self.rows(w, (p.b, p.bx, p.by, p.bd)[piece])
        return self.move(w, zz, rows, self.S_OUT + piece, self.S_IN + piece, p.sib, core)

    def whole(self, w):
        p = self.p
        here = self.fulls[w].at[p.s]
        return p.copy(
            self.held[w], here, self.sems.at[self.S_OUT, w, p.z], self.sems.at[self.S_IN, w, p.z], p.sib
        )

    def start(self, w):
        p, own = self.p, self.held[w]
        here = self.fulls[w].at[p.s]
        rows = self.rows(w, p.b)
        for cond, device, out in (
            (p.has_up, p.up, self.Z_UP),
            (p.has_down, p.down, self.Z_DOWN),
        ):
            p.send(
                lambda device=device, out=out: p.copy(
                    own.at[rows],
                    here.at[rows],
                    self.sems.at[out, w, p.z],
                    self.sems.at[self.Z_IN, w, p.z],
                    device,
                ),
                cond,
            )
        p.send(lambda: self.whole(w))
        pltpu.make_async_copy(own, here, self.local_sems.at[w]).start()

    def sides(self, d):
        p = self.p
        return (
            (p.z >= d, p.z - d, p.has_up, p.up, self.Z_UP),
            (p.z + d < p.planes, p.z + d, p.has_down, p.down, self.Z_DOWN),
        )

    def from_z(self, w, d):
        p = self.p
        rows = self.rows(w, p.b)
        for cond, zz, more, device, out in self.sides(d):
            run_if(
                cond, lambda zz=zz: self.move(w, zz, rows, self.Z_UP, self.Z_IN, p.up).wait_recv()
            )
            p.send(
                lambda zz=zz, device=device, out=out: self.move(
                    w, zz, rows, out, self.Z_IN, device
                ),
                jnp.logical_and(cond, more),
            )
            p.send(lambda zz=zz: self.across(w, zz, 0), cond)

    def to_plane(self, w, d):
        p = self.p
        rows = self.rows(w, p.b)
        for cond, zz, *_ in self.sides(d):
            p.send(lambda zz=zz: self.move(w, zz, rows, self.X_OUT, self.X_IN, p.x), cond)
            p.send(lambda zz=zz: self.move(w, zz, rows, self.Y_OUT, self.Y_IN, p.y), cond)

    def from_plane(self, w, d):
        p = self.p
        from_x, from_y = self.rows(w, p.bx), self.rows(w, p.by)
        half_x, half_y = self.rows(w, p.bx, 0), self.rows(w, p.by, 1)
        for cond, zz, *_ in self.sides(d):
            run_if(
                cond, lambda zz=zz: self.move(w, zz, from_x, self.X_OUT, self.X_IN, p.x).wait_recv()
            )
            p.send(lambda zz=zz: self.move(w, zz, half_x, self.FY_OUT, self.FY_IN, p.y), cond)
            run_if(
                cond, lambda zz=zz: self.move(w, zz, from_y, self.Y_OUT, self.Y_IN, p.y).wait_recv()
            )
            p.send(lambda zz=zz: self.move(w, zz, half_y, self.FX_OUT, self.FX_IN, p.x), cond)
            p.send(lambda zz=zz: self.across(w, zz, 1), cond)
            p.send(lambda zz=zz: self.across(w, zz, 2), cond)

    def from_diagonal(self, w, d):
        p = self.p
        half_0, half_1 = self.rows(w, p.bd, 0), self.rows(w, p.bd, 1)
        for cond, zz, *_ in self.sides(d):
            run_if(
                cond,
                lambda zz=zz: self.move(w, zz, half_0, self.FY_OUT, self.FY_IN, p.y).wait_recv(),
            )
            run_if(
                cond,
                lambda zz=zz: self.move(w, zz, half_1, self.FX_OUT, self.FX_IN, p.x).wait_recv(),
            )
            p.send(lambda zz=zz: self.across(w, zz, 3), cond)

    def nearest(self, k):
        planes = self.p.planes
        found = jnp.int32(0)
        for z in range(planes):
            order = sorted(range(planes), key=lambda t: (abs(t - z), t))
            found = jnp.where(self.p.z == z, order[k], found)
        return found

    def have(self, w, k):
        p = self.p
        if k == 0:
            pltpu.make_async_copy(
                self.held[w], self.fulls[w].at[p.s], self.local_sems.at[w]
            ).wait()
            self.whole(w).wait_recv()
            return p.z
        zz = self.nearest(k)
        for piece in range(4 if self.quartered[w] else 1):
            self.across(w, zz, piece, 1 - p.c).wait_recv()
        return zz


class Steps:
    def __init__(self, table):
        self.table, self.todo, self.ticks = table, {}, 0

    def add(self, name, fn, *args):
        self.todo[name] = functools.partial(fn, *args)

    def run(self, name):
        step = self.todo.pop(name, None)
        if step is not None:
            step()

    def tick(self):
        for name in self.table.get(self.ticks, ()):
            self.run(name)
        self.ticks += 1

    def finish(self, wanted=lambda name: True):
        for name in [name for name in self.todo if wanted(name)]:
            self.run(name)


def plan_gather(steps, g, count):
    far = g.p.planes - 1
    for w in range(count):
        steps.add(("start", w), g.start, w)
        for d in range(1, far + 1):
            steps.add(("z", w, d), g.from_z, w, d)
        if g.quartered[w]:
            for name, step in (("x", g.to_plane), ("p", g.from_plane), ("g", g.from_diagonal)):
                for d in range(1, far + 1):
                    steps.add((name, w, d), step, w, d)


def add_into(dst, src, row, rows):
    cols = dst.shape[-1]
    chunk = max(
        k for k in range(16, rows + 1, 16) if rows % k == 0 and (k * cols <= 49152 or k == 16)
    )

    def body(i, _):
        here = pl.ds(pl.multiple_of(row + i * chunk, 16), chunk)
        there = pl.ds(pl.multiple_of(i * chunk, 16), chunk)
        dst[here, :] = (dst[here, :].astype(F32) + src[there, :].astype(F32)).astype(BF16)
        return 0

    lax.fori_loop(0, rows // chunk, body, 0)


class Reduce:
    (X1_OUT, X1_IN, Y1_OUT, Y1_IN, X2_OUT, X2_IN, Y2_OUT, Y2_IN, X3_OUT, X3_IN, Y3_OUT, Y3_IN) = range(12)
    KINDS = 12
    S_OUT, S_IN = range(2)
    Z_UP, Z_UP_IN, Z_DOWN, Z_DOWN_IN, FETCH = range(5)
    GX_OUT, GX_IN, GY_OUT, GY_IN, FX_OUT, FX_IN, FY_OUT, FY_IN, LOCAL = range(9)
    LAST_KINDS = 9

    def __init__(self, place, wide, z_parts, out, zin_far, refs):
        self.p, self.wide, self.out = place, wide and place.square, out
        self.part, self.x1, self.y1, self.x2, self.y2, zin, self.stage = refs[:7]
        self.core_sems, self.sems, self.z_sems, self.last_sems = refs[7:]
        self.zin = zin if self.wide else zin_far
        self.total = self.part.shape[1]
        self.quarter = self.total // 4
        self.cut = first_half(self.quarter)
        self.z_parts = 1 if self.wide else z_parts

    @staticmethod
    def scratch(square, wide, planes, rows, cols, core_parts, z_parts):
        wide = wide and square
        pieces = planes if wide else 1
        cut = first_half(rows // 4)
        one = (pieces, cut, cols) if square else (1, 16, 128)
        two = (pieces, rows // 4 - cut, cols) if square else (1, 16, 128)
        large = (pieces, rows // 4, cols) if square else (1, 16, 128)
        return [
            pltpu.VMEM((planes, rows, cols), BF16),
            pltpu.VMEM(one, BF16),
            pltpu.VMEM(two, BF16),
            pltpu.VMEM(large, BF16),
            pltpu.VMEM(large, BF16),
            pltpu.VMEM((planes + 1, rows // 4, cols) if wide else (1, 16, 128), BF16),
            pltpu.VMEM((16, 128) if wide else (rows // z_parts, cols), BF16),
            pltpu.SemaphoreType.DMA((2, planes, core_parts)),
            pltpu.SemaphoreType.DMA((Reduce.KINDS, pieces)),
            pltpu.SemaphoreType.DMA((5, planes + 1, z_parts)),
            pltpu.SemaphoreType.DMA((Reduce.LAST_KINDS,)),
        ]

    @staticmethod
    def far(square, wide, planes, rows, cols):
        shape = (1, 16, 128) if wide and square else (planes + 1, rows, cols)
        return jax.ShapeDtypeStruct(shape, BF16)

    def at(self, owner, half=None):
        return quarter_rows(owner, self.quarter, half)

    def sem(self, kind, k):
        return self.sems.at[kind, k]

    def core_copy(self, zz, src, row, rows, k):
        block = self.part.at[zz, pl.ds(row, rows)]
        return self.p.copy(
            block if src is None else src,
            block,
            self.core_sems.at[self.S_OUT, zz, k],
            self.core_sems.at[self.S_IN, zz, k],
            self.p.sib,
        )

    def slot(self, zz):
        return zz if self.wide else 0

    def hop(self, zz, rows, dst, out, into, device):
        return self.p.copy(
            self.part.at[zz, rows],
            dst,
            self.sem(out, self.slot(zz)),
            self.sem(into, self.slot(zz)),
            device,
        )

    def plane_1(self, zz):
        p, k, h = self.p, self.slot(zz), self.cut
        lo, hi = pl.ds(0, h), pl.ds(h, self.quarter - h)
        p.send(lambda: self.hop(zz, self.at(p.bd, 0), self.x1.at[k], self.X1_OUT, self.X1_IN, p.x))
        p.send(lambda: self.hop(zz, self.at(p.bd, 1), self.y1.at[k], self.Y1_OUT, self.Y1_IN, p.y))
        p.send(lambda: self.hop(zz, self.at(p.bx, 0), self.x2.at[k, lo], self.X2_OUT, self.X2_IN, p.x))
        p.send(lambda: self.hop(zz, self.at(p.by, 1), self.y2.at[k, hi], self.Y2_OUT, self.Y2_IN, p.y))

    def plane_2(self, zz):
        p, k, h = self.p, self.slot(zz), self.cut
        lo, hi = pl.ds(0, h), pl.ds(h, self.quarter - h)
        self.hop(zz, self.at(p.bd, 0), self.x1.at[k], self.X1_OUT, self.X1_IN, p.x).wait_recv()
        add_into(self.part.at[zz], self.x1.at[k], p.by * self.quarter, h)
        p.send(lambda: self.hop(zz, self.at(p.by, 0), self.y2.at[k, lo], self.Y3_OUT, self.Y3_IN, p.y))
        self.hop(zz, self.at(p.bd, 1), self.y1.at[k], self.Y1_OUT, self.Y1_IN, p.y).wait_recv()
        add_into(self.part.at[zz], self.y1.at[k], p.bx * self.quarter + h, self.quarter - h)
        p.send(lambda: self.hop(zz, self.at(p.bx, 1), self.x2.at[k, hi], self.X3_OUT, self.X3_IN, p.x))

    def plane_3(self, zz):
        p, k, h = self.p, self.slot(zz), self.cut
        lo, hi = pl.ds(0, h), pl.ds(h, self.quarter - h)
        self.hop(zz, self.at(p.bx, 0), self.x2.at[k, lo], self.X2_OUT, self.X2_IN, p.x).wait_recv()
        self.hop(zz, self.at(p.by, 1), self.y2.at[k, hi], self.Y2_OUT, self.Y2_IN, p.y).wait_recv()
        self.hop(zz, self.at(p.bx, 1), self.x2.at[k, hi], self.X3_OUT, self.X3_IN, p.x).wait_recv()
        add_into(self.part.at[zz], self.x2.at[k], p.b * self.quarter, self.quarter)
        self.hop(zz, self.at(p.by, 0), self.y2.at[k, lo], self.Y3_OUT, self.Y3_IN, p.y).wait_recv()
        add_into(self.part.at[zz], self.y2.at[k], p.b * self.quarter, self.quarter)

    def z_rows(self, k):
        p = self.p
        rows = self.total // self.z_parts
        return (p.b * self.quarter, self.quarter) if self.wide else (k * rows, rows)

    def z_slot(self, zz, upward, k):
        slot = zz + 1 if upward else zz
        if self.wide:
            return self.zin.at[slot]
        row, rows = self.z_rows(k)
        return self.zin.at[slot, pl.ds(row, rows)]

    def z_hop(self, zz, upward, k):
        p = self.p
        row, rows = self.z_rows(k)
        here = pl.ds(pl.multiple_of(row, 16), rows)
        out, into = (self.Z_UP, self.Z_UP_IN) if upward else (self.Z_DOWN, self.Z_DOWN_IN)
        return p.copy(
            self.part.at[zz, here],
            self.z_slot(zz, upward, k),
            self.z_sems.at[out, zz, k],
            self.z_sems.at[into, zz, k],
            p.up if upward else p.down,
        )

    def z_take(self, zz, upward, k):
        self.z_hop(zz, upward, k).wait_recv()
        row, rows = self.z_rows(k)
        src = self.z_slot(zz, upward, k)
        if not self.wide:
            slot = zz + 1 if upward else zz
            fetch = pltpu.make_async_copy(src, self.stage, self.z_sems.at[self.FETCH, slot, k])
            fetch.start()
            fetch.wait()
            src = self.stage
        add_into(self.part.at[zz], src, row, rows)

    def z_step(self, zz, d, k):
        p = self.p
        for upward, at in ((True, zz - d), (False, zz + d)):
            if not 0 <= at < p.planes:
                continue

            @pl.when(p.z == at)
            def _(upward=upward, at=at):
                if at != (0 if upward else p.planes - 1):
                    self.z_take(zz, upward, k)
                self.z_hop(zz, upward, k).start()

            p.sent.append((p.z == at, functools.partial(self.z_hop, zz, upward, k)))

    def z_last(self, zz, k):
        @pl.when(self.p.z == zz)
        def _():
            if zz > 0:
                self.z_take(zz, True, k)
            if zz < self.p.planes - 1:
                self.z_take(zz, False, k)

    def z_plan(self, steps, r, zz):
        for k in range(self.z_parts):
            for d in range(max(zz, self.p.planes - 1 - zz), 0, -1):
                steps.add(("z", r, zz, d, k), self.z_step, zz, d, k)
            steps.add(("zl", r, zz, k), self.z_last, zz, k)

    def plane_plan(self, steps, r, zz):
        if self.p.square:
            steps.add(("p2", r, zz), self.plane_2, zz)
            steps.add(("p3", r, zz), self.plane_3, zz)

    def late_plan(self, steps, r):
        if self.p.square:
            for n, step in enumerate((self.plane_1, self.plane_2, self.plane_3)):
                steps.add(("p%d" % (n + 1), r, -1), step, self.p.z)

    def spread_plan(self, steps, r):
        for n, step in enumerate((self.spread_1, self.spread_2, self.spread_3)):
            steps.add(("s%d" % (n + 1), r), step)

    def last_hop(self, src, rows, out, into, device):
        return self.p.copy(
            src, self.out.at[rows], self.last_sems.at[out], self.last_sems.at[into], device
        )

    def spread_1(self):
        p = self.p
        if not p.square:
            pltpu.make_async_copy(self.part.at[p.z], self.out, self.last_sems.at[self.LOCAL]).start()
            return
        rows = self.at(p.b)
        src = self.part.at[p.z, rows]
        p.send(lambda: self.last_hop(src, rows, self.GX_OUT, self.GX_IN, p.x))
        p.send(lambda: self.last_hop(src, rows, self.GY_OUT, self.GY_IN, p.y))
        pltpu.make_async_copy(src, self.out.at[rows], self.last_sems.at[self.LOCAL]).start()

    def spread_2(self):
        p = self.p
        if not p.square:
            return
        from_x, from_y = self.at(p.bx), self.at(p.by)
        half_x, half_y = self.at(p.bx, 0), self.at(p.by, 1)
        self.last_hop(self.out.at[from_x], from_x, self.GX_OUT, self.GX_IN, p.x).wait_recv()
        p.send(lambda: self.last_hop(self.out.at[half_x], half_x, self.FY_OUT, self.FY_IN, p.y))
        self.last_hop(self.out.at[from_y], from_y, self.GY_OUT, self.GY_IN, p.y).wait_recv()
        p.send(lambda: self.last_hop(self.out.at[half_y], half_y, self.FX_OUT, self.FX_IN, p.x))

    def spread_3(self):
        p = self.p
        if not p.square:
            pltpu.make_async_copy(self.part.at[p.z], self.out, self.last_sems.at[self.LOCAL]).wait()
            return
        rows = self.at(p.b)
        half_0, half_1 = self.at(p.bd, 0), self.at(p.bd, 1)
        self.last_hop(self.out.at[half_0], half_0, self.FY_OUT, self.FY_IN, p.y).wait_recv()
        self.last_hop(self.out.at[half_1], half_1, self.FX_OUT, self.FX_IN, p.x).wait_recv()
        pltpu.make_async_copy(
            self.part.at[p.z, rows], self.out.at[rows], self.last_sems.at[self.LOCAL]
        ).wait()


FORWARD_STEPS = {
    0: (('z', 0, 1), ('x', 0, 1),),
    1: (('start', 1), ('z', 0, 2), ('x', 0, 2), ('z', 1, 1), ('start', 2),),
    3: (('p', 0, 1), ('z', 0, 3), ('x', 0, 3), ('p', 0, 2), ('x', 1, 1), ('start', 3), ('g', 0, 1), ('z', 1, 2), ('x', 1, 2),),
    4: (('p', 0, 3), ('z', 2, 1), ('x', 2, 1),),
    5: (('g', 0, 2), ('z', 3, 1),),
    6: (('z', 1, 3),),
    7: (('g', 0, 3), ('p', 1, 2), ('x', 1, 3),),
    10: (('z', 2, 2), ('p', 1, 1), ('x', 2, 2), ('c', 0, 0), ('c', 0, 1),),
    12: (('p', 1, 3), ('c', 1, 0),),
    13: (('c', 1, 1),),
    14: (('c', 0, 2), ('g', 1, 2), ('g', 1, 1), ('p', 2, 1),),
    15: (('g', 1, 3), ('z', 2, 3), ('c', 1, 2), ('x', 2, 3),),
    16: (('c', 0, 3), ('z', 3, 2), ('p', 2, 2),),
    17: (('c', 1, 3),),
    21: (('g', 2, 1),),
    22: (('p', 2, 3),),
    23: (('x', 3, 1),),
    24: (('g', 2, 2), ('z', 3, 3), ('x', 3, 3),),
    25: (('g', 2, 3), ('x', 3, 2),),
    28: (('p', 3, 1),),
    29: (('p', 3, 3),),
    30: (('p', 3, 2),),
    31: (('g', 3, 1),),
    32: (('g', 3, 3),),
    33: (('g', 3, 2),),
}
BACKWARD_STEPS = {
    0: (('z', 0, 3, 3, 0), ('z', 0, 0, 3, 0),),
    7: (('z', 0, 1, 2, 0),),
    8: (('z', 0, 2, 2, 0),),
    10: (('z', 0, 0, 2, 0), ('z', 0, 3, 2, 0),),
    11: (('p2', 1, 0),),
    16: (('z', 0, 2, 1, 0), ('z', 0, 1, 1, 0),),
    17: (('z', 0, 3, 1, 0), ('z', 0, 0, 1, 0),),
    18: (('p2', 1, 1),),
    21: (('c', 0, 0), ('p2', 1, 3),),
    23: (('p2', 1, 2), ('p3', 1, 0), ('c', 1, 0), ('zl', 0, 1, 0),),
    24: (('zl', 0, 2, 0), ('z', 2, 3, 3, 0),),
    25: (('c', 0, 1), ('z', 2, 1, 2, 0), ('c', 1, 1),),
    26: (('z', 2, 2, 2, 0), ('zl', 0, 0, 0), ('zl', 0, 3, 0),),
    27: (('c', 0, 2), ('z', 1, 0, 3, 0), ('p1', 0, -1),),
    28: (('c', 1, 2),),
    29: (('p2', 3, 3),),
    30: (('z', 2, 0, 3, 0), ('p3', 1, 3), ('z', 1, 3, 3, 0), ('p2', 0, -1), ('z', 2, 2, 1, 0), ('c', 0, 3), ('c', 1, 3),),
    32: (('z', 1, 0, 2, 0),),
    33: (('z', 1, 3, 2, 0),),
    34: (('p3', 1, 2), ('z', 1, 2, 2, 0), ('p2', 3, 0),),
    35: (('p3', 1, 1), ('z', 1, 1, 2, 0),),
    36: (('z', 2, 0, 2, 0), ('zl', 2, 2, 0), ('p3', 3, 3), ('z', 3, 3, 3, 0),),
    37: (('z', 1, 3, 1, 0), ('z', 2, 3, 2, 0), ('z', 1, 1, 1, 0), ('z', 2, 1, 1, 0), ('z', 1, 2, 1, 0), ('p2', 3, 1), ('z', 1, 0, 1, 0), ('p3', 0, -1), ('z', 2, 0, 1, 0), ('p2', 3, 2),),
    38: (('p3', 3, 0), ('s1', 0), ('z', 3, 0, 3, 0),),
    39: (('zl', 1, 0, 0), ('p3', 3, 1), ('z', 3, 1, 2, 0), ('zl', 1, 1, 0), ('z', 2, 3, 1, 0), ('p3', 3, 2), ('z', 3, 3, 2, 0), ('zl', 1, 3, 0), ('zl', 1, 2, 0), ('s1', 1), ('z', 3, 2, 2, 0), ('z', 3, 0, 2, 0),),
    40: (('zl', 2, 1, 0), ('s2', 0), ('zl', 2, 3, 0),),
    41: (('z', 3, 1, 1, 0), ('zl', 2, 0, 0), ('z', 3, 2, 1, 0), ('z', 3, 3, 1, 0), ('z', 3, 0, 1, 0), ('p1', 2, -1), ('s2', 1),),
    42: (('p2', 2, -1), ('zl', 3, 1, 0), ('zl', 3, 3, 0),),
    43: (('zl', 3, 2, 0), ('zl', 3, 0, 0), ('s1', 3), ('p3', 2, -1), ('s1', 2), ('s3', 0), ('s2', 3), ('s2', 2), ('s3', 1), ('s3', 3), ('s3', 2),),
}


def dot(a, b):
    return jnp.dot(a, b, preferred_element_type=F32)


def dot_nt(a, b):
    return lax.dot_general(a, b, (((1,), (1,)), ((), ())), preferred_element_type=F32)


def dot_tn(a, b):
    return lax.dot_general(a, b, (((0,), (0,)), ((), ())), preferred_element_type=F32)


def row_loop(rows, chunk, body):
    def step(i, _):
        body(pl.ds(pl.multiple_of(i * chunk, chunk), chunk))
        return 0

    lax.fori_loop(0, rows // chunk, step, 0)


def lanes(block, width=128):
    return pl.ds(pl.multiple_of(block * width, width), width)


def tokens(i, span):
    return pl.ds(pl.multiple_of(i * span, span), span)


def transpose(src, dst):
    rows, cols = src.shape
    whole = cols // 128

    def step(j, _):
        at = lanes(j)
        dst[at, :] = src[:, at].T
        return 0

    lax.fori_loop(0, whole, step, 0)
    if cols % 128:
        dst[whole * 128 :, :] = src[:, whole * 128 :].T


def mean_square(v):
    return jnp.mean(v * v, axis=-1, keepdims=True)


def pair_masks(span):
    lane = lax.broadcasted_iota(jnp.int32, (span, 128), 1)
    first = (lane < HEAD_DIM).astype(F32)
    row = lax.broadcasted_iota(jnp.int32, (128, 128), 0)
    col = lax.broadcasted_iota(jnp.int32, (128, 128), 1)
    own = ((row < HEAD_DIM) == (col < HEAD_DIM)).astype(F32)
    return first.astype(BF16), (1.0 - first).astype(BF16), own.astype(BF16), own


def by_head(pair, first, second):
    return jnp.concatenate([pair * first, pair * second], axis=0)


def pack_state(state):
    lane = lax.broadcasted_iota(jnp.int32, (HEAD_DIM, 128), 1)
    return jnp.where(lane < HEAD_DIM, state[:HEAD_DIM], state[HEAD_DIM:])


def unpack_state(packed, own):
    return jnp.concatenate([packed, packed], axis=0) * own


def head_sums(v, own):
    return dot(v.astype(BF16), own)


def grouped(lo, hi, compute, store, size=4):
    def step(m, _):
        first = lo + m * size
        results = [compute(first + u) for u in range(size)]
        for u in range(size):
            store(first + u, results[u])
        return 0

    lax.fori_loop(0, (hi - lo) // size, step, 0)


class Chain:
    S_OUT, S_IN, Z_OUT, Z_IN, P_OUT, P_IN = range(6)
    PARTS = 2

    def __init__(self, place, forward, mine, other, before, out, sems):
        self.p, self.forward = place, forward
        self.mine, self.other, self.before, self.out, self.sems = mine, other, before, out, sems
        self.count = mine.shape[0] // self.PARTS
        self.half = self.count // 2
        if forward:
            self.prev, self.next = place.has_down, place.has_up
            self.device, self.counts = place.up, place.c == 1
        else:
            self.prev, self.next = place.has_up, place.has_down
            self.device, self.counts = place.down, place.c == 0

    @staticmethod
    def scratch(count):
        return [pltpu.VMEM((count, HEAD_DIM, 128), BF16)] * 4 + [pltpu.SemaphoreType.DMA((6, Chain.PARTS))]

    def part(self, k, core):
        return pl.ds(k * self.count + core * self.half, self.half)

    def sibling_copy(self, k):
        here = pl.ds(k * self.count, self.count)
        return self.p.copy(
            self.mine.at[here], self.other.at[here], self.sems.at[self.S_OUT, k],
            self.sems.at[self.S_IN, k], self.p.sib,
        )

    def next_copy(self, k):
        here = self.part(k, self.p.c)
        return self.p.copy(
            self.out.at[here], self.before.at[here], self.sems.at[self.Z_OUT, k],
            self.sems.at[self.Z_IN, k], self.device,
        )

    def across_copy(self, k, core):
        here = self.part(k, core)
        return self.p.copy(
            self.before.at[here], self.before.at[here], self.sems.at[self.P_OUT, k],
            self.sems.at[self.P_IN, k], self.p.sib,
        )

    def start(self, k, steps):
        self.p.send(lambda: self.sibling_copy(k))

        @pl.when(jnp.logical_not(self.prev))
        def _():
            def body(n, _):
                self.before[k * self.count + n] = jnp.zeros(self.before.shape[1:], BF16)
                return 0

            lax.fori_loop(0, self.count, body, 0)

        for h in range(self.p.planes):
            steps.add(("c", k, h), self.step, k, h)

    def step(self, k, h):
        p = self.p
        here = p.z == (h if self.forward else p.planes - 1 - h)

        @pl.when(here)
        def _():
            self.sibling_copy(k).wait_recv()
            if h > 0:
                self.next_copy(k).wait_recv()
                self.across_copy(k, p.c).start()
            if h < p.planes - 1:

                def body(i, _):
                    n = k * self.count + p.c * self.half + i
                    total = self.before[n].astype(F32) + self.mine[n].astype(F32)
                    self.out[n] = (total + self.other[n].astype(F32)).astype(BF16)
                    return 0

                lax.fori_loop(0, self.half, body, 0)
                self.next_copy(k).start()

        if h > 0:
            p.sent.append((here, lambda: self.across_copy(k, p.c)))
        if h < p.planes - 1:
            p.sent.append((here, lambda: self.next_copy(k)))

    def finish(self, k, steps, result):
        p = self.p
        steps.finish(lambda name: name[:2] == ("c", k))
        pl.when(self.prev)(lambda: self.across_copy(k, 1 - p.c).wait_recv())
        weight = self.counts.astype(F32)

        def body(i, _):
            n = k * self.count + i
            total = self.before[n].astype(F32) + self.other[n].astype(F32) * weight
            result[n] = total.astype(BF16)
            return 0

        lax.fori_loop(0, self.count, body, 0)


class Locals:
    def __init__(self, sems):
        self.sems, self.used, self.open = sems, 0, []

    def copy(self, src, dst):
        made = pltpu.make_async_copy(src, dst, self.sems.at[self.used])
        self.used += 1
        made.start()
        return made

    def save(self, src, dst):
        self.open.append(self.copy(src, dst))

    def finish(self):
        for made in self.open:
            made.wait()


def load_columns(local, full, rows, dst, stage):
    seq, _, cols = full.shape
    if cols % 128 == 0:
        return [local.copy(full.at[s, rows], dst.at[:, pl.ds(s * cols, cols)]) for s in range(seq)]
    for s in range(seq):
        local.copy(full.at[s, rows], stage.at[pl.ds(0, rows.size)]).wait()
        dst[:, s * cols : (s + 1) * cols] = stage[: rows.size]
    return []


def load_plane(local, full, rows, zz, dst, stage):
    cols = full.shape[2]
    if cols % 128 == 0:
        return [
            local.copy(full.at[2 * zz + core, rows], dst.at[:, pl.ds(core * cols, cols)])
            for core in range(2)
        ]
    for core in range(2):
        local.copy(full.at[2 * zz + core, rows], stage.at[core, pl.ds(0, rows.size)]).wait()
    dst[...] = jnp.concatenate([stage[0, 0 : rows.size], stage[1, 0 : rows.size]], axis=1)
    return []


def stream(order, source, slots, sems, body, after):
    def fetch(n):
        return pltpu.make_async_copy(source(order[n]), slots.at[n % 2], sems.at[n % 2])

    fetch(0).start()
    for n, s in enumerate(order):
        if n + 1 < len(order):
            fetch(n + 1).start()
        fetch(n).wait()
        body(s, n % 2)
        after()


def forward_kernel(batch, seq, spans, *refs):
    (x_hbm, in_hbm, out_w_hbm, gain_hbm, pair_hbm, down_hbm), refs = refs[:6], refs[6:]
    fulls, refs = refs[:4], refs[4:]
    out_hbm, saved, refs = refs[0], refs[1:13], refs[13:]
    (q_out, k_out, v_out, raw_out, att_out, e_out, gated_out, mid_out, nb_out, pair_out, hid_out, na_out) = saved
    (x, na, tmp, qkvr, att, gated, mid, nb, w_in, w_out, gain, w_pair, tmp_g, tmp_u, pair, hid,
     w_down, res, stage, gain_own, na_t, gated_t, hid_t, mine, other, before, chain_out, early, chain_sems, slot_sems, pair_sems,
     local_sems, gather_sems, gather_local, *held) = refs
    place = Place(batch, seq)
    local = Locals(local_sems)
    load_in = local.copy(in_hbm, held[0])
    load_x = local.copy(x_hbm, x)
    load_gain = local.copy(gain_hbm, gain_own)
    load_out = local.copy(out_w_hbm, held[1].at[pl.ds(0, D)])
    load_pair = local.copy(pair_hbm, held[2])
    load_down = local.copy(down_hbm, held[3])
    gather = Gather(place, held, fulls, (True, True, True, True), gather_sems, gather_local)
    place.barrier()
    rows, span = x.shape[0], spans
    per_group = seq // 4
    blocks = rows // span
    pairs = D // 128
    cols_in = w_in.shape[-1]
    half = seq // 2
    planes = place.planes
    cols_two = 2 * fulls[1].shape[2]
    q, k, v, raw = (qkvr.at[n] for n in range(4))
    first, second, own, own_f = pair_masks(span)
    steps = Steps(FORWARD_STEPS if place.square and place.planes == 4 else {})
    plan_gather(steps, gather, 4)

    def have(w, n):
        steps.finish(lambda name: not steps.table and name[0] != "c" and name[1] <= w)
        return gather.have(w, n)

    load_in.wait()
    steps.run(("start", 0))
    steps.tick()
    load_x.wait()

    def norm_rows(r):
        xr = x[r, :].astype(F32)
        na[r, :] = (xr * lax.rsqrt(mean_square(xr) + 1e-6)).astype(BF16)

    row_loop(rows, 64, norm_rows)
    load_gain.wait()
    load_out.wait()
    top = lax.broadcasted_iota(jnp.int32, (GAIN_ROWS, gain_own.shape[1]), 0) == 0
    held[1][D : D + GAIN_ROWS, :] = jnp.where(top, gain_own[...].astype(F32), 0.0).astype(BF16)
    load_pair.wait()
    load_down.wait()
    steps.tick()

    def project(s, slot):
        group, n = lax.div(s, per_group), lax.rem(s, per_group)
        tmp[...] = dot(na[...], w_in[slot])
        at = pl.ds(pl.multiple_of(n * cols_in, 128), cols_in)

        @pl.when(s < 2 * per_group)
        def _():
            def finish_rows(r):
                value = tmp[r, :]
                value = jnp.maximum(value, 0.0) + jnp.log1p(jnp.exp(-jnp.abs(value)))
                qkvr[group, r, at] = value.astype(BF16)

            row_loop(rows, 64, finish_rows)

        @pl.when(s >= 2 * per_group)
        def _():
            def finish_rows(r):
                qkvr[group, r, at] = tmp[r, :].astype(BF16)

            row_loop(rows, 64, finish_rows)

    for n in range(planes):
        zz = have(0, n)
        blocks_in = [
            pltpu.make_async_copy(fulls[0].at[2 * zz + c], w_in.at[c], slot_sems.at[c]) for c in range(2)
        ]
        for made in blocks_in:
            made.start()
        for c, made in enumerate(blocks_in):
            made.wait()
            project(2 * zz + c, c)
            steps.tick()

    def state(n):
        i, j = lax.div(n, pairs), lax.rem(n, pairs)
        at, block = tokens(i, span), lanes(j)
        return pack_state(dot_tn(k[at, block], v[at, block])).astype(BF16)

    def keep_state(n, value):
        mine[n] = value

    chain = Chain(place, True, mine, other, before, chain_out, chain_sems)
    for part in range(Chain.PARTS):
        grouped(part * chain.count, (part + 1) * chain.count, state, keep_state)
        chain.start(part, steps)
        steps.tick()
    for src, dst in ((q, q_out), (k, k_out), (v, v_out), (raw, raw_out)):
        local.save(src, dst)

    row = lax.rem(lax.broadcasted_iota(jnp.int32, (2 * span, span), 0), span)
    col = lax.broadcasted_iota(jnp.int32, (2 * span, span), 1)
    lane = lax.broadcasted_iota(jnp.int32, (span, 128), 1)

    def inner(n):
        i, j = lax.div(n, pairs), lax.rem(n, pairs)
        at, block = tokens(i, span), lanes(j)
        scores = dot_nt(by_head(q[at, block], first, second), k[at, block])
        scores = jnp.where(row >= col, scores, 0.0).astype(BF16)
        both = dot(scores, v[at, block])
        return jnp.where(lane < HEAD_DIM, both[:span], both[span:])

    def keep_inner(n, value):
        att[tokens(lax.div(n, pairs), span), lanes(lax.rem(n, pairs))] = value

    for i in range(blocks):
        grouped(i * pairs, (i + 1) * pairs, inner, keep_inner)
        steps.tick()

    transpose(na, na_t)
    local.save(na_t, na_out)
    steps.tick()
    chain.finish(0, steps, early)
    loads = []
    for n in range(planes):
        zz = have(1, n)
        to = pl.ds(pl.multiple_of(zz * cols_two, 128), cols_two)
        loads += load_plane(local, fulls[1], pl.ds(0, D), zz, w_out.at[:, to], stage)
        loads += load_plane(local, fulls[1], pl.ds(D, 16), zz, gain.at[:, to], stage)
    for made in loads:
        made.wait()
    steps.tick()

    def outer(n):
        i, j = lax.div(n, pairs), lax.rem(n, pairs)
        at, block = tokens(i, span), lanes(j)
        a = att[at, block] + dot(q[at, block], unpack_state(early[n], own))
        unit = a * lax.rsqrt(head_sums(a * a, own) * (1.0 / HEAD_DIM) + 1e-5)
        normed = unit * gain[0:1, block].astype(F32)
        return a, (jax.nn.sigmoid(raw[at, block].astype(F32)) * normed).astype(BF16)

    def keep_outer(n, value):
        at, block = tokens(lax.div(n, pairs), span), lanes(lax.rem(n, pairs))
        att[at, block], gated[at, block] = value

    for i in range(blocks):
        if i == blocks // 2:
            chain.finish(1, steps, early)
        grouped(i * pairs, (i + 1) * pairs, outer, keep_outer)
        steps.tick()
    local.save(early, e_out)
    local.save(att, att_out)

    def turn(src, dst, blocks_of):
        for block in blocks_of:
            at = slice(block * 128, min((block + 1) * 128, src.shape[1]))
            dst[at, :] = src[:, at].T

    for n in range(D // 512):
        at = pl.ds(n * 512, 512)
        mid[:, at] = x[:, at].astype(F32) + dot(gated[...], w_out[:, at])
        turn(gated, gated_t, range(n * 4, n * 4 + 4))
        steps.tick()
    local.save(gated_t, gated_out)

    def norm_mid(r):
        m = mid[r, :]
        nb[r, :] = (m * lax.rsqrt(mean_square(m) + 1e-6)).astype(BF16)

    row_loop(rows, 64, norm_mid)
    local.save(mid, mid_out)
    local.save(nb, nb_out)
    steps.tick()

    def fetch_pair(j, slot):
        return [
            pltpu.make_async_copy(
                fulls[2].at[j + side * half], w_pair.at[slot, side], pair_sems.at[slot, side]
            )
            for side in range(2)
        ]

    early_half = planes == 4
    away = jnp.where(place.z < 2, 0, 2) if early_half else 0
    for n in range(planes - 1 if early_half else planes):
        have(2, n)
    for made in fetch_pair(away, 0):
        made.start()
    count_t = -(-hid.shape[-1] // 128)

    def finish_pair(n, part):
        j, slot = lax.rem(n + away, half), n % 2
        for row in range(part * rows // 2, (part + 1) * rows // 2, 64):
            r = slice(row, row + 64)
            gate, up = tmp_g[slot, r, :], tmp_u[slot, r, :]
            pair[j, r, :] = gate.astype(BF16)
            pair[j + half, r, :] = up.astype(BF16)
            hid[j, r, :] = (gate * up).astype(BF16)

    def save_pair(n):
        j = lax.rem(n + away, half)
        local.save(pair.at[j], pair_out.at[j])
        local.save(pair.at[j + half], pair_out.at[j + half])

    def turn_hid(n):
        j = lax.rem(n + away, half)
        turn(hid.at[j], hid_t.at[j], range(count_t))
        local.save(hid_t.at[j], hid_out.at[j])

    for n in range(half):
        j, slot = lax.rem(n + away, half), n % 2
        if early_half and n == 1:
            have(2, planes - 1)
        if n + 1 < half:
            for made in fetch_pair(lax.rem(n + 1 + away, half), 1 - slot):
                made.start()
        for made in fetch_pair(j, slot):
            made.wait()
        tmp_g[slot] = dot_nt(nb[...], w_pair[slot, 0])
        if n > 0:
            finish_pair(n - 1, 0)
        steps.tick()
        tmp_u[slot] = dot_nt(nb[...], w_pair[slot, 1])
        if n > 0:
            finish_pair(n - 1, 1)
            save_pair(n - 1)
        if n > 1:
            turn_hid(n - 2)
        steps.tick()
    finish_pair(half - 1, 0)
    finish_pair(half - 1, 1)
    save_pair(half - 1)
    steps.tick()

    width = hid.shape[-1]

    def down(zz, slot):
        at = pl.ds(pl.multiple_of(zz * cols_two, 128), cols_two)
        total = mid[:, at]
        for j in range(half):
            total = total + dot(hid[j], w_down[slot, j * width : (j + 1) * width, :])
        res[:, at] = total.astype(BF16)

    later = [half - 2, half - 1]
    before_it = None
    for n in range(planes):
        zz = have(3, n)
        loads = load_plane(local, fulls[3], pl.ds(0, FF), zz, w_down.at[n % 2], stage)
        if before_it is not None:
            down(*before_it)
            if later:
                turn_hid(later.pop(0))
            steps.tick()
        for made in loads:
            made.wait()
        before_it = (zz, n % 2)
    down(*before_it)
    local.save(res, out_hbm)
    steps.tick()
    steps.finish()
    local.finish()
    place.finish()


def forward(batch, seq, x, span, shards):
    attn_in, attn_out, out_gain, glu_in, glu_out = shards
    shards = (attn_in, jax.ShapeDtypeStruct((D + GAIN_ROWS, attn_out.shape[1]), BF16), glu_in.T, glu_out)
    rows = x.shape[0]
    cols_in, cols_pair = shards[0].shape[1], shards[2].shape[0]
    half = seq // 2
    states = (rows // span) * (D // 128)
    big = jax.ShapeDtypeStruct((rows, D), BF16)
    big_f = jax.ShapeDtypeStruct((rows, D), F32)
    narrow = shards[3].shape[1] % 128 != 0
    any_space = pl.BlockSpec(memory_space=pl.ANY)
    out_shape = [jax.ShapeDtypeStruct((seq, *a.shape), a.dtype) for a in shards]
    out_shape += [big, big, big, big, big, big_f]
    turned = jax.ShapeDtypeStruct((D, rows), BF16)
    out_shape += [jax.ShapeDtypeStruct((states, HEAD_DIM, 128), BF16), turned, big_f, big]
    out_shape += [
        jax.ShapeDtypeStruct((seq, rows, cols_pair), BF16),
        jax.ShapeDtypeStruct((half, cols_pair, rows), BF16),
        turned,
    ]
    wide, wide_f = pltpu.VMEM((rows, D), BF16), pltpu.VMEM((rows, D), F32)
    pair_f = pltpu.VMEM((2, rows, cols_pair), F32)
    scratch = [
        wide, wide, pltpu.VMEM((rows, cols_in), F32), pltpu.VMEM((4, rows, D), BF16), wide_f, wide, wide_f, wide,
        pltpu.VMEM((2, D, cols_in), BF16),
        pltpu.VMEM((D, D), BF16),
        pltpu.VMEM((16, D), BF16),
        pltpu.VMEM((2, 2, cols_pair, D), BF16),
        pair_f, pair_f,
        pltpu.VMEM((seq, rows, cols_pair), BF16),
        pltpu.VMEM((half, rows, cols_pair), BF16),
        pltpu.VMEM((2, FF, 2 * shards[3].shape[1]), BF16),
        wide,
        pltpu.VMEM((2, FF, shards[3].shape[1]) if narrow else (2, 16, 128), BF16),
        pltpu.VMEM((1, attn_out.shape[1]), BF16),
        *[pltpu.VMEM((D, rows), BF16)] * 2,
        pltpu.VMEM((half, cols_pair, rows), BF16),
        *[pltpu.VMEM((states, HEAD_DIM, 128), BF16)] * 5,
        pltpu.SemaphoreType.DMA((6, Chain.PARTS)),
        pltpu.SemaphoreType.DMA((2,)),
        pltpu.SemaphoreType.DMA((2, 2)),
        pltpu.SemaphoreType.DMA((128,)),
        pltpu.SemaphoreType.DMA((Gather.KINDS, 4, half)),
        pltpu.SemaphoreType.DMA((4,)),
        *[pltpu.VMEM(a.shape, a.dtype) for a in shards],
    ]
    return pl.pallas_call(
        functools.partial(forward_kernel, batch, seq, span),
        out_shape=out_shape,
        in_specs=[any_space] * 6,
        out_specs=[any_space] * len(out_shape),
        scratch_shapes=scratch,
        compiler_params=pltpu.CompilerParams(
            collective_id=0, has_side_effects=True, vmem_limit_bytes=62 * 1024 * 1024
        ),
        name="forward",
    )(x, attn_in, attn_out, out_gain.reshape(1, -1), glu_in.T, glu_out)


WIDE = (False, True, False, True)
Z_PARTS = (1, 4, 1, 4)


def z_parts(w, rows):
    return max(k for k in range(1, Z_PARTS[w] + 1) if rows % (16 * k) == 0)


def slope(plus):
    series = plus * (1.0 - plus * (0.5 - plus * (1.0 / 6.0)))
    return jnp.where(plus < 0.02, series, 1.0 - jnp.exp(-plus))


def backward_kernel(batch, seq, span, *refs):
    g_hbm, x_hbm, *fulls = refs[:6]
    (q_in, k_in, v_in, raw_in, att_in, e_in, gated_in, mid_in, nb_in, pair_in, hid_in, na_in) = refs[6:18]
    grad_hbm, sums, gm_hbm, far = refs[18], refs[19:23], refs[23], refs[24:28]
    refs = list(refs[28:])
    place = Place(batch, seq)
    reds = []
    for w in range(4):
        reds.append(Reduce(place, WIDE[w], z_parts(w, sums[w].shape[0]), sums[w], far[w], refs[:11]))
        refs = refs[11:]
    (tall, turned, pair, fields, f0, f1, g, split, low, down, slots, wide_out, in_out, slim_out, gain, gain_sums, gain_split,
     early, mine, other, before, chain_out, stage, chain_sems, slot_sems, local_sems) = refs
    red_down, red_pair, red_out, red_in = reds
    local = Locals(local_sems)
    rows = g.shape[0]
    half = seq // 2
    planes = half
    width = hid_in.shape[1]
    cols_in, cols_out, cols_pair = fulls[0].shape[2], fulls[1].shape[2], fulls[2].shape[1]
    per_group, per_block = seq // 4, cols_in // 128
    blocks, pairs = rows // span, D // 128
    first, second, own, own_f = pair_masks(span)
    core, sibling = place.c, 1 - place.c
    steps = Steps(BACKWARD_STEPS if place.square and place.planes == 4 else {})

    load_g = local.copy(g_hbm, g)
    load_hid = [local.copy(hid_in.at[j], tall.at[pl.ds(j * width, width)]) for j in range(half)]
    load_nb = local.copy(nb_in, low)
    load_gated = local.copy(gated_in, turned)
    load_pair = [local.copy(pair_in.at[s], pair.at[s]) for s in range(seq)]
    load_e = local.copy(e_in, early)
    place.barrier()

    def split_columns(src):
        for s in range(seq):
            to = (s % 2) * (D // 2) + (s // 2) * cols_out
            split[:, to : to + cols_out] = src[:, s * cols_out : (s + 1) * cols_out]

    def by_core(which):
        return pl.ds(pl.multiple_of(which * (D // 2), D // 2), D // 2)

    slim_sent = []

    def slim_send(red, row, count, k, fill):
        slot = len(slim_sent) % 2
        if len(slim_sent) >= 2:
            for made in slim_sent[-2]:
                made().wait_send()
        fill(slot)
        sent = []
        for zz in range(planes):
            src = slim_out.at[slot, zz, pl.ds(0, count)]
            sent.append(functools.partial(red.core_copy, zz, src, row, count, k))
            sent[-1]().start()
        slim_sent.append(sent)

    def slim_theirs(red, lhs, at, row, count, k):
        def fill(slot):
            value = dot(lhs[at : at + count, :], split[:, by_core(sibling)])
            for zz in range(planes):
                slim_out[slot, zz, 0:count, :] = value[:, zz * cols_out : (zz + 1) * cols_out].astype(BF16)

        slim_send(red, row, count, k, fill)

    def slim_mine(red, lhs, at, row, count, k):
        value = dot(lhs[at : at + count, :], split[:, by_core(core)])
        for zz in range(planes):
            red.core_copy(zz, None, row, count, k).wait_recv()
            here = red.part[zz, row : row + count, :].astype(F32)
            here = here + value[:, zz * cols_out : (zz + 1) * cols_out]
            red.part[zz, row : row + count, :] = here.astype(BF16)

    wide_sent = []

    def pair_block(s, row):
        r = slice(row, min(row + 256, cols_pair))
        return r, dot_tn(pair[s, :, r], low[...])

    def in_block(s, row):
        r = slice(row, row + 256)
        return r, dot(turned[r, :], pair[s, :, 0:cols_in])

    def wide_theirs(red, block, out, zz):
        slot = len(wide_sent) % 2
        if len(wide_sent) >= 2:
            wide_sent[-2]().wait_send()
        for row in range(0, red.total, 256):
            r, value = block(2 * zz + sibling, row)
            out[slot, r, :] = value.astype(BF16)
        wide_sent.append(functools.partial(red.core_copy, zz, out.at[slot], 0, red.total, 0))
        wide_sent[-1]().start()
        steps.tick()

    def wide_mine(red, r, block, zz):
        red.core_copy(zz, None, 0, red.total, 0).wait_recv()
        for row in range(0, red.total, 256):
            at, value = block(2 * zz + core, row)
            red.part[zz, at, :] = (red.part[zz, at, :].astype(F32) + value).astype(BF16)
        if red.wide:
            red.plane_1(zz)
        red.plane_plan(steps, r, zz)
        red.z_plan(steps, r, zz)
        steps.tick()

    load_g.wait()
    split_columns(g)
    for made in load_hid:
        made.wait()
    for j in range(half):
        slim_theirs(red_down, tall, j * width, j * width, width, j)
    for j in range(half):
        slim_mine(red_down, tall, j * width, j * width, width, j)
    for zz in range(planes):
        red_down.z_plan(steps, 0, zz)
    red_down.late_plan(steps, 0)
    red_down.spread_plan(steps, 0)
    steps.tick()

    def load_down(j):
        at = pl.ds((j % 2) * width, width)
        return load_columns(local, fulls[3], pl.ds(j * width, width), down.at[at], stage)

    for made in load_pair:
        made.wait()
    waits = load_down(0)
    grads = (f0, f1)

    def finish_pair(j):
        for row in range(0, rows, 64):
            r = slice(row, row + 64)
            grad = grads[j % 2][r, 0:width]
            gate, up = pair[j, r, :].astype(F32), pair[j + half, r, :].astype(F32)
            pair[j, r, :] = (grad * up).astype(BF16)
            pair[j + half, r, :] = (grad * gate).astype(BF16)

    for j in range(half):
        after = load_down(j + 1) if j + 1 < half else []
        for made in waits:
            made.wait()
        waits = after
        at = (j % 2) * width
        grads[j % 2][:, 0:width] = dot_nt(g[...], down[at : at + width, :])
        if j > 0:
            finish_pair(j - 1)
        steps.tick()
    finish_pair(half - 1)
    load_mid = local.copy(mid_in, f1)

    load_nb.wait()
    wide_theirs(red_pair, pair_block, wide_out, 0)
    for zz in range(planes):
        if zz + 1 < planes:
            wide_theirs(red_pair, pair_block, wide_out, zz + 1)
        wide_mine(red_pair, 1, pair_block, zz)
    red_pair.spread_plan(steps, 1)
    w_out = down.at[pl.ds(0, D)]
    load_out = load_columns(local, fulls[1], pl.ds(0, D), w_out, stage)
    load_out += load_columns(local, fulls[1], pl.ds(D, 16), gain, stage)
    views = []
    for k, src in enumerate((q_in, k_in, v_in, raw_in)):
        for side in range(2):
            to = tall.at[pl.ds((2 * k + side) * rows, rows)]
            views.append(local.copy(src.at[:, pl.ds(side * (D // 2), D // 2)], to))

    for made in wide_sent[-2:]:
        made().wait_send()
    wide_sent.clear()
    places = (slots.at[0], slots.at[1], wide_out.at[0], wide_out.at[1])

    def fetch_pair(n):
        return [
            pltpu.make_async_copy(fulls[2].at[s], places[s % 4], slot_sems.at[s % 4])
            for s in (2 * n, 2 * n + 1)
        ]

    for made in fetch_pair(0):
        made.start()
    for n in range(half):
        if n + 1 < half:
            for made in fetch_pair(n + 1):
                made.start()
        for made in fetch_pair(n):
            made.wait()
        value = sum(dot(pair[s], places[s % 4][...]) for s in (2 * n, 2 * n + 1))
        f0[...] = value if n == 0 else f0[...] + value
        steps.tick()
    load_mid.wait()

    def back_mid(r):
        m, grad = f1[r, :], f0[r, :]
        scale = lax.rsqrt(mean_square(m) + 1e-6)
        inner = jnp.mean(grad * m, axis=-1, keepdims=True)
        total = g[r, :].astype(F32) + scale * grad - m * (scale * scale * scale) * inner
        f1[r, :] = total
        low[r, :] = total.astype(BF16)

    row_loop(rows, 64, back_mid)
    save_gm = local.copy(f1, gm_hbm)
    split_columns(low)
    steps.tick()

    load_gated.wait()
    for k in range(2):
        slim_theirs(red_out, turned, k * (D // 2), k * (D // 2), D // 2, k)
    for made in load_out:
        made.wait()
    for n in range(D // 512):
        at = pl.ds(n * 512, 512)
        f0[:, at] = dot_nt(low[...], w_out[at, :])
    for k in range(2):
        slim_mine(red_out, turned, k * (D // 2), k * (D // 2), D // 2, k)
    load_na = local.copy(na_in, turned)
    load_x = local.copy(x_hbm, low)
    save_gm.wait()
    load_att = local.copy(att_in, f1)
    gain_sums[...] = jnp.zeros_like(gain_sums)
    for made in views:
        made.wait()
    load_e.wait()
    load_att.wait()
    steps.tick()

    def view(k, i, j):
        row = pl.multiple_of((2 * k + lax.div(j, pairs // 2)) * rows + i * span, span)
        return pl.ds(row, span), lanes(lax.rem(j, pairs // 2))

    def put(group, i, j, value):
        s = group * per_group + lax.div(j, per_block)
        pair[s, tokens(i, span), lanes(lax.rem(j, per_block))] = value

    def place_of(n):
        return lax.div(n, pairs), lax.rem(n, pairs)

    def back_gate(n):
        i, j = place_of(n)
        at, block = tokens(i, span), lanes(j)
        a, grad = f1[at, block], f0[at, block]
        scale = lax.rsqrt(head_sums(a * a, own) * (1.0 / HEAD_DIM) + 1e-5)
        unit = a * scale
        gains = gain[0:1, block].astype(F32)
        sig = jax.nn.sigmoid(tall[view(3, i, j)].astype(F32))
        grad_normed = grad * sig
        grad_gate = (grad * (unit * gains) * sig * (1.0 - sig)).astype(BF16)
        gain_sum = jnp.sum(grad_normed * unit, axis=0, keepdims=True)
        grad_unit = grad_normed * gains
        inner = head_sums(grad_unit * a, own) * (1.0 / HEAD_DIM)
        grad_a = (scale * grad_unit - a * (scale * scale * scale) * inner).astype(BF16)
        state = pack_state(dot_tn(tall[view(0, i, j)], grad_a)).astype(BF16)
        return grad_gate, gain_sum, grad_a, state

    def keep_gate(n, value):
        i, j = place_of(n)
        put(3, i, j, value[0])
        gain_sums[0:1, lanes(j)] += value[1]
        g[tokens(i, span), lanes(j)] = value[2]
        mine[n] = value[3]

    chain = Chain(place, False, mine, other, before, chain_out, chain_sems)
    for i in range(blocks):
        grouped(i * pairs, (i + 1) * pairs, back_gate, keep_gate)
        if (i + 1) % (blocks // Chain.PARTS) == 0:
            chain.start(i // (blocks // Chain.PARTS), steps)
        steps.tick()

    for s in range(seq):
        to = (s // 2) * cols_out
        gain_split[s % 2, :, to : to + cols_out] = gain_sums[:, s * cols_out : (s + 1) * cols_out]
    top = lax.broadcasted_iota(jnp.int32, (GAIN_ROWS, cols_out), 0) == 0

    def gain_rows(which, zz):
        row = gain_split[which, 0:1, zz * cols_out : (zz + 1) * cols_out]
        return jnp.where(top, row, 0.0)

    def fill_gain(slot):
        for zz in range(planes):
            slim_out[slot, zz, 0:GAIN_ROWS, :] = gain_rows(sibling, zz).astype(BF16)

    slim_send(red_out, D, GAIN_ROWS, 2, fill_gain)
    load_na.wait()
    ready = [zz for zz in range(planes) if zz * 2 >= 3 * per_group]
    for zz in ready:
        wide_theirs(red_in, in_block, in_out, zz)
    for zz in range(planes):
        red_out.core_copy(zz, None, D, GAIN_ROWS, 2).wait_recv()
        here = red_out.part[zz, D : D + GAIN_ROWS, :].astype(F32) + gain_rows(core, zz)
        red_out.part[zz, D : D + GAIN_ROWS, :] = here.astype(BF16)
    for zz in range(planes):
        red_out.z_plan(steps, 2, zz)
    red_out.late_plan(steps, 2)
    red_out.spread_plan(steps, 2)
    steps.tick()
    for zz in ready:
        wide_mine(red_in, 3, in_block, zz)

    t_of = lax.rem(lax.broadcasted_iota(jnp.int32, (span, 2 * span), 1), span)
    s_of = lax.broadcasted_iota(jnp.int32, (span, 2 * span), 0)
    t_down = lax.rem(lax.broadcasted_iota(jnp.int32, (2 * span, span), 0), span)
    s_down = lax.broadcasted_iota(jnp.int32, (2 * span, span), 1)
    lane = lax.broadcasted_iota(jnp.int32, (span, 128), 1)

    def back_attention(n):
        i, j = place_of(n)
        qs, ks, vs = (tall[view(k, i, j)] for k in range(3))
        grads = g[tokens(i, span), lanes(j)]
        q2, g2 = by_head(qs, first, second), by_head(grads, first, second)
        scores = jnp.where(t_of >= s_of, dot_nt(ks, q2), 0.0).astype(BF16)
        grad_t = jnp.where(t_of >= s_of, dot_nt(vs, g2), 0.0).astype(BF16)
        grad_s = jnp.where(t_down >= s_down, dot_nt(g2, vs), 0.0).astype(BF16)
        both = dot(grad_s, ks)
        grad_q = jnp.where(lane < HEAD_DIM, both[:span], both[span:])
        grad_q = grad_q + dot_nt(grads, unpack_state(early[n], own))
        return dot(grad_t, q2), dot(scores, g2), (grad_q * slope(qs.astype(F32))).astype(BF16)

    def keep_attention(n, value):
        i, j = place_of(n)
        at, block = tokens(i, span), lanes(j)
        f0[at, block], f1[at, block] = value[:2]
        put(0, i, j, value[2])

    for i in range(blocks):
        grouped(i * pairs, (i + 1) * pairs, back_attention, keep_attention, 2)
        steps.tick()
    ready_q = [zz for zz in range(planes) if (zz + 1) * 2 <= per_group]
    for zz in ready_q:
        wide_theirs(red_in, in_block, in_out, zz)
    for zz in ready_q:
        wide_mine(red_in, 3, in_block, zz)

    def back_states(n):
        i, j = place_of(n)
        at, block = tokens(i, span), lanes(j)
        ks, vs = tall[view(1, i, j)], tall[view(2, i, j)]
        later = unpack_state(other[n], own)
        grad_k = (f0[at, block] + dot_nt(vs, later)) * slope(ks.astype(F32))
        return grad_k.astype(BF16), (f1[at, block] + dot(ks, later)).astype(BF16)

    def keep_states(n, value):
        put(1, *place_of(n), value[0])
        put(2, *place_of(n), value[1])

    for part in range(Chain.PARTS):
        chain.finish(part, steps, other)
        grouped(part * chain.count, (part + 1) * chain.count, back_states, keep_states)
        steps.tick()
    load_gm = local.copy(gm_hbm, f1)
    rest = [zz for zz in range(planes) if zz not in ready and zz not in ready_q]
    for n, zz in enumerate(rest):
        if n >= 2:
            wide_mine(red_in, 3, in_block, rest[n - 2])
        wide_theirs(red_in, in_block, in_out, zz)
    for zz in rest[-2:]:
        wide_mine(red_in, 3, in_block, zz)
    red_in.spread_plan(steps, 3)

    for made in wide_sent[-2:]:
        made().wait_send()
    wide_sent.clear()
    places_in = [in_out.at[k] for k in range(2)]
    places_in += [down.at[pl.ds(0, D), pl.ds(k * (D // 2), cols_in)] for k in range(2)]

    def fetch_in(n):
        return [
            pltpu.make_async_copy(fulls[0].at[s], places_in[s % 4], slot_sems.at[s % 4])
            for s in (2 * n, 2 * n + 1)
        ]

    for made in fetch_in(0):
        made.start()
    for n in range(half):
        if n + 1 < half:
            for made in fetch_in(n + 1):
                made.start()
        for made in fetch_in(n):
            made.wait()
        value = sum(dot_nt(pair[s, :, 0:cols_in], places_in[s % 4][...]) for s in (2 * n, 2 * n + 1))
        f0[...] = value if n == 0 else f0[...] + value
        steps.tick()
    load_gm.wait()
    load_x.wait()

    def back_x(r):
        x, grad = low[r, :].astype(F32), f0[r, :]
        scale = lax.rsqrt(mean_square(x) + 1e-6)
        inner = jnp.mean(grad * x, axis=-1, keepdims=True)
        f1[r, :] += scale * grad - x * (scale * scale * scale) * inner

    row_loop(rows, 64, back_x)
    local.save(f1, grad_hbm)
    steps.tick()
    steps.finish()
    local.finish()
    for sent in slim_sent[-2:]:
        for made in sent:
            made().wait_send()
    for made in wide_sent[-2:]:
        made().wait_send()
    place.finish()


def backward(batch, seq, span, grad, x, fulls, saved):
    rows = x.shape[0]
    half = seq // 2
    cols_in, cols_out, cols_pair = fulls[0].shape[2], fulls[1].shape[2], fulls[2].shape[1]
    width = saved[10].shape[1]
    square = batch == 4
    shapes = ((FF, cols_out), (cols_pair, D), (D + GAIN_ROWS, cols_out), (D, cols_in))
    states = (rows // span) * (D // 128)
    any_space = pl.BlockSpec(memory_space=pl.ANY)
    big_f = jax.ShapeDtypeStruct((rows, D), F32)
    out_shape = [big_f] + [jax.ShapeDtypeStruct(shape, BF16) for shape in shapes] + [big_f]
    out_shape += [Reduce.far(square, WIDE[w], half, *shapes[w]) for w in range(4)]
    scratch = []
    core_parts = (half, 1, 3, 1)
    for w in range(4):
        scratch += Reduce.scratch(square, WIDE[w], half, *shapes[w], core_parts[w], z_parts(w, shapes[w][0]))
    narrow = cols_out % 128 != 0
    state = pltpu.VMEM((states, HEAD_DIM, 128), BF16)
    scratch += [
        pltpu.VMEM((max(FF, 8 * rows), D // 2), BF16),
        pltpu.VMEM((D, rows), BF16),
        pltpu.VMEM((seq, rows, cols_pair), BF16),
        pltpu.VMEM((16, 128), BF16),
        pltpu.VMEM((rows, D), F32),
        pltpu.VMEM((rows, D), F32),
        pltpu.VMEM((rows, D), BF16),
        pltpu.VMEM((rows, D), BF16),
        pltpu.VMEM((rows, D), BF16),
        pltpu.VMEM((max(2 * width, D), D), BF16),
        pltpu.VMEM((2, cols_pair, D), BF16),
        pltpu.VMEM((2, cols_pair, D), BF16),
        pltpu.VMEM((2, D, cols_in), BF16),
        pltpu.VMEM((2, half, max(width, D // 2), cols_out), BF16),
        pltpu.VMEM((16, D), BF16),
        pltpu.VMEM((8, D), F32),
        pltpu.VMEM((2, 8, D // 2), F32),
        state, state, state, state, state,
        pltpu.VMEM((D, cols_out) if narrow else (16, 128), BF16),
        pltpu.SemaphoreType.DMA((6, Chain.PARTS)),
        pltpu.SemaphoreType.DMA((4,)),
        pltpu.SemaphoreType.DMA((192,)),
    ]
    return pl.pallas_call(
        functools.partial(backward_kernel, batch, seq, span),
        out_shape=out_shape,
        in_specs=[any_space] * 18,
        out_specs=[any_space] * len(out_shape),
        scratch_shapes=scratch,
        compiler_params=pltpu.CompilerParams(
            collective_id=1, has_side_effects=True, vmem_limit_bytes=63 * 1024 * 1024
        ),
        name="backward",
    )(grad, x, *fulls, *saved)


def local(block_in, attn_in, attn_out, out_gain, glu_in, glu_out, block_grad):
    seq_count, span = block_in.shape[:2]
    rows = seq_count * span
    batch, seq = lax.axis_size("batch"), lax.axis_size("seq")
    x = block_in.reshape(rows, D)
    parts = forward(batch, seq, x, span, (attn_in, attn_out, out_gain, glu_in, glu_out))
    fulls, block_out, saved = parts[:4], parts[4], parts[5:]
    grads = backward(batch, seq, span, block_grad.reshape(rows, D), x, fulls, saved)
    input_grad, sums = grads[0], list(grads[1:5])
    if batch != 4:
        sums = [lax.psum(a, "batch") for a in sums]
    block_out, input_grad, down, pair, out, gain, into = finish(block_out, input_grad, sums)
    return (
        block_out.reshape(block_in.shape),
        input_grad.reshape(block_in.shape),
        into,
        out,
        gain.reshape(-1),
        pair.T,
        down,
    )


def finish_kernel(*refs):
    ins, outs, refs = refs[:6], refs[6:13], refs[13:]
    held, wide, (gain, load_sems, save_sems) = refs[:6], refs[6:10], refs[10:]
    loads = [pltpu.make_async_copy(src, dst, load_sems.at[k]) for k, (src, dst) in enumerate(zip(ins, held))]
    order = (3, 5, 2, 4, 1, 0)
    for k in order:
        loads[k].start()
    saves = []

    def save(src, dst):
        saves.append(pltpu.make_async_copy(src, dst, save_sems.at[len(saves)]))
        saves[-1].start()

    for k in order[:4]:
        loads[k].wait()
        src, dst = held[k], wide[k - 2]

        def widen(r, src=src, dst=dst):
            dst[r, :] = src[r, :].astype(F32)

        row_loop(src.shape[0], 64 if src.shape[0] % 64 == 0 else 32, widen)
        if k == 4:
            save(dst.at[pl.ds(0, D)], outs[4])
            gain[...] = dst[D : D + 1, :]
            save(gain, outs[5])
        else:
            save(dst, outs[k] if k < 4 else outs[6])
    for k in order[4:]:
        loads[k].wait()
        save(held[k], outs[k])
    for made in saves:
        made.wait()


def finish(block_out, input_grad, sums):
    ins = [block_out, input_grad, *sums]
    any_space = pl.BlockSpec(memory_space=pl.ANY)
    shapes = [a.shape for a in sums]
    cols = shapes[2][1]
    out_shape = [jax.ShapeDtypeStruct(a.shape, a.dtype) for a in (block_out, input_grad)]
    out_shape += [
        jax.ShapeDtypeStruct(s, F32) for s in (shapes[0], shapes[1], (D, cols), (1, cols), shapes[3])
    ]
    outs = pl.pallas_call(
        finish_kernel,
        out_shape=out_shape,
        in_specs=[any_space] * 6,
        out_specs=[any_space] * 7,
        scratch_shapes=[
            *[pltpu.VMEM(a.shape, a.dtype) for a in ins],
            *[pltpu.VMEM(s, F32) for s in shapes],
            pltpu.VMEM((1, cols), F32),
            pltpu.SemaphoreType.DMA((6,)),
            pltpu.SemaphoreType.DMA((7,)),
        ],
        compiler_params=pltpu.CompilerParams(vmem_limit_bytes=63 * 1024 * 1024),
        name="finish",
    )(*ins)
    return outs


def solution(mesh):
    rows, columns = P("batch", "seq", None), P(None, "seq")
    return jax.shard_map(
        local,
        mesh=mesh,
        in_specs=(rows, columns, columns, P("seq"), columns, columns, rows),
        out_specs=(rows, rows, columns, columns, P("seq"), columns, columns),
        check_vma=False,
    )
```

```python
import functools

import jax
import jax.numpy as jnp
from jax import lax
from jax.experimental import pallas as pl
from jax.experimental.pallas import tpu as pltpu
from jax.sharding import PartitionSpec as P

HEADS = 16
HEAD_DIM = 64
D = 1024
FF = 2816
MESH = pl.DeviceIdType.MESH
BF16 = jnp.bfloat16
F32 = jnp.float32
GAIN_ROWS = 128


def run_if(cond, fn):
    if cond is None:
        fn()
    else:
        pl.when(cond)(fn)


class Place:
    def __init__(self, batch, seq):
        self.planes = seq // 2
        self.square = batch == 4
        self.b = lax.axis_index("batch")
        self.s = lax.axis_index("seq")
        self.z = lax.div(self.s, 2)
        self.c = lax.rem(self.s, 2)
        self.bx = self.b + 1 - 2 * lax.rem(self.b, 2)
        self.by = lax.rem(self.b + 2, 4)
        self.bd = lax.rem(self.bx + 2, 4)
        self.sib = (self.b, self.s + 1 - 2 * self.c)
        self.up = (self.b, self.s + 2)
        self.down = (self.b, self.s - 2)
        self.x = (self.bx, self.s)
        self.y = (self.by, self.s)
        self.has_up = self.z < self.planes - 1
        self.has_down = self.z > 0
        self.sent = []

    def barrier(self):
        sem = pltpu.get_barrier_semaphore()
        always = [self.sib] + ([self.x, self.y] if self.square else [])
        for device in always:
            pl.semaphore_signal(sem, inc=1, device_id=device, device_id_type=MESH)
        for cond, device in ((self.has_up, self.up), (self.has_down, self.down)):
            pl.when(cond)(
                lambda device=device: pl.semaphore_signal(
                    sem, inc=1, device_id=device, device_id_type=MESH
                )
            )
        ends = self.has_up.astype(jnp.int32) + self.has_down.astype(jnp.int32)
        pl.semaphore_wait(sem, len(always) + ends)

    def copy(self, src, dst, send_sem, recv_sem, device):
        return pltpu.make_async_remote_copy(
            src_ref=src,
            dst_ref=dst,
            send_sem=send_sem,
            recv_sem=recv_sem,
            device_id=device,
            device_id_type=MESH,
        )

    def send(self, make, cond=None):
        run_if(cond, lambda: make().start())
        self.sent.append((cond, make))

    def finish(self):
        for cond, make in self.sent:
            run_if(cond, lambda make=make: make().wait_send())
        self.sent = []


def first_half(quarter):
    return -(-quarter // 32) * 16


def quarter_rows(owner, quarter, half=None):
    if half is None:
        return pl.ds(pl.multiple_of(owner * quarter, 16), quarter)
    cut = first_half(quarter)
    start, rows = ((0, cut), (cut, quarter - cut))[half]
    return pl.ds(pl.multiple_of(owner * quarter + start, 16), rows)


class Gather:
    Z_UP, Z_DOWN, Z_IN, X_OUT, X_IN, Y_OUT, Y_IN, FX_OUT, FX_IN, FY_OUT, FY_IN = range(11)
    S_OUT, S_IN = 11, 15
    KINDS = 19

    def __init__(self, place, held, fulls, quartered, sems, local_sems):
        self.p, self.held, self.fulls, self.sems = place, held, fulls, sems
        self.local_sems = local_sems
        self.quartered = [q and place.square for q in quartered]

    def rows(self, w, owner, half=None):
        rows = self.held[w].shape[0]
        if not self.quartered[w]:
            return pl.ds(0, rows)
        return quarter_rows(owner, rows // 4, half)

    def move(self, w, zz, rows, out, into, device, core=None):
        core = self.p.c if core is None else core
        block = self.fulls[w].at[2 * zz + core, rows]
        return self.p.copy(
            block, block, self.sems.at[out, w, zz], self.sems.at[into, w, zz], device
        )

    def across(self, w, zz, piece, core=None):
        p = self.p
        rows = self.rows(w, (p.b, p.bx, p.by, p.bd)[piece])
        return self.move(w, zz, rows, self.S_OUT + piece, self.S_IN + piece, p.sib, core)

    def whole(self, w):
        p = self.p
        here = self.fulls[w].at[p.s]
        return p.copy(
            self.held[w], here, self.sems.at[self.S_OUT, w, p.z], self.sems.at[self.S_IN, w, p.z], p.sib
        )

    def start(self, w):
        p, own = self.p, self.held[w]
        here = self.fulls[w].at[p.s]
        rows = self.rows(w, p.b)
        for cond, device, out in (
            (p.has_up, p.up, self.Z_UP),
            (p.has_down, p.down, self.Z_DOWN),
        ):
            p.send(
                lambda device=device, out=out: p.copy(
                    own.at[rows],
                    here.at[rows],
                    self.sems.at[out, w, p.z],
                    self.sems.at[self.Z_IN, w, p.z],
                    device,
                ),
                cond,
            )
        p.send(lambda: self.whole(w))
        pltpu.make_async_copy(own, here, self.local_sems.at[w]).start()

    def sides(self, d):
        p = self.p
        return (
            (p.z >= d, p.z - d, p.has_up, p.up, self.Z_UP),
            (p.z + d < p.planes, p.z + d, p.has_down, p.down, self.Z_DOWN),
        )

    def from_z(self, w, d):
        p = self.p
        rows = self.rows(w, p.b)
        for cond, zz, more, device, out in self.sides(d):
            run_if(
                cond, lambda zz=zz: self.move(w, zz, rows, self.Z_UP, self.Z_IN, p.up).wait_recv()
            )
            p.send(
                lambda zz=zz, device=device, out=out: self.move(
                    w, zz, rows, out, self.Z_IN, device
                ),
                jnp.logical_and(cond, more),
            )
            p.send(lambda zz=zz: self.across(w, zz, 0), cond)

    def to_plane(self, w, d):
        p = self.p
        rows = self.rows(w, p.b)
        for cond, zz, *_ in self.sides(d):
            p.send(lambda zz=zz: self.move(w, zz, rows, self.X_OUT, self.X_IN, p.x), cond)
            p.send(lambda zz=zz: self.move(w, zz, rows, self.Y_OUT, self.Y_IN, p.y), cond)

    def from_plane(self, w, d):
        p = self.p
        from_x, from_y = self.rows(w, p.bx), self.rows(w, p.by)
        half_x, half_y = self.rows(w, p.bx, 0), self.rows(w, p.by, 1)
        for cond, zz, *_ in self.sides(d):
            run_if(
                cond, lambda zz=zz: self.move(w, zz, from_x, self.X_OUT, self.X_IN, p.x).wait_recv()
            )
            p.send(lambda zz=zz: self.move(w, zz, half_x, self.FY_OUT, self.FY_IN, p.y), cond)
            run_if(
                cond, lambda zz=zz: self.move(w, zz, from_y, self.Y_OUT, self.Y_IN, p.y).wait_recv()
            )
            p.send(lambda zz=zz: self.move(w, zz, half_y, self.FX_OUT, self.FX_IN, p.x), cond)
            p.send(lambda zz=zz: self.across(w, zz, 1), cond)
            p.send(lambda zz=zz: self.across(w, zz, 2), cond)

    def from_diagonal(self, w, d):
        p = self.p
        half_0, half_1 = self.rows(w, p.bd, 0), self.rows(w, p.bd, 1)
        for cond, zz, *_ in self.sides(d):
            run_if(
                cond,
                lambda zz=zz: self.move(w, zz, half_0, self.FY_OUT, self.FY_IN, p.y).wait_recv(),
            )
            run_if(
                cond,
                lambda zz=zz: self.move(w, zz, half_1, self.FX_OUT, self.FX_IN, p.x).wait_recv(),
            )
            p.send(lambda zz=zz: self.across(w, zz, 3), cond)

    def nearest(self, k):
        planes = self.p.planes
        found = jnp.int32(0)
        for z in range(planes):
            order = sorted(range(planes), key=lambda t: (abs(t - z), t))
            found = jnp.where(self.p.z == z, order[k], found)
        return found

    def have(self, w, k):
        p = self.p
        if k == 0:
            pltpu.make_async_copy(
                self.held[w], self.fulls[w].at[p.s], self.local_sems.at[w]
            ).wait()
            self.whole(w).wait_recv()
            return p.z
        zz = self.nearest(k)
        for piece in range(4 if self.quartered[w] else 1):
            self.across(w, zz, piece, 1 - p.c).wait_recv()
        return zz


class Steps:
    def __init__(self, table):
        self.table, self.todo, self.ticks = table, {}, 0

    def add(self, name, fn, *args):
        self.todo[name] = functools.partial(fn, *args)

    def run(self, name):
        step = self.todo.pop(name, None)
        if step is not None:
            step()

    def tick(self):
        for name in self.table.get(self.ticks, ()):
            self.run(name)
        self.ticks += 1

    def finish(self, wanted=lambda name: True):
        for name in [name for name in self.todo if wanted(name)]:
            self.run(name)


def plan_gather(steps, g, count):
    far = g.p.planes - 1
    for w in range(count):
        steps.add(("start", w), g.start, w)
        for d in range(1, far + 1):
            steps.add(("z", w, d), g.from_z, w, d)
        if g.quartered[w]:
            for name, step in (("x", g.to_plane), ("p", g.from_plane), ("g", g.from_diagonal)):
                for d in range(1, far + 1):
                    steps.add((name, w, d), step, w, d)


def add_into(dst, src, row, rows):
    cols = dst.shape[-1]
    chunk = max(
        k for k in range(16, rows + 1, 16) if rows % k == 0 and (k * cols <= 49152 or k == 16)
    )

    def body(i, _):
        here = pl.ds(pl.multiple_of(row + i * chunk, 16), chunk)
        there = pl.ds(pl.multiple_of(i * chunk, 16), chunk)
        dst[here, :] = (dst[here, :].astype(F32) + src[there, :].astype(F32)).astype(BF16)
        return 0

    lax.fori_loop(0, rows // chunk, body, 0)


class Reduce:
    (X1_OUT, X1_IN, Y1_OUT, Y1_IN, X2_OUT, X2_IN, Y2_OUT, Y2_IN, X3_OUT, X3_IN, Y3_OUT, Y3_IN) = range(12)
    KINDS = 12
    S_OUT, S_IN = range(2)
    Z_UP, Z_UP_IN, Z_DOWN, Z_DOWN_IN, FETCH = range(5)
    GX_OUT, GX_IN, GY_OUT, GY_IN, FX_OUT, FX_IN, FY_OUT, FY_IN, LOCAL = range(9)
    LAST_KINDS = 9

    def __init__(self, place, wide, z_parts, out, zin_far, refs):
        self.p, self.wide, self.out = place, wide and place.square, out
        self.part, self.x1, self.y1, self.x2, self.y2, zin, self.stage = refs[:7]
        self.core_sems, self.sems, self.z_sems, self.last_sems = refs[7:]
        self.zin = zin if self.wide else zin_far
        self.total = self.part.shape[1]
        self.quarter = self.total // 4
        self.cut = first_half(self.quarter)
        self.z_parts = 1 if self.wide else z_parts

    @staticmethod
    def scratch(square, wide, planes, rows, cols, core_parts, z_parts):
        wide = wide and square
        pieces = planes if wide else 1
        cut = first_half(rows // 4)
        one = (pieces, cut, cols) if square else (1, 16, 128)
        two = (pieces, rows // 4 - cut, cols) if square else (1, 16, 128)
        large = (pieces, rows // 4, cols) if square else (1, 16, 128)
        return [
            pltpu.VMEM((planes, rows, cols), BF16),
            pltpu.VMEM(one, BF16),
            pltpu.VMEM(two, BF16),
            pltpu.VMEM(large, BF16),
            pltpu.VMEM(large, BF16),
            pltpu.VMEM((planes + 1, rows // 4, cols) if wide else (1, 16, 128), BF16),
            pltpu.VMEM((16, 128) if wide else (rows // z_parts, cols), BF16),
            pltpu.SemaphoreType.DMA((2, planes, core_parts)),
            pltpu.SemaphoreType.DMA((Reduce.KINDS, pieces)),
            pltpu.SemaphoreType.DMA((5, planes + 1, z_parts)),
            pltpu.SemaphoreType.DMA((Reduce.LAST_KINDS,)),
        ]

    @staticmethod
    def far(square, wide, planes, rows, cols):
        shape = (1, 16, 128) if wide and square else (planes + 1, rows, cols)
        return jax.ShapeDtypeStruct(shape, BF16)

    def at(self, owner, half=None):
        return quarter_rows(owner, self.quarter, half)

    def sem(self, kind, k):
        return self.sems.at[kind, k]

    def core_copy(self, zz, src, row, rows, k):
        block = self.part.at[zz, pl.ds(row, rows)]
        return self.p.copy(
            block if src is None else src,
            block,
            self.core_sems.at[self.S_OUT, zz, k],
            self.core_sems.at[self.S_IN, zz, k],
            self.p.sib,
        )

    def slot(self, zz):
        return zz if self.wide else 0

    def hop(self, zz, rows, dst, out, into, device):
        return self.p.copy(
            self.part.at[zz, rows],
            dst,
            self.sem(out, self.slot(zz)),
            self.sem(into, self.slot(zz)),
            device,
        )

    def plane_1(self, zz):
        p, k, h = self.p, self.slot(zz), self.cut
        lo, hi = pl.ds(0, h), pl.ds(h, self.quarter - h)
        p.send(lambda: self.hop(zz, self.at(p.bd, 0), self.x1.at[k], self.X1_OUT, self.X1_IN, p.x))
        p.send(lambda: self.hop(zz, self.at(p.bd, 1), self.y1.at[k], self.Y1_OUT, self.Y1_IN, p.y))
        p.send(lambda: self.hop(zz, self.at(p.bx, 0), self.x2.at[k, lo], self.X2_OUT, self.X2_IN, p.x))
        p.send(lambda: self.hop(zz, self.at(p.by, 1), self.y2.at[k, hi], self.Y2_OUT, self.Y2_IN, p.y))

    def plane_2(self, zz):
        p, k, h = self.p, self.slot(zz), self.cut
        lo, hi = pl.ds(0, h), pl.ds(h, self.quarter - h)
        self.hop(zz, self.at(p.bd, 0), self.x1.at[k], self.X1_OUT, self.X1_IN, p.x).wait_recv()
        add_into(self.part.at[zz], self.x1.at[k], p.by * self.quarter, h)
        p.send(lambda: self.hop(zz, self.at(p.by, 0), self.y2.at[k, lo], self.Y3_OUT, self.Y3_IN, p.y))
        self.hop(zz, self.at(p.bd, 1), self.y1.at[k], self.Y1_OUT, self.Y1_IN, p.y).wait_recv()
        add_into(self.part.at[zz], self.y1.at[k], p.bx * self.quarter + h, self.quarter - h)
        p.send(lambda: self.hop(zz, self.at(p.bx, 1), self.x2.at[k, hi], self.X3_OUT, self.X3_IN, p.x))

    def plane_3(self, zz):
        p, k, h = self.p, self.slot(zz), self.cut
        lo, hi = pl.ds(0, h), pl.ds(h, self.quarter - h)
        self.hop(zz, self.at(p.bx, 0), self.x2.at[k, lo], self.X2_OUT, self.X2_IN, p.x).wait_recv()
        self.hop(zz, self.at(p.by, 1), self.y2.at[k, hi], self.Y2_OUT, self.Y2_IN, p.y).wait_recv()
        self.hop(zz, self.at(p.bx, 1), self.x2.at[k, hi], self.X3_OUT, self.X3_IN, p.x).wait_recv()
        add_into(self.part.at[zz], self.x2.at[k], p.b * self.quarter, self.quarter)
        self.hop(zz, self.at(p.by, 0), self.y2.at[k, lo], self.Y3_OUT, self.Y3_IN, p.y).wait_recv()
        add_into(self.part.at[zz], self.y2.at[k], p.b * self.quarter, self.quarter)

    def z_rows(self, k):
        p = self.p
        rows = self.total // self.z_parts
        return (p.b * self.quarter, self.quarter) if self.wide else (k * rows, rows)

    def z_slot(self, zz, upward, k):
        slot = zz + 1 if upward else zz
        if self.wide:
            return self.zin.at[slot]
        row, rows = self.z_rows(k)
        return self.zin.at[slot, pl.ds(row, rows)]

    def z_hop(self, zz, upward, k):
        p = self.p
        row, rows = self.z_rows(k)
        here = pl.ds(pl.multiple_of(row, 16), rows)
        out, into = (self.Z_UP, self.Z_UP_IN) if upward else (self.Z_DOWN, self.Z_DOWN_IN)
        return p.copy(
            self.part.at[zz, here],
            self.z_slot(zz, upward, k),
            self.z_sems.at[out, zz, k],
            self.z_sems.at[into, zz, k],
            p.up if upward else p.down,
        )

    def z_take(self, zz, upward, k):
        self.z_hop(zz, upward, k).wait_recv()
        row, rows = self.z_rows(k)
        src = self.z_slot(zz, upward, k)
        if not self.wide:
            slot = zz + 1 if upward else zz
            fetch = pltpu.make_async_copy(src, self.stage, self.z_sems.at[self.FETCH, slot, k])
            fetch.start()
            fetch.wait()
            src = self.stage
        add_into(self.part.at[zz], src, row, rows)

    def z_step(self, zz, d, k):
        p = self.p
        for upward, at in ((True, zz - d), (False, zz + d)):
            if not 0 <= at < p.planes:
                continue

            @pl.when(p.z == at)
            def _(upward=upward, at=at):
                if at != (0 if upward else p.planes - 1):
                    self.z_take(zz, upward, k)
                self.z_hop(zz, upward, k).start()

            p.sent.append((p.z == at, functools.partial(self.z_hop, zz, upward, k)))

    def z_last(self, zz, k):
        @pl.when(self.p.z == zz)
        def _():
            if zz > 0:
                self.z_take(zz, True, k)
            if zz < self.p.planes - 1:
                self.z_take(zz, False, k)

    def z_plan(self, steps, r, zz):
        for k in range(self.z_parts):
            for d in range(max(zz, self.p.planes - 1 - zz), 0, -1):
                steps.add(("z", r, zz, d, k), self.z_step, zz, d, k)
            steps.add(("zl", r, zz, k), self.z_last, zz, k)

    def plane_plan(self, steps, r, zz):
        if self.p.square:
            steps.add(("p2", r, zz), self.plane_2, zz)
            steps.add(("p3", r, zz), self.plane_3, zz)

    def late_plan(self, steps, r):
        if self.p.square:
            for n, step in enumerate((self.plane_1, self.plane_2, self.plane_3)):
                steps.add(("p%d" % (n + 1), r, -1), step, self.p.z)

    def spread_plan(self, steps, r):
        for n, step in enumerate((self.spread_1, self.spread_2, self.spread_3)):
            steps.add(("s%d" % (n + 1), r), step)

    def last_hop(self, src, rows, out, into, device):
        return self.p.copy(
            src, self.out.at[rows], self.last_sems.at[out], self.last_sems.at[into], device
        )

    def spread_1(self):
        p = self.p
        if not p.square:
            pltpu.make_async_copy(self.part.at[p.z], self.out, self.last_sems.at[self.LOCAL]).start()
            return
        rows = self.at(p.b)
        src = self.part.at[p.z, rows]
        p.send(lambda: self.last_hop(src, rows, self.GX_OUT, self.GX_IN, p.x))
        p.send(lambda: self.last_hop(src, rows, self.GY_OUT, self.GY_IN, p.y))
        pltpu.make_async_copy(src, self.out.at[rows], self.last_sems.at[self.LOCAL]).start()

    def spread_2(self):
        p = self.p
        if not p.square:
            return
        from_x, from_y = self.at(p.bx), self.at(p.by)
        half_x, half_y = self.at(p.bx, 0), self.at(p.by, 1)
        self.last_hop(self.out.at[from_x], from_x, self.GX_OUT, self.GX_IN, p.x).wait_recv()
        p.send(lambda: self.last_hop(self.out.at[half_x], half_x, self.FY_OUT, self.FY_IN, p.y))
        self.last_hop(self.out.at[from_y], from_y, self.GY_OUT, self.GY_IN, p.y).wait_recv()
        p.send(lambda: self.last_hop(self.out.at[half_y], half_y, self.FX_OUT, self.FX_IN, p.x))

    def spread_3(self):
        p = self.p
        if not p.square:
            pltpu.make_async_copy(self.part.at[p.z], self.out, self.last_sems.at[self.LOCAL]).wait()
            return
        rows = self.at(p.b)
        half_0, half_1 = self.at(p.bd, 0), self.at(p.bd, 1)
        self.last_hop(self.out.at[half_0], half_0, self.FY_OUT, self.FY_IN, p.y).wait_recv()
        self.last_hop(self.out.at[half_1], half_1, self.FX_OUT, self.FX_IN, p.x).wait_recv()
        pltpu.make_async_copy(
            self.part.at[p.z, rows], self.out.at[rows], self.last_sems.at[self.LOCAL]
        ).wait()


FORWARD_STEPS = {
    0: (('z', 0, 1), ('x', 0, 1),),
    1: (('start', 1), ('z', 0, 2), ('x', 0, 2), ('z', 1, 1), ('start', 2),),
    3: (('p', 0, 1), ('z', 0, 3), ('x', 0, 3), ('p', 0, 2), ('x', 1, 1), ('start', 3), ('g', 0, 1), ('z', 1, 2), ('x', 1, 2),),
    4: (('p', 0, 3), ('z', 2, 1), ('x', 2, 1),),
    5: (('g', 0, 2), ('z', 3, 1),),
    6: (('z', 1, 3),),
    7: (('g', 0, 3), ('p', 1, 2), ('x', 1, 3),),
    10: (('z', 2, 2), ('p', 1, 1), ('x', 2, 2), ('c', 0, 0), ('c', 0, 1),),
    12: (('p', 1, 3), ('c', 1, 0),),
    13: (('c', 1, 1),),
    14: (('c', 0, 2), ('g', 1, 2), ('g', 1, 1), ('p', 2, 1),),
    15: (('g', 1, 3), ('z', 2, 3), ('c', 1, 2), ('x', 2, 3),),
    16: (('c', 0, 3), ('z', 3, 2), ('p', 2, 2),),
    17: (('c', 1, 3),),
    21: (('g', 2, 1),),
    22: (('p', 2, 3),),
    23: (('x', 3, 1),),
    24: (('g', 2, 2), ('z', 3, 3), ('x', 3, 3),),
    25: (('g', 2, 3), ('x', 3, 2),),
    28: (('p', 3, 1),),
    29: (('p', 3, 3),),
    30: (('p', 3, 2),),
    31: (('g', 3, 1),),
    32: (('g', 3, 3),),
    33: (('g', 3, 2),),
}
BACKWARD_STEPS = {
    0: (('z', 0, 3, 3, 0), ('z', 0, 0, 3, 0),),
    7: (('z', 0, 1, 2, 0),),
    8: (('z', 0, 2, 2, 0),),
    10: (('z', 0, 0, 2, 0), ('z', 0, 3, 2, 0),),
    11: (('p2', 1, 0),),
    16: (('z', 0, 2, 1, 0), ('z', 0, 1, 1, 0),),
    17: (('z', 0, 3, 1, 0), ('z', 0, 0, 1, 0),),
    18: (('p2', 1, 1),),
    21: (('c', 0, 0), ('p2', 1, 3),),
    23: (('p2', 1, 2), ('p3', 1, 0), ('c', 1, 0), ('zl', 0, 1, 0),),
    24: (('zl', 0, 2, 0), ('z', 2, 3, 3, 0),),
    25: (('c', 0, 1), ('z', 2, 1, 2, 0), ('c', 1, 1),),
    26: (('z', 2, 2, 2, 0), ('zl', 0, 0, 0), ('zl', 0, 3, 0),),
    27: (('c', 0, 2), ('z', 1, 0, 3, 0), ('p1', 0, -1),),
    28: (('c', 1, 2),),
    29: (('p2', 3, 3),),
    30: (('z', 2, 0, 3, 0), ('p3', 1, 3), ('z', 1, 3, 3, 0), ('p2', 0, -1), ('z', 2, 2, 1, 0), ('c', 0, 3), ('c', 1, 3),),
    32: (('z', 1, 0, 2, 0),),
    33: (('z', 1, 3, 2, 0),),
    34: (('p3', 1, 2), ('z', 1, 2, 2, 0), ('p2', 3, 0),),
    35: (('p3', 1, 1), ('z', 1, 1, 2, 0),),
    36: (('z', 2, 0, 2, 0), ('zl', 2, 2, 0), ('p3', 3, 3), ('z', 3, 3, 3, 0),),
    37: (('z', 1, 3, 1, 0), ('z', 2, 3, 2, 0), ('z', 1, 1, 1, 0), ('z', 2, 1, 1, 0), ('z', 1, 2, 1, 0), ('p2', 3, 1), ('z', 1, 0, 1, 0), ('p3', 0, -1), ('z', 2, 0, 1, 0), ('p2', 3, 2),),
    38: (('p3', 3, 0), ('s1', 0), ('z', 3, 0, 3, 0),),
    39: (('zl', 1, 0, 0), ('p3', 3, 1), ('z', 3, 1, 2, 0), ('zl', 1, 1, 0), ('z', 2, 3, 1, 0), ('p3', 3, 2), ('z', 3, 3, 2, 0), ('zl', 1, 3, 0), ('zl', 1, 2, 0), ('s1', 1), ('z', 3, 2, 2, 0), ('z', 3, 0, 2, 0),),
    40: (('zl', 2, 1, 0), ('s2', 0), ('zl', 2, 3, 0),),
    41: (('z', 3, 1, 1, 0), ('zl', 2, 0, 0), ('z', 3, 2, 1, 0), ('z', 3, 3, 1, 0), ('z', 3, 0, 1, 0), ('p1', 2, -1), ('s2', 1),),
    42: (('p2', 2, -1), ('zl', 3, 1, 0), ('zl', 3, 3, 0),),
    43: (('zl', 3, 2, 0), ('zl', 3, 0, 0), ('s1', 3), ('p3', 2, -1), ('s1', 2), ('s3', 0), ('s2', 3), ('s2', 2), ('s3', 1), ('s3', 3), ('s3', 2),),
}


def dot(a, b):
    return jnp.dot(a, b, preferred_element_type=F32)


def dot_nt(a, b):
    return lax.dot_general(a, b, (((1,), (1,)), ((), ())), preferred_element_type=F32)


def dot_tn(a, b):
    return lax.dot_general(a, b, (((0,), (0,)), ((), ())), preferred_element_type=F32)


def row_loop(rows, chunk, body):
    def step(i, _):
        body(pl.ds(pl.multiple_of(i * chunk, chunk), chunk))
        return 0

    lax.fori_loop(0, rows // chunk, step, 0)


def lanes(block, width=128):
    return pl.ds(pl.multiple_of(block * width, width), width)


def tokens(i, span):
    return pl.ds(pl.multiple_of(i * span, span), span)


def transpose(src, dst):
    rows, cols = src.shape
    whole = cols // 128

    def step(j, _):
        at = lanes(j)
        dst[at, :] = src[:, at].T
        return 0

    lax.fori_loop(0, whole, step, 0)
    if cols % 128:
        dst[whole * 128 :, :] = src[:, whole * 128 :].T


def mean_square(v):
    return jnp.mean(v * v, axis=-1, keepdims=True)


def pair_masks(span):
    lane = lax.broadcasted_iota(jnp.int32, (span, 128), 1)
    first = (lane < HEAD_DIM).astype(F32)
    row = lax.broadcasted_iota(jnp.int32, (128, 128), 0)
    col = lax.broadcasted_iota(jnp.int32, (128, 128), 1)
    own = ((row < HEAD_DIM) == (col < HEAD_DIM)).astype(F32)
    return first.astype(BF16), (1.0 - first).astype(BF16), own.astype(BF16), own


def by_head(pair, first, second):
    return jnp.concatenate([pair * first, pair * second], axis=0)


def pack_state(state):
    lane = lax.broadcasted_iota(jnp.int32, (HEAD_DIM, 128), 1)
    return jnp.where(lane < HEAD_DIM, state[:HEAD_DIM], state[HEAD_DIM:])


def unpack_state(packed, own):
    return jnp.concatenate([packed, packed], axis=0) * own


def head_sums(v, own):
    return dot(v.astype(BF16), own)


def grouped(lo, hi, compute, store, size=4):
    def step(m, _):
        first = lo + m * size
        results = [compute(first + u) for u in range(size)]
        for u in range(size):
            store(first + u, results[u])
        return 0

    lax.fori_loop(0, (hi - lo) // size, step, 0)


class Chain:
    S_OUT, S_IN, Z_OUT, Z_IN, P_OUT, P_IN = range(6)
    PARTS = 2

    def __init__(self, place, forward, mine, other, before, out, sems):
        self.p, self.forward = place, forward
        self.mine, self.other, self.before, self.out, self.sems = mine, other, before, out, sems
        self.count = mine.shape[0] // self.PARTS
        self.half = self.count // 2
        if forward:
            self.prev, self.next = place.has_down, place.has_up
            self.device, self.counts = place.up, place.c == 1
        else:
            self.prev, self.next = place.has_up, place.has_down
            self.device, self.counts = place.down, place.c == 0

    @staticmethod
    def scratch(count):
        return [pltpu.VMEM((count, HEAD_DIM, 128), BF16)] * 4 + [pltpu.SemaphoreType.DMA((6, Chain.PARTS))]

    def part(self, k, core):
        return pl.ds(k * self.count + core * self.half, self.half)

    def sibling_copy(self, k):
        here = pl.ds(k * self.count, self.count)
        return self.p.copy(
            self.mine.at[here], self.other.at[here], self.sems.at[self.S_OUT, k],
            self.sems.at[self.S_IN, k], self.p.sib,
        )

    def next_copy(self, k):
        here = self.part(k, self.p.c)
        return self.p.copy(
            self.out.at[here], self.before.at[here], self.sems.at[self.Z_OUT, k],
            self.sems.at[self.Z_IN, k], self.device,
        )

    def across_copy(self, k, core):
        here = self.part(k, core)
        return self.p.copy(
            self.before.at[here], self.before.at[here], self.sems.at[self.P_OUT, k],
            self.sems.at[self.P_IN, k], self.p.sib,
        )

    def start(self, k, steps):
        self.p.send(lambda: self.sibling_copy(k))

        @pl.when(jnp.logical_not(self.prev))
        def _():
            def body(n, _):
                self.before[k * self.count + n] = jnp.zeros(self.before.shape[1:], BF16)
                return 0

            lax.fori_loop(0, self.count, body, 0)

        for h in range(self.p.planes):
            steps.add(("c", k, h), self.step, k, h)

    def step(self, k, h):
        p = self.p
        here = p.z == (h if self.forward else p.planes - 1 - h)

        @pl.when(here)
        def _():
            self.sibling_copy(k).wait_recv()
            if h > 0:
                self.next_copy(k).wait_recv()
                self.across_copy(k, p.c).start()
            if h < p.planes - 1:

                def body(i, _):
                    n = k * self.count + p.c * self.half + i
                    total = self.before[n].astype(F32) + self.mine[n].astype(F32)
                    self.out[n] = (total + self.other[n].astype(F32)).astype(BF16)
                    return 0

                lax.fori_loop(0, self.half, body, 0)
                self.next_copy(k).start()

        if h > 0:
            p.sent.append((here, lambda: self.across_copy(k, p.c)))
        if h < p.planes - 1:
            p.sent.append((here, lambda: self.next_copy(k)))

    def finish(self, k, steps, result):
        p = self.p
        steps.finish(lambda name: name[:2] == ("c", k))
        pl.when(self.prev)(lambda: self.across_copy(k, 1 - p.c).wait_recv())
        weight = self.counts.astype(F32)

        def body(i, _):
            n = k * self.count + i
            total = self.before[n].astype(F32) + self.other[n].astype(F32) * weight
            result[n] = total.astype(BF16)
            return 0

        lax.fori_loop(0, self.count, body, 0)


class Locals:
    def __init__(self, sems):
        self.sems, self.used, self.open = sems, 0, []

    def copy(self, src, dst):
        made = pltpu.make_async_copy(src, dst, self.sems.at[self.used])
        self.used += 1
        made.start()
        return made

    def save(self, src, dst):
        self.open.append(self.copy(src, dst))

    def finish(self):
        for made in self.open:
            made.wait()


def load_columns(local, full, rows, dst, stage):
    seq, _, cols = full.shape
    if cols % 128 == 0:
        return [local.copy(full.at[s, rows], dst.at[:, pl.ds(s * cols, cols)]) for s in range(seq)]
    for s in range(seq):
        local.copy(full.at[s, rows], stage.at[pl.ds(0, rows.size)]).wait()
        dst[:, s * cols : (s + 1) * cols] = stage[: rows.size]
    return []


def load_plane(local, full, rows, zz, dst, stage):
    cols = full.shape[2]
    if cols % 128 == 0:
        return [
            local.copy(full.at[2 * zz + core, rows], dst.at[:, pl.ds(core * cols, cols)])
            for core in range(2)
        ]
    for core in range(2):
        local.copy(full.at[2 * zz + core, rows], stage.at[core, pl.ds(0, rows.size)]).wait()
    dst[...] = jnp.concatenate([stage[0, 0 : rows.size], stage[1, 0 : rows.size]], axis=1)
    return []


def stream(order, source, slots, sems, body, after):
    def fetch(n):
        return pltpu.make_async_copy(source(order[n]), slots.at[n % 2], sems.at[n % 2])

    fetch(0).start()
    for n, s in enumerate(order):
        if n + 1 < len(order):
            fetch(n + 1).start()
        fetch(n).wait()
        body(s, n % 2)
        after()


def forward_kernel(batch, seq, spans, *refs):
    (x_hbm, in_hbm, out_w_hbm, gain_hbm, pair_hbm, down_hbm), refs = refs[:6], refs[6:]
    fulls, refs = refs[:4], refs[4:]
    out_hbm, saved, refs = refs[0], refs[1:13], refs[13:]
    (q_out, k_out, v_out, raw_out, att_out, e_out, gated_out, mid_out, nb_out, pair_out, hid_out, na_out) = saved
    (x, na, tmp, qkvr, att, gated, mid, nb, w_in, w_out, gain, w_pair, tmp_g, tmp_u, pair, hid,
     w_down, res, stage, gain_own, na_t, gated_t, hid_t, mine, other, before, chain_out, early, chain_sems, slot_sems, pair_sems,
     local_sems, gather_sems, gather_local, *held) = refs
    place = Place(batch, seq)
    local = Locals(local_sems)
    load_in = local.copy(in_hbm, held[0])
    load_x = local.copy(x_hbm, x)
    load_gain = local.copy(gain_hbm, gain_own)
    load_out = local.copy(out_w_hbm, held[1].at[pl.ds(0, D)])
    load_pair = local.copy(pair_hbm, held[2])
    load_down = local.copy(down_hbm, held[3])
    gather = Gather(place, held, fulls, (True, True, True, True), gather_sems, gather_local)
    place.barrier()
    rows, span = x.shape[0], spans
    per_group = seq // 4
    blocks = rows // span
    pairs = D // 128
    cols_in = w_in.shape[-1]
    half = seq // 2
    planes = place.planes
    cols_two = 2 * fulls[1].shape[2]
    q, k, v, raw = (qkvr.at[n] for n in range(4))
    first, second, own, own_f = pair_masks(span)
    steps = Steps(FORWARD_STEPS if place.square and place.planes == 4 else {})
    plan_gather(steps, gather, 4)

    def have(w, n):
        steps.finish(lambda name: not steps.table and name[0] != "c" and name[1] <= w)
        return gather.have(w, n)

    load_in.wait()
    steps.run(("start", 0))
    steps.tick()
    load_x.wait()

    def norm_rows(r):
        xr = x[r, :].astype(F32)
        na[r, :] = (xr * lax.rsqrt(mean_square(xr) + 1e-6)).astype(BF16)

    row_loop(rows, 64, norm_rows)
    load_gain.wait()
    load_out.wait()
    top = lax.broadcasted_iota(jnp.int32, (GAIN_ROWS, gain_own.shape[1]), 0) == 0
    held[1][D : D + GAIN_ROWS, :] = jnp.where(top, gain_own[...].astype(F32), 0.0).astype(BF16)
    load_pair.wait()
    load_down.wait()
    steps.tick()

    def project(s, slot):
        group, n = lax.div(s, per_group), lax.rem(s, per_group)
        tmp[...] = dot(na[...], w_in[slot])
        at = pl.ds(pl.multiple_of(n * cols_in, 128), cols_in)

        @pl.when(s < 2 * per_group)
        def _():
            def finish_rows(r):
                value = tmp[r, :]
                value = jnp.maximum(value, 0.0) + jnp.log1p(jnp.exp(-jnp.abs(value)))
                qkvr[group, r, at] = value.astype(BF16)

            row_loop(rows, 64, finish_rows)

        @pl.when(s >= 2 * per_group)
        def _():
            def finish_rows(r):
                qkvr[group, r, at] = tmp[r, :].astype(BF16)

            row_loop(rows, 64, finish_rows)

    for n in range(planes):
        zz = have(0, n)
        blocks_in = [
            pltpu.make_async_copy(fulls[0].at[2 * zz + c], w_in.at[c], slot_sems.at[c]) for c in range(2)
        ]
        for made in blocks_in:
            made.start()
        for c, made in enumerate(blocks_in):
            made.wait()
            project(2 * zz + c, c)
            steps.tick()

    def state(n):
        i, j = lax.div(n, pairs), lax.rem(n, pairs)
        at, block = tokens(i, span), lanes(j)
        return pack_state(dot_tn(k[at, block], v[at, block])).astype(BF16)

    def keep_state(n, value):
        mine[n] = value

    chain = Chain(place, True, mine, other, before, chain_out, chain_sems)
    for part in range(Chain.PARTS):
        grouped(part * chain.count, (part + 1) * chain.count, state, keep_state)
        chain.start(part, steps)
        steps.tick()
    for src, dst in ((q, q_out), (k, k_out), (v, v_out), (raw, raw_out)):
        local.save(src, dst)

    row = lax.rem(lax.broadcasted_iota(jnp.int32, (2 * span, span), 0), span)
    col = lax.broadcasted_iota(jnp.int32, (2 * span, span), 1)
    lane = lax.broadcasted_iota(jnp.int32, (span, 128), 1)

    def inner(n):
        i, j = lax.div(n, pairs), lax.rem(n, pairs)
        at, block = tokens(i, span), lanes(j)
        scores = dot_nt(by_head(q[at, block], first, second), k[at, block])
        scores = jnp.where(row >= col, scores, 0.0).astype(BF16)
        both = dot(scores, v[at, block])
        return jnp.where(lane < HEAD_DIM, both[:span], both[span:])

    def keep_inner(n, value):
        att[tokens(lax.div(n, pairs), span), lanes(lax.rem(n, pairs))] = value

    for i in range(blocks):
        grouped(i * pairs, (i + 1) * pairs, inner, keep_inner)
        steps.tick()

    transpose(na, na_t)
    local.save(na_t, na_out)
    steps.tick()
    chain.finish(0, steps, early)
    loads = []
    for n in range(planes):
        zz = have(1, n)
        to = pl.ds(pl.multiple_of(zz * cols_two, 128), cols_two)
        loads += load_plane(local, fulls[1], pl.ds(0, D), zz, w_out.at[:, to], stage)
        loads += load_plane(local, fulls[1], pl.ds(D, 16), zz, gain.at[:, to], stage)
    for made in loads:
        made.wait()
    steps.tick()

    def outer(n):
        i, j = lax.div(n, pairs), lax.rem(n, pairs)
        at, block = tokens(i, span), lanes(j)
        a = att[at, block] + dot(q[at, block], unpack_state(early[n], own))
        unit = a * lax.rsqrt(head_sums(a * a, own) * (1.0 / HEAD_DIM) + 1e-5)
        normed = unit * gain[0:1, block].astype(F32)
        return a, (jax.nn.sigmoid(raw[at, block].astype(F32)) * normed).astype(BF16)

    def keep_outer(n, value):
        at, block = tokens(lax.div(n, pairs), span), lanes(lax.rem(n, pairs))
        att[at, block], gated[at, block] = value

    for i in range(blocks):
        if i == blocks // 2:
            chain.finish(1, steps, early)
        grouped(i * pairs, (i + 1) * pairs, outer, keep_outer)
        steps.tick()
    local.save(early, e_out)
    local.save(att, att_out)

    def turn(src, dst, blocks_of):
        for block in blocks_of:
            at = slice(block * 128, min((block + 1) * 128, src.shape[1]))
            dst[at, :] = src[:, at].T

    for n in range(D // 512):
        at = pl.ds(n * 512, 512)
        mid[:, at] = x[:, at].astype(F32) + dot(gated[...], w_out[:, at])
        turn(gated, gated_t, range(n * 4, n * 4 + 4))
        steps.tick()
    local.save(gated_t, gated_out)

    def norm_mid(r):
        m = mid[r, :]
        nb[r, :] = (m * lax.rsqrt(mean_square(m) + 1e-6)).astype(BF16)

    row_loop(rows, 64, norm_mid)
    local.save(mid, mid_out)
    local.save(nb, nb_out)
    steps.tick()

    def fetch_pair(j, slot):
        return [
            pltpu.make_async_copy(
                fulls[2].at[j + side * half], w_pair.at[slot, side], pair_sems.at[slot, side]
            )
            for side in range(2)
        ]

    early_half = planes == 4
    away = jnp.where(place.z < 2, 0, 2) if early_half else 0
    for n in range(planes - 1 if early_half else planes):
        have(2, n)
    for made in fetch_pair(away, 0):
        made.start()
    count_t = -(-hid.shape[-1] // 128)

    def make_pair(n, part):
        j, slot = lax.rem(n + away, half), n % 2
        for row in range(part * rows // 2, (part + 1) * rows // 2, 128):
            r = slice(row, row + 128)
            gate = dot_nt(nb[r, :], w_pair[slot, 0])
            up = dot_nt(nb[r, :], w_pair[slot, 1])
            pair[j, r, :] = gate.astype(BF16)
            pair[j + half, r, :] = up.astype(BF16)
            hid[j, r, :] = (gate * up).astype(BF16)

    def save_pair(n):
        j = lax.rem(n + away, half)
        local.save(pair.at[j], pair_out.at[j])
        local.save(pair.at[j + half], pair_out.at[j + half])

    def turn_hid(n):
        j = lax.rem(n + away, half)
        turn(hid.at[j], hid_t.at[j], range(count_t))
        local.save(hid_t.at[j], hid_out.at[j])

    for n in range(half):
        j, slot = lax.rem(n + away, half), n % 2
        if early_half and n == 1:
            have(2, planes - 1)
        if n + 1 < half:
            for made in fetch_pair(lax.rem(n + 1 + away, half), 1 - slot):
                made.start()
        for made in fetch_pair(j, slot):
            made.wait()
        make_pair(n, 0)
        steps.tick()
        make_pair(n, 1)
        save_pair(n)
        if n > 0:
            turn_hid(n - 1)
        steps.tick()
    steps.tick()

    width = hid.shape[-1]

    def down(zz, slot):
        at = pl.ds(pl.multiple_of(zz * cols_two, 128), cols_two)
        total = mid[:, at]
        for j in range(half):
            total = total + dot(hid[j], w_down[slot, j * width : (j + 1) * width, :])
        res[:, at] = total.astype(BF16)

    later = [half - 1]
    before_it = None
    for n in range(planes):
        zz = have(3, n)
        loads = load_plane(local, fulls[3], pl.ds(0, FF), zz, w_down.at[n % 2], stage)
        if before_it is not None:
            down(*before_it)
            if later:
                turn_hid(later.pop(0))
            steps.tick()
        for made in loads:
            made.wait()
        before_it = (zz, n % 2)
    down(*before_it)
    local.save(res, out_hbm)
    steps.tick()
    steps.finish()
    local.finish()
    place.finish()


def forward(batch, seq, x, span, shards):
    attn_in, attn_out, out_gain, glu_in, glu_out = shards
    shards = (attn_in, jax.ShapeDtypeStruct((D + GAIN_ROWS, attn_out.shape[1]), BF16), glu_in.T, glu_out)
    rows = x.shape[0]
    cols_in, cols_pair = shards[0].shape[1], shards[2].shape[0]
    half = seq // 2
    states = (rows // span) * (D // 128)
    big = jax.ShapeDtypeStruct((rows, D), BF16)
    big_f = jax.ShapeDtypeStruct((rows, D), F32)
    narrow = shards[3].shape[1] % 128 != 0
    any_space = pl.BlockSpec(memory_space=pl.ANY)
    out_shape = [jax.ShapeDtypeStruct((seq, *a.shape), a.dtype) for a in shards]
    out_shape += [big, big, big, big, big, big_f]
    turned = jax.ShapeDtypeStruct((D, rows), BF16)
    out_shape += [jax.ShapeDtypeStruct((states, HEAD_DIM, 128), BF16), turned, big_f, big]
    out_shape += [
        jax.ShapeDtypeStruct((seq, rows, cols_pair), BF16),
        jax.ShapeDtypeStruct((half, cols_pair, rows), BF16),
        turned,
    ]
    wide, wide_f = pltpu.VMEM((rows, D), BF16), pltpu.VMEM((rows, D), F32)
    pair_f = pltpu.VMEM((2, rows, cols_pair), F32)
    scratch = [
        wide, wide, pltpu.VMEM((rows, cols_in), F32), pltpu.VMEM((4, rows, D), BF16), wide_f, wide, wide_f, wide,
        pltpu.VMEM((2, D, cols_in), BF16),
        pltpu.VMEM((D, D), BF16),
        pltpu.VMEM((16, D), BF16),
        pltpu.VMEM((2, 2, cols_pair, D), BF16),
        pair_f, pair_f,
        pltpu.VMEM((seq, rows, cols_pair), BF16),
        pltpu.VMEM((half, rows, cols_pair), BF16),
        pltpu.VMEM((2, FF, 2 * shards[3].shape[1]), BF16),
        wide,
        pltpu.VMEM((2, FF, shards[3].shape[1]) if narrow else (2, 16, 128), BF16),
        pltpu.VMEM((1, attn_out.shape[1]), BF16),
        *[pltpu.VMEM((D, rows), BF16)] * 2,
        pltpu.VMEM((half, cols_pair, rows), BF16),
        *[pltpu.VMEM((states, HEAD_DIM, 128), BF16)] * 5,
        pltpu.SemaphoreType.DMA((6, Chain.PARTS)),
        pltpu.SemaphoreType.DMA((2,)),
        pltpu.SemaphoreType.DMA((2, 2)),
        pltpu.SemaphoreType.DMA((128,)),
        pltpu.SemaphoreType.DMA((Gather.KINDS, 4, half)),
        pltpu.SemaphoreType.DMA((4,)),
        *[pltpu.VMEM(a.shape, a.dtype) for a in shards],
    ]
    return pl.pallas_call(
        functools.partial(forward_kernel, batch, seq, span),
        out_shape=out_shape,
        in_specs=[any_space] * 6,
        out_specs=[any_space] * len(out_shape),
        scratch_shapes=scratch,
        compiler_params=pltpu.CompilerParams(
            collective_id=0, has_side_effects=True, vmem_limit_bytes=62 * 1024 * 1024
        ),
        name="forward",
    )(x, attn_in, attn_out, out_gain.reshape(1, -1), glu_in.T, glu_out)


WIDE = (False, True, False, True)
Z_PARTS = (1, 4, 1, 4)


def z_parts(w, rows):
    return max(k for k in range(1, Z_PARTS[w] + 1) if rows % (16 * k) == 0)


def slope(plus):
    series = plus * (1.0 - plus * (0.5 - plus * (1.0 / 6.0)))
    return jnp.where(plus < 0.02, series, 1.0 - jnp.exp(-plus))


def backward_kernel(batch, seq, span, *refs):
    g_hbm, x_hbm, *fulls = refs[:6]
    (q_in, k_in, v_in, raw_in, att_in, e_in, gated_in, mid_in, nb_in, pair_in, hid_in, na_in) = refs[6:18]
    grad_hbm, sums, gm_hbm, far = refs[18], refs[19:23], refs[23], refs[24:28]
    refs = list(refs[28:])
    place = Place(batch, seq)
    reds = []
    for w in range(4):
        reds.append(Reduce(place, WIDE[w], z_parts(w, sums[w].shape[0]), sums[w], far[w], refs[:11]))
        refs = refs[11:]
    (tall, turned, pair, fields, f0, f1, g, split, low, down, slots, wide_out, in_out, slim_out, gain, gain_sums, gain_split,
     early, mine, other, before, chain_out, stage, chain_sems, slot_sems, local_sems) = refs
    red_down, red_pair, red_out, red_in = reds
    local = Locals(local_sems)
    rows = g.shape[0]
    half = seq // 2
    planes = half
    width = hid_in.shape[1]
    cols_in, cols_out, cols_pair = fulls[0].shape[2], fulls[1].shape[2], fulls[2].shape[1]
    per_group, per_block = seq // 4, cols_in // 128
    blocks, pairs = rows // span, D // 128
    first, second, own, own_f = pair_masks(span)
    core, sibling = place.c, 1 - place.c
    steps = Steps(BACKWARD_STEPS if place.square and place.planes == 4 else {})

    load_g = local.copy(g_hbm, g)
    load_hid = [local.copy(hid_in.at[j], tall.at[pl.ds(j * width, width)]) for j in range(half)]
    load_nb = local.copy(nb_in, low)
    load_gated = local.copy(gated_in, turned)
    load_pair = [local.copy(pair_in.at[s], pair.at[s]) for s in range(seq)]
    load_e = local.copy(e_in, early)
    place.barrier()

    def split_columns(src):
        for s in range(seq):
            to = (s % 2) * (D // 2) + (s // 2) * cols_out
            split[:, to : to + cols_out] = src[:, s * cols_out : (s + 1) * cols_out]

    def by_core(which):
        return pl.ds(pl.multiple_of(which * (D // 2), D // 2), D // 2)

    slim_sent = []

    def slim_send(red, row, count, k, fill):
        slot = len(slim_sent) % 2
        if len(slim_sent) >= 2:
            for made in slim_sent[-2]:
                made().wait_send()
        fill(slot)
        sent = []
        for zz in range(planes):
            src = slim_out.at[slot, zz, pl.ds(0, count)]
            sent.append(functools.partial(red.core_copy, zz, src, row, count, k))
            sent[-1]().start()
        slim_sent.append(sent)

    def slim_theirs(red, lhs, at, row, count, k):
        def fill(slot):
            value = dot(lhs[at : at + count, :], split[:, by_core(sibling)])
            for zz in range(planes):
                slim_out[slot, zz, 0:count, :] = value[:, zz * cols_out : (zz + 1) * cols_out].astype(BF16)

        slim_send(red, row, count, k, fill)

    def slim_mine(red, lhs, at, row, count, k):
        value = dot(lhs[at : at + count, :], split[:, by_core(core)])
        for zz in range(planes):
            red.core_copy(zz, None, row, count, k).wait_recv()
            here = red.part[zz, row : row + count, :].astype(F32)
            here = here + value[:, zz * cols_out : (zz + 1) * cols_out]
            red.part[zz, row : row + count, :] = here.astype(BF16)

    wide_sent = []

    def pair_block(s, row):
        r = slice(row, min(row + 256, cols_pair))
        return r, dot_tn(pair[s, :, r], low[...])

    def in_block(s, row):
        r = slice(row, row + 256)
        return r, dot(turned[r, :], pair[s, :, 0:cols_in])

    def wide_theirs(red, block, out, zz):
        slot = len(wide_sent) % 2
        if len(wide_sent) >= 2:
            wide_sent[-2]().wait_send()
        for row in range(0, red.total, 256):
            r, value = block(2 * zz + sibling, row)
            out[slot, r, :] = value.astype(BF16)
        wide_sent.append(functools.partial(red.core_copy, zz, out.at[slot], 0, red.total, 0))
        wide_sent[-1]().start()
        steps.tick()

    def wide_mine(red, r, block, zz):
        red.core_copy(zz, None, 0, red.total, 0).wait_recv()
        for row in range(0, red.total, 256):
            at, value = block(2 * zz + core, row)
            red.part[zz, at, :] = (red.part[zz, at, :].astype(F32) + value).astype(BF16)
        if red.wide:
            red.plane_1(zz)
        red.plane_plan(steps, r, zz)
        red.z_plan(steps, r, zz)
        steps.tick()

    load_g.wait()
    split_columns(g)
    for made in load_hid:
        made.wait()
    for j in range(half):
        slim_theirs(red_down, tall, j * width, j * width, width, j)
    for j in range(half):
        slim_mine(red_down, tall, j * width, j * width, width, j)
    for zz in range(planes):
        red_down.z_plan(steps, 0, zz)
    red_down.late_plan(steps, 0)
    red_down.spread_plan(steps, 0)
    steps.tick()

    def load_down(j):
        at = pl.ds((j % 2) * width, width)
        return load_columns(local, fulls[3], pl.ds(j * width, width), down.at[at], stage)

    for made in load_pair:
        made.wait()
    waits = load_down(0)
    for j in range(half):
        after = load_down(j + 1) if j + 1 < half else []
        for made in waits:
            made.wait()
        waits = after
        at = (j % 2) * width
        for row in range(0, rows, 128):
            r = slice(row, row + 128)
            grad = dot_nt(g[r, :], down[at : at + width, :])
            gate, up = pair[j, r, :].astype(F32), pair[j + half, r, :].astype(F32)
            pair[j, r, :] = (grad * up).astype(BF16)
            pair[j + half, r, :] = (grad * gate).astype(BF16)
        steps.tick()
    load_mid = local.copy(mid_in, f1)

    load_nb.wait()
    wide_theirs(red_pair, pair_block, wide_out, 0)
    for zz in range(planes):
        if zz + 1 < planes:
            wide_theirs(red_pair, pair_block, wide_out, zz + 1)
        wide_mine(red_pair, 1, pair_block, zz)
    red_pair.spread_plan(steps, 1)
    w_out = down.at[pl.ds(0, D)]
    load_out = load_columns(local, fulls[1], pl.ds(0, D), w_out, stage)
    load_out += load_columns(local, fulls[1], pl.ds(D, 16), gain, stage)
    views = []
    for k, src in enumerate((q_in, k_in, v_in, raw_in)):
        for side in range(2):
            to = tall.at[pl.ds((2 * k + side) * rows, rows)]
            views.append(local.copy(src.at[:, pl.ds(side * (D // 2), D // 2)], to))

    for made in wide_sent[-2:]:
        made().wait_send()
    wide_sent.clear()
    places = (slots.at[0], slots.at[1], wide_out.at[0], wide_out.at[1])

    def fetch_pair(n):
        return [
            pltpu.make_async_copy(fulls[2].at[s], places[s % 4], slot_sems.at[s % 4])
            for s in (2 * n, 2 * n + 1)
        ]

    for made in fetch_pair(0):
        made.start()
    for n in range(half):
        if n + 1 < half:
            for made in fetch_pair(n + 1):
                made.start()
        for made in fetch_pair(n):
            made.wait()
        value = sum(dot(pair[s], places[s % 4][...]) for s in (2 * n, 2 * n + 1))
        f0[...] = value if n == 0 else f0[...] + value
        steps.tick()
    load_mid.wait()

    def back_mid(r):
        m, grad = f1[r, :], f0[r, :]
        scale = lax.rsqrt(mean_square(m) + 1e-6)
        inner = jnp.mean(grad * m, axis=-1, keepdims=True)
        total = g[r, :].astype(F32) + scale * grad - m * (scale * scale * scale) * inner
        f1[r, :] = total
        low[r, :] = total.astype(BF16)

    row_loop(rows, 64, back_mid)
    save_gm = local.copy(f1, gm_hbm)
    split_columns(low)
    steps.tick()

    load_gated.wait()
    for k in range(2):
        slim_theirs(red_out, turned, k * (D // 2), k * (D // 2), D // 2, k)
    for made in load_out:
        made.wait()
    for n in range(D // 512):
        at = pl.ds(n * 512, 512)
        f0[:, at] = dot_nt(low[...], w_out[at, :])
    for k in range(2):
        slim_mine(red_out, turned, k * (D // 2), k * (D // 2), D // 2, k)
    load_na = local.copy(na_in, turned)
    load_x = local.copy(x_hbm, low)
    save_gm.wait()
    load_att = local.copy(att_in, f1)
    gain_sums[...] = jnp.zeros_like(gain_sums)
    for made in views:
        made.wait()
    load_e.wait()
    load_att.wait()
    steps.tick()

    def view(k, i, j):
        row = pl.multiple_of((2 * k + lax.div(j, pairs // 2)) * rows + i * span, span)
        return pl.ds(row, span), lanes(lax.rem(j, pairs // 2))

    def put(group, i, j, value):
        s = group * per_group + lax.div(j, per_block)
        pair[s, tokens(i, span), lanes(lax.rem(j, per_block))] = value

    def place_of(n):
        return lax.div(n, pairs), lax.rem(n, pairs)

    def back_gate(n):
        i, j = place_of(n)
        at, block = tokens(i, span), lanes(j)
        a, grad = f1[at, block], f0[at, block]
        scale = lax.rsqrt(head_sums(a * a, own) * (1.0 / HEAD_DIM) + 1e-5)
        unit = a * scale
        gains = gain[0:1, block].astype(F32)
        sig = jax.nn.sigmoid(tall[view(3, i, j)].astype(F32))
        grad_normed = grad * sig
        grad_gate = (grad * (unit * gains) * sig * (1.0 - sig)).astype(BF16)
        gain_sum = jnp.sum(grad_normed * unit, axis=0, keepdims=True)
        grad_unit = grad_normed * gains
        inner = head_sums(grad_unit * a, own) * (1.0 / HEAD_DIM)
        grad_a = (scale * grad_unit - a * (scale * scale * scale) * inner).astype(BF16)
        state = pack_state(dot_tn(tall[view(0, i, j)], grad_a)).astype(BF16)
        return grad_gate, gain_sum, grad_a, state

    def keep_gate(n, value):
        i, j = place_of(n)
        put(3, i, j, value[0])
        gain_sums[0:1, lanes(j)] += value[1]
        g[tokens(i, span), lanes(j)] = value[2]
        mine[n] = value[3]

    chain = Chain(place, False, mine, other, before, chain_out, chain_sems)
    for i in range(blocks):
        grouped(i * pairs, (i + 1) * pairs, back_gate, keep_gate)
        if (i + 1) % (blocks // Chain.PARTS) == 0:
            chain.start(i // (blocks // Chain.PARTS), steps)
        steps.tick()

    for s in range(seq):
        to = (s // 2) * cols_out
        gain_split[s % 2, :, to : to + cols_out] = gain_sums[:, s * cols_out : (s + 1) * cols_out]
    top = lax.broadcasted_iota(jnp.int32, (GAIN_ROWS, cols_out), 0) == 0

    def gain_rows(which, zz):
        row = gain_split[which, 0:1, zz * cols_out : (zz + 1) * cols_out]
        return jnp.where(top, row, 0.0)

    def fill_gain(slot):
        for zz in range(planes):
            slim_out[slot, zz, 0:GAIN_ROWS, :] = gain_rows(sibling, zz).astype(BF16)

    slim_send(red_out, D, GAIN_ROWS, 2, fill_gain)
    load_na.wait()
    ready = [zz for zz in range(planes) if zz * 2 >= 3 * per_group]
    for zz in ready:
        wide_theirs(red_in, in_block, in_out, zz)
    for zz in range(planes):
        red_out.core_copy(zz, None, D, GAIN_ROWS, 2).wait_recv()
        here = red_out.part[zz, D : D + GAIN_ROWS, :].astype(F32) + gain_rows(core, zz)
        red_out.part[zz, D : D + GAIN_ROWS, :] = here.astype(BF16)
    for zz in range(planes):
        red_out.z_plan(steps, 2, zz)
    red_out.late_plan(steps, 2)
    red_out.spread_plan(steps, 2)
    steps.tick()
    for zz in ready:
        wide_mine(red_in, 3, in_block, zz)

    t_of = lax.rem(lax.broadcasted_iota(jnp.int32, (span, 2 * span), 1), span)
    s_of = lax.broadcasted_iota(jnp.int32, (span, 2 * span), 0)
    t_down = lax.rem(lax.broadcasted_iota(jnp.int32, (2 * span, span), 0), span)
    s_down = lax.broadcasted_iota(jnp.int32, (2 * span, span), 1)
    lane = lax.broadcasted_iota(jnp.int32, (span, 128), 1)

    def back_attention(n):
        i, j = place_of(n)
        qs, ks, vs = (tall[view(k, i, j)] for k in range(3))
        grads = g[tokens(i, span), lanes(j)]
        q2, g2 = by_head(qs, first, second), by_head(grads, first, second)
        scores = jnp.where(t_of >= s_of, dot_nt(ks, q2), 0.0).astype(BF16)
        grad_t = jnp.where(t_of >= s_of, dot_nt(vs, g2), 0.0).astype(BF16)
        grad_s = jnp.where(t_down >= s_down, dot_nt(g2, vs), 0.0).astype(BF16)
        both = dot(grad_s, ks)
        grad_q = jnp.where(lane < HEAD_DIM, both[:span], both[span:])
        grad_q = grad_q + dot_nt(grads, unpack_state(early[n], own))
        return dot(grad_t, q2), dot(scores, g2), (grad_q * slope(qs.astype(F32))).astype(BF16)

    def keep_attention(n, value):
        i, j = place_of(n)
        at, block = tokens(i, span), lanes(j)
        f0[at, block], f1[at, block] = value[:2]
        put(0, i, j, value[2])

    for i in range(blocks):
        grouped(i * pairs, (i + 1) * pairs, back_attention, keep_attention, 2)
        steps.tick()
    ready_q = [zz for zz in range(planes) if (zz + 1) * 2 <= per_group]
    for zz in ready_q:
        wide_theirs(red_in, in_block, in_out, zz)
    for zz in ready_q:
        wide_mine(red_in, 3, in_block, zz)

    def back_states(n):
        i, j = place_of(n)
        at, block = tokens(i, span), lanes(j)
        ks, vs = tall[view(1, i, j)], tall[view(2, i, j)]
        later = unpack_state(other[n], own)
        grad_k = (f0[at, block] + dot_nt(vs, later)) * slope(ks.astype(F32))
        return grad_k.astype(BF16), (f1[at, block] + dot(ks, later)).astype(BF16)

    def keep_states(n, value):
        put(1, *place_of(n), value[0])
        put(2, *place_of(n), value[1])

    for part in range(Chain.PARTS):
        chain.finish(part, steps, other)
        grouped(part * chain.count, (part + 1) * chain.count, back_states, keep_states)
        steps.tick()
    load_gm = local.copy(gm_hbm, f1)
    rest = [zz for zz in range(planes) if zz not in ready and zz not in ready_q]
    for n, zz in enumerate(rest):
        if n >= 2:
            wide_mine(red_in, 3, in_block, rest[n - 2])
        wide_theirs(red_in, in_block, in_out, zz)
    for zz in rest[-2:]:
        wide_mine(red_in, 3, in_block, zz)
    red_in.spread_plan(steps, 3)

    for made in wide_sent[-2:]:
        made().wait_send()
    wide_sent.clear()
    places_in = [in_out.at[k] for k in range(2)]
    places_in += [down.at[pl.ds(0, D), pl.ds(k * (D // 2), cols_in)] for k in range(2)]

    def fetch_in(n):
        return [
            pltpu.make_async_copy(fulls[0].at[s], places_in[s % 4], slot_sems.at[s % 4])
            for s in (2 * n, 2 * n + 1)
        ]

    for made in fetch_in(0):
        made.start()
    for n in range(half):
        if n + 1 < half:
            for made in fetch_in(n + 1):
                made.start()
        for made in fetch_in(n):
            made.wait()
        value = sum(dot_nt(pair[s, :, 0:cols_in], places_in[s % 4][...]) for s in (2 * n, 2 * n + 1))
        f0[...] = value if n == 0 else f0[...] + value
        steps.tick()
    load_gm.wait()
    load_x.wait()

    def back_x(r):
        x, grad = low[r, :].astype(F32), f0[r, :]
        scale = lax.rsqrt(mean_square(x) + 1e-6)
        inner = jnp.mean(grad * x, axis=-1, keepdims=True)
        f1[r, :] += scale * grad - x * (scale * scale * scale) * inner

    row_loop(rows, 64, back_x)
    local.save(f1, grad_hbm)
    steps.tick()
    steps.finish()
    local.finish()
    for sent in slim_sent[-2:]:
        for made in sent:
            made().wait_send()
    for made in wide_sent[-2:]:
        made().wait_send()
    place.finish()


def backward(batch, seq, span, grad, x, fulls, saved):
    rows = x.shape[0]
    half = seq // 2
    cols_in, cols_out, cols_pair = fulls[0].shape[2], fulls[1].shape[2], fulls[2].shape[1]
    width = saved[10].shape[1]
    square = batch == 4
    shapes = ((FF, cols_out), (cols_pair, D), (D + GAIN_ROWS, cols_out), (D, cols_in))
    states = (rows // span) * (D // 128)
    any_space = pl.BlockSpec(memory_space=pl.ANY)
    big_f = jax.ShapeDtypeStruct((rows, D), F32)
    out_shape = [big_f] + [jax.ShapeDtypeStruct(shape, BF16) for shape in shapes] + [big_f]
    out_shape += [Reduce.far(square, WIDE[w], half, *shapes[w]) for w in range(4)]
    scratch = []
    core_parts = (half, 1, 3, 1)
    for w in range(4):
        scratch += Reduce.scratch(square, WIDE[w], half, *shapes[w], core_parts[w], z_parts(w, shapes[w][0]))
    narrow = cols_out % 128 != 0
    state = pltpu.VMEM((states, HEAD_DIM, 128), BF16)
    scratch += [
        pltpu.VMEM((max(FF, 8 * rows), D // 2), BF16),
        pltpu.VMEM((D, rows), BF16),
        pltpu.VMEM((seq, rows, cols_pair), BF16),
        pltpu.VMEM((16, 128), BF16),
        pltpu.VMEM((rows, D), F32),
        pltpu.VMEM((rows, D), F32),
        pltpu.VMEM((rows, D), BF16),
        pltpu.VMEM((rows, D), BF16),
        pltpu.VMEM((rows, D), BF16),
        pltpu.VMEM((max(2 * width, D), D), BF16),
        pltpu.VMEM((2, cols_pair, D), BF16),
        pltpu.VMEM((2, cols_pair, D), BF16),
        pltpu.VMEM((2, D, cols_in), BF16),
        pltpu.VMEM((2, half, max(width, D // 2), cols_out), BF16),
        pltpu.VMEM((16, D), BF16),
        pltpu.VMEM((8, D), F32),
        pltpu.VMEM((2, 8, D // 2), F32),
        state, state, state, state, state,
        pltpu.VMEM((D, cols_out) if narrow else (16, 128), BF16),
        pltpu.SemaphoreType.DMA((6, Chain.PARTS)),
        pltpu.SemaphoreType.DMA((4,)),
        pltpu.SemaphoreType.DMA((192,)),
    ]
    return pl.pallas_call(
        functools.partial(backward_kernel, batch, seq, span),
        out_shape=out_shape,
        in_specs=[any_space] * 18,
        out_specs=[any_space] * len(out_shape),
        scratch_shapes=scratch,
        compiler_params=pltpu.CompilerParams(
            collective_id=1, has_side_effects=True, vmem_limit_bytes=63 * 1024 * 1024
        ),
        name="backward",
    )(grad, x, *fulls, *saved)


def local(block_in, attn_in, attn_out, out_gain, glu_in, glu_out, block_grad):
    seq_count, span = block_in.shape[:2]
    rows = seq_count * span
    batch, seq = lax.axis_size("batch"), lax.axis_size("seq")
    x = block_in.reshape(rows, D)
    parts = forward(batch, seq, x, span, (attn_in, attn_out, out_gain, glu_in, glu_out))
    fulls, block_out, saved = parts[:4], parts[4], parts[5:]
    grads = backward(batch, seq, span, block_grad.reshape(rows, D), x, fulls, saved)
    input_grad, sums = grads[0], list(grads[1:5])
    if batch != 4:
        sums = [lax.psum(a, "batch") for a in sums]
    block_out, input_grad, down, pair, out, gain, into = finish(block_out, input_grad, sums)
    return (
        block_out.reshape(block_in.shape),
        input_grad.reshape(block_in.shape),
        into,
        out,
        gain.reshape(-1),
        pair.T,
        down,
    )


def finish_kernel(*refs):
    ins, outs, refs = refs[:6], refs[6:13], refs[13:]
    held, wide, (gain, load_sems, save_sems) = refs[:6], refs[6:10], refs[10:]
    loads = [pltpu.make_async_copy(src, dst, load_sems.at[k]) for k, (src, dst) in enumerate(zip(ins, held))]
    order = (3, 5, 2, 4, 1, 0)
    for k in order:
        loads[k].start()
    saves = []

    def save(src, dst):
        saves.append(pltpu.make_async_copy(src, dst, save_sems.at[len(saves)]))
        saves[-1].start()

    for k in order[:4]:
        loads[k].wait()
        src, dst = held[k], wide[k - 2]

        def widen(r, src=src, dst=dst):
            dst[r, :] = src[r, :].astype(F32)

        row_loop(src.shape[0], 64 if src.shape[0] % 64 == 0 else 32, widen)
        if k == 4:
            save(dst.at[pl.ds(0, D)], outs[4])
            gain[...] = dst[D : D + 1, :]
            save(gain, outs[5])
        else:
            save(dst, outs[k] if k < 4 else outs[6])
    for k in order[4:]:
        loads[k].wait()
        save(held[k], outs[k])
    for made in saves:
        made.wait()


def finish(block_out, input_grad, sums):
    ins = [block_out, input_grad, *sums]
    any_space = pl.BlockSpec(memory_space=pl.ANY)
    shapes = [a.shape for a in sums]
    cols = shapes[2][1]
    out_shape = [jax.ShapeDtypeStruct(a.shape, a.dtype) for a in (block_out, input_grad)]
    out_shape += [
        jax.ShapeDtypeStruct(s, F32) for s in (shapes[0], shapes[1], (D, cols), (1, cols), shapes[3])
    ]
    outs = pl.pallas_call(
        finish_kernel,
        out_shape=out_shape,
        in_specs=[any_space] * 6,
        out_specs=[any_space] * 7,
        scratch_shapes=[
            *[pltpu.VMEM(a.shape, a.dtype) for a in ins],
            *[pltpu.VMEM(s, F32) for s in shapes],
            pltpu.VMEM((1, cols), F32),
            pltpu.SemaphoreType.DMA((6,)),
            pltpu.SemaphoreType.DMA((7,)),
        ],
        compiler_params=pltpu.CompilerParams(vmem_limit_bytes=63 * 1024 * 1024),
        name="finish",
    )(*ins)
    return outs


def solution(mesh):
    rows, columns = P("batch", "seq", None), P(None, "seq")
    return jax.shard_map(
        local,
        mesh=mesh,
        in_specs=(rows, columns, columns, P("seq"), columns, columns, rows),
        out_specs=(rows, rows, columns, columns, P("seq"), columns, columns),
        check_vma=False,
    )
```
